512 devices in a mesh: gy: 16 (over x_hi, y), gx: 16 (over x_lo, z), img: 2 (over core).
Axes of the slice: x: 4 (x_hi: 2, x_lo: 2; x = x_hi * 2 + x_lo), y: 8, z: 8, core: 2. Of those that a mesh axis runs over, the one named last changes fastest.
Arguments:
- heights: float32 [4096, 4096], P('gy', 'gx'), may hold values from -4 to 4
- albedo: float32 [4096, 4096], P('gy', 'gx'), may hold values from 0.5 to 1.2
- images: bfloat16 [8, 4096, 4096], P('img', 'gy', 'gx'), may hold values from 0 to 1.5
- weights: bfloat16 [8, 4096, 4096], P('img', 'gy', 'gx'), may hold values from 0 to 1
- sun_index: int32 [8], P('img'), may hold values from 0 to 7
- expo_index: int32 [8], P('img'), may hold values from 0 to 7
- sun_azimuth: float32 [8], replicated, may hold values from -3.140625 to 3.140625
- sun_elevation: float32 [8], replicated, may hold values from 0.005 to 0.05
- exposure: float32 [8], replicated, may hold values from 0.5 to 1.5
Outputs:
- refined_heights: float32 [4096, 4096], P('gy', 'gx')
- refined_albedo: float32 [4096, 4096], P('gy', 'gx')
The draws below stay inside these ranges and needn't reach their ends.
All inputs are finite; a program needn't handle non-finite values.
Results may differ from the reference program's by a relative error of at most 0.0003.
Values sent between devices are 32-bit elements; how exact they have to be, the bound alone decides.
No kernel may reach another device: no remote copies, remote signals or barrier semaphores. Data moves between devices by JAX's collectives and lax.ppermute only.
A program may use at most 64 MiB of HBM per device.

```python
import jax
import jax.numpy as jnp
from jax import lax

SUN_TABLE = 8
EXPO_TABLE = 8
ITERS = 3
IMAGES = 8
ROWS = 4096
COLS = 4096


def place_ends(array, own_key, low, largest):
    dims = array.shape
    spot = [jax.random.randint(jax.random.fold_in(own_key, axis), (), 0, dims[axis]) for axis in range(len(dims))]
    array = array.at[tuple(spot)].set(low)
    longest = dims.index(max(dims))
    spot[longest] = (spot[longest] + 1) % dims[longest]
    return array.at[tuple(spot)].set(largest)


def steps_of(stream_key, shape, cuts, smallest, high):
    def one(dim, shards_of):
        steps = jax.random.uniform(jax.random.fold_in(jax.random.fold_in(stream_key, 6), dim), (shards_of,), jnp.float32, smallest / len(cuts), high / len(cuts))
        return jnp.repeat(jnp.exp(steps), shape[dim] // shards_of).reshape((-1,) + (1,) * (len(shape) - dim - 1))

    loudness = one(*cuts[0])
    for cut in cuts[1:]:
        loudness = loudness * one(*cut)
    return loudness


def normal_values(stream_key, extent, scale, most, pieces=(), held_as=jnp.bfloat16):
    level = steps_of(stream_key, extent, pieces, -0.22, 0.18) if pieces else 1.0
    array = jax.random.normal(stream_key, extent, jnp.float32) * scale * level
    return jnp.minimum(jnp.maximum(array, -most), most).astype(held_as)


def setup_inputs(seed: int = 0) -> dict:
    streams_of = jax.random.split(jax.random.key(seed), 10)
    return {
        "heights": normal_values(streams_of[0], (ROWS, COLS), 0.5, 4.0, ((0, 16), (1, 16)), jnp.float32),
        "albedo": jnp.clip(0.5 + 0.70000005 * jax.random.uniform(streams_of[1], (ROWS, COLS), jnp.float32) ** steps_of(streams_of[1], (ROWS, COLS), ((0, 16), (1, 16)), -0.2, 0.2), 0.5, 1.2),
        "images": jnp.clip(1.5 * jax.random.uniform(streams_of[2], (IMAGES, ROWS, COLS), jnp.float32) ** steps_of(streams_of[2], (IMAGES, ROWS, COLS), ((0, 2), (1, 16), (2, 16)), -0.2, 0.2), 0.0, 1.5).astype(jnp.bfloat16),
        "weights": jnp.clip(1.0 * jax.random.uniform(streams_of[3], (IMAGES, ROWS, COLS), jnp.float32) ** steps_of(streams_of[3], (IMAGES, ROWS, COLS), ((0, 2), (1, 16), (2, 16)), -0.2, 0.2), 0.0, 1.0).astype(jnp.bfloat16),
        "sun_index": place_ends(jax.random.randint(streams_of[4], (IMAGES,), 0, SUN_TABLE), jax.random.fold_in(streams_of[4], 1), 0, SUN_TABLE - 1).astype(jnp.int32),
        "expo_index": place_ends(jax.random.randint(streams_of[5], (IMAGES,), 0, EXPO_TABLE), jax.random.fold_in(streams_of[5], 1), 0, EXPO_TABLE - 1).astype(jnp.int32),
        "sun_azimuth": jnp.clip(jax.random.uniform(streams_of[6], (SUN_TABLE,), jnp.float32, -3.140625, 3.140625), -3.140625, 3.140625),
        "sun_elevation": jnp.clip(jax.random.uniform(streams_of[7], (SUN_TABLE,), jnp.float32, 0.005, 0.05), 0.005, 0.05),
        "exposure": jnp.clip(jax.random.uniform(streams_of[8], (EXPO_TABLE,), jnp.float32, 0.5, 1.5), 0.5, 1.5),
    }


def slopes(h):
    padded = jnp.pad(h, 1, mode='edge')
    p = 0.5 * (padded[1:-1, 2:] - padded[1:-1, :-2])
    q = 0.5 * (padded[2:, 1:-1] - padded[:-2, 1:-1])
    return (p, q)

def adjoint(gp, gq):
    wide = jnp.concatenate([-gp[:, :1], gp, -gp[:, -1:]], axis=1)
    tall = jnp.concatenate([-gq[:1], gq, -gq[-1:]], axis=0)
    return 0.5 * (wide[:, :-2] - wide[:, 2:]) + 0.5 * (tall[:-2] - tall[2:])

def lookup(index, table):
    hits = index[:, None] == jnp.arange(table.shape[0], dtype=jnp.int32)[None, :]
    return lax.optimization_barrier(jnp.sum(jnp.where(hits, table[None, :], jnp.float32(0.0)), axis=1))

def reference(heights, albedo, images, weights, sun_index, expo_index, sun_azimuth, sun_elevation, exposure):
    azim = lookup(sun_index, sun_azimuth)
    elev = lookup(sun_index, sun_elevation)
    gains = lookup(expo_index, exposure)
    sun_x = jnp.cos(elev) * jnp.cos(azim)
    sun_y = jnp.cos(elev) * jnp.sin(azim)
    sun_z = jnp.sin(elev)
    count = images.shape[0]
    rate_h = 0.2 / count
    rate_a = 0.5 / count
    h = heights
    a = albedo
    for step in range(ITERS):
        p, q = slopes(h)
        scale = 1.0 / jnp.sqrt(1.0 + p * p + q * q)
        cubed = scale * scale * scale
        gp = jnp.zeros_like(h)
        gq = jnp.zeros_like(h)
        ga = jnp.zeros_like(h)
        for k in range(count):
            shade = sun_z[k] - p * sun_x[k] - q * sun_y[k]
            resid = weights[k].astype(jnp.float32) * (gains[k] * a * shade * scale - images[k].astype(jnp.float32)) * gains[k]
            gp = gp + resid * a * (-sun_x[k] * scale - shade * p * cubed)
            gq = gq + resid * a * (-sun_y[k] * scale - shade * q * cubed)
            ga = ga + resid * shade * scale
        gp = gp + 0.3 * p
        gq = gq + 0.3 * q
        gh = adjoint(gp, gq)
        h = h - rate_h * gh
        a = a - rate_a * ga
    return (h, a)
```

```python
import functools

import jax
import jax.numpy as jnp
from jax import lax
from jax.experimental import pallas as pl
from jax.experimental.pallas import tpu as pltpu
from jax.sharding import PartitionSpec as P

ITERS = 3
AXES = ("gy", "gx", "img")
LANES = 128
ROW = 8
MOMENTS = 9
PLANES = 2 + MOMENTS
WIDTHS = (6,) + (5,) * (PLANES - 1)
STARTS = tuple(6 if k == 0 else 17 + 10 * (k - 1) for k in range(PLANES))
F32 = jnp.float32


def lane_ids(rows):
    return lax.broadcasted_iota(jnp.int32, (rows, LANES), 1)


def east_lanes(lane):
    hit = lane < 0
    for start, width in zip(STARTS, WIDTHS):
        hit = hit | ((lane >= start) & (lane < start + width))
    return hit


def moments_kernel(
    sun_index, expo_index, azimuth, elevation, exposure, height, albedo, images, weights, sums, edges
):
    count, rows, _ = images.shape
    line = lax.broadcasted_iota(jnp.int32, (ROW, LANES), 0)
    azim = jnp.zeros((ROW, LANES), F32)
    elev = jnp.zeros((ROW, LANES), F32)
    gain = jnp.zeros((ROW, LANES), F32)
    for k in range(count):
        azim = jnp.where(line == k, azimuth[sun_index[k]], azim)
        elev = jnp.where(line == k, elevation[sun_index[k]], elev)
        gain = jnp.where(line == k, exposure[expo_index[k]], gain)
    flat = jnp.cos(elev)
    sx = gain * flat * jnp.cos(azim)
    sy = gain * flat * jnp.sin(azim)
    sz = gain * jnp.sin(elev)
    pairs = (sx * sx, sx * sy, sx * sz, sy * sy, sy * sz, sz * sz)
    singles = (sx, sy, sz)
    step = 16
    lane = lane_ids(step)
    masks = [(lane >= s - w) & (lane < s + w) for s, w in zip(STARTS, WIDTHS)]

    def block(i, carry):
        at = pl.ds(pl.multiple_of(i * step, step), step)
        acc = [None] * MOMENTS
        for k in range(count):
            w = weights[k, at, :].astype(F32)
            u = w * images[k, at, :].astype(F32)
            for m, table in enumerate(pairs):
                term = w * table[k : k + 1, :1]
                acc[m] = term if k == 0 else acc[m] + term
            for m, table in enumerate(singles):
                term = u * table[k : k + 1, :1]
                acc[6 + m] = term if k == 0 else acc[6 + m] + term
        for m in range(MOMENTS):
            sums[m, at, :] = acc[m]
        packed = jnp.zeros((step, LANES), F32)
        planes = [0.5 * height[at, :], 0.5 * albedo[at, :]] + acc
        for start, mask, plane in zip(STARTS, masks, planes):
            ends = jnp.where(lane < LANES // 2, plane[:, :LANES], plane[:, -LANES:])
            packed = jnp.where(mask, pltpu.roll(ends, start, 1), packed)
        edges[at, :] = packed
        return carry

    lax.fori_loop(0, rows // step, block, 0)


def rows_kernel(height, albedo, mine, theirs, sides, out):
    rows = height.shape[0]
    start = pl.multiple_of(lax.axis_index("img") * (rows - ROW), ROW)
    at = pl.ds(start, ROW)
    out[pl.ds(0, ROW), :] = height[at, :]
    out[pl.ds(ROW, ROW), :] = albedo[at, :]
    for m in range(MOMENTS):
        out[pl.ds((2 + m) * ROW, ROW), :] = mine[m, at, :] + theirs[m, at, :]
    both = jnp.where(east_lanes(lane_ids(ROW)), sides[1, at, :], sides[0, at, :])
    out[pl.ds(PLANES * ROW, ROW), :] = jnp.concatenate([both, both], axis=1)


def steps_kernel(rates, height, albedo, mine, theirs, sides, ends, out_h, out_a, hs, al, mo, gps, gqs):
    rows, cols = height.shape
    first_y = lax.axis_index("gy") == 0
    last_y = lax.axis_index("gy") == lax.axis_size("gy") - 1
    first_x = lax.axis_index("gx") == 0
    last_x = lax.axis_index("gx") == lax.axis_size("gx") - 1
    rate_h, rate_a = rates
    top = 2 * ROW
    bottom = top + rows
    step = 16

    def plane(k):
        return hs if k == 0 else al if k == 1 else mo.at[k - 2]

    east = east_lanes(lane_ids(step))

    def fill(i, carry):
        src = pl.ds(pl.multiple_of(i * step, step), step)
        dst = pl.ds(pl.multiple_of(i * step + top, ROW), step)
        both = jnp.where(east, sides[1, src, :], sides[0, src, :])
        for k in range(PLANES):
            if k == 0:
                body = height[src, :]
            elif k == 1:
                body = albedo[src, :]
            else:
                body = mine[k - 2, src, :] + theirs[k - 2, src, :]
            ref = plane(k)
            ref[0, dst, :] = body[:, :LANES]
            ref[1, dst, :] = body[:, LANES:]
            ref[2, dst, :] = pltpu.roll(both, LANES - STARTS[k], 1)
        return carry

    lax.fori_loop(0, rows // step, fill, 0)
    for side, row in ((0, top - ROW), (1, bottom)):
        both = ends[side, pl.ds(PLANES * ROW, ROW), :LANES]
        for k in range(PLANES):
            ref = plane(k)
            body = ends[side, pl.ds(k * ROW, ROW), :]
            ref[0, pl.ds(row, ROW), :] = body[:, :LANES]
            ref[1, pl.ds(row, ROW), :] = body[:, LANES:]
            ref[2, pl.ds(row, ROW), :] = pltpu.roll(both, LANES - STARTS[k], 1)

    lane = lane_ids(ROW)
    head = lane == 0
    tail = lane == LANES - 1
    wall_w = head & first_x
    wall_e = tail & last_x

    def beside(blocks, sign):
        fore = [pltpu.roll(b, LANES - 1, 1) for b in blocks]
        back = [pltpu.roll(b, 1, 1) for b in blocks]
        easts = [jnp.where(tail, fore[(t + 1) % 3], fore[t]) for t in range(3)]
        wests = [jnp.where(head, back[(t + 2) % 3], back[t]) for t in range(3)]
        easts[1] = jnp.where(wall_e, sign * blocks[1], easts[1])
        wests[0] = jnp.where(wall_w, sign * blocks[0], wests[0])
        return easts, wests

    def borders(ref, sign):
        @pl.when(first_y)
        def _():
            ref[:, pl.ds(top - 1, 1), :] = sign * ref[:, pl.ds(top, 1), :]

        @pl.when(last_y)
        def _():
            ref[:, pl.ds(bottom, 1), :] = sign * ref[:, pl.ds(bottom - 1, 1), :]

    def slopes(i, carry):
        base = pl.multiple_of(i * ROW, ROW)
        at = pl.ds(pl.multiple_of(base + ROW, ROW), ROW)
        tall = [hs[t, pl.ds(base, 3 * ROW), :] for t in range(3)]
        easts, wests = beside([v[ROW : 2 * ROW] for v in tall], 1.0)
        for t in range(3):
            p = 0.5 * (easts[t] - wests[t])
            q = 0.5 * (tall[t][ROW + 1 : 2 * ROW + 1] - tall[t][ROW - 1 : 2 * ROW - 1])
            scale = lax.rsqrt(1.0 + p * p + q * q)
            xx, xy, xz, yy, yz, zz, vx, vy, vz = [mo[m, t, at, :] for m in range(MOMENTS)]
            alb = al[t, at, :]
            lit = alb * scale
            gx = lit * (xz - p * xx - q * xy) - vx
            gy = lit * (yz - p * xy - q * yy) - vy
            gz = lit * (zz - p * xz - q * yz) - vz
            grad_a = scale * (gz - p * gx - q * gy)
            turn = scale * grad_a
            gps[t, at, :] = 0.3 * p - lit * (gx + p * turn)
            gqs[t, at, :] = 0.3 * q - lit * (gy + q * turn)
            al[t, at, :] = alb - rate_a * grad_a
        return carry

    def descend(i, carry):
        base = pl.multiple_of(i * ROW, ROW)
        at = pl.ds(pl.multiple_of(base + ROW, ROW), ROW)
        easts, wests = beside([gps[t, at, :] for t in range(3)], -1.0)
        for t in range(3):
            tall = gqs[t, pl.ds(base, 3 * ROW), :]
            grad_h = 0.5 * (wests[t] - easts[t]) + 0.5 * (
                tall[ROW - 1 : 2 * ROW - 1] - tall[ROW + 1 : 2 * ROW + 1]
            )
            hs[t, at, :] = hs[t, at, :] - rate_h * grad_h
        return carry

    blocks = (rows + 2 * ROW) // ROW
    borders(hs, 1.0)

    def iterate(n, carry):
        lax.fori_loop(0, blocks, slopes, 0)
        borders(gqs, -1.0)
        lax.fori_loop(0, blocks, descend, 0)
        borders(hs, 1.0)
        return carry

    lax.fori_loop(0, ITERS, iterate, 0)
    center = pl.ds(top, rows)
    for t in range(2):
        lanes = pl.ds(t * LANES, LANES)
        out_h[:, lanes] = hs[t, center, :]
        out_a[:, lanes] = al[t, center, :]


def pair_groups(sizes, axis):
    ny, nx = sizes

    def flat(y, x, core):
        return (y % ny * nx + x % nx) * 2 + core

    dy, dx = (1, 0) if axis == "gy" else (0, 1)
    return [[flat(y, x, 1), flat(y + dy, x + dx, 0)] for y in range(ny) for x in range(nx)]


def from_next(x, axis, core):
    groups = pair_groups((lax.axis_size("gy"), lax.axis_size("gx")), axis)
    both = lax.all_gather(x, AXES, axis_index_groups=groups)
    return lax.dynamic_index_in_dim(both, core, 0, keepdims=False)


VMEM = pl.BlockSpec(memory_space=pltpu.VMEM)
SMEM = pl.BlockSpec(memory_space=pltpu.SMEM)


def shards(
    heights, albedo, images, weights, sun_index, expo_index, sun_azimuth, sun_elevation, exposure
):
    rows, cols = heights.shape
    core = lax.axis_index("img")
    total = images.shape[0] * lax.axis_size("img")
    shape = jax.ShapeDtypeStruct
    mine, edges = pl.pallas_call(
        moments_kernel,
        out_shape=(shape((MOMENTS, rows, cols), F32), shape((rows, LANES), F32)),
        in_specs=[SMEM] * 5 + [VMEM] * 4,
        out_specs=(VMEM, VMEM),
        compiler_params=pltpu.CompilerParams(vmem_limit_bytes=24 << 20),
        name="moments",
    )(sun_index, expo_index, sun_azimuth, sun_elevation, exposure, heights, albedo, images, weights)
    swap = [(i, i ^ 1) for i in range(2)]
    theirs = lax.ppermute(mine, "img", swap)
    edges = jnp.sum(lax.all_gather(edges, "img"), axis=0)
    sides = lax.all_gather(from_next(edges, "gx", core), "img")
    ends = pl.pallas_call(
        rows_kernel,
        out_shape=shape(((PLANES + 1) * ROW, cols), F32),
        in_specs=[VMEM] * 5,
        out_specs=VMEM,
        compiler_params=pltpu.CompilerParams(vmem_limit_bytes=24 << 20),
        name="edge_rows",
    )(heights, albedo, mine, theirs, sides)
    ends = lax.all_gather(from_next(ends, "gy", core), "img")
    tall = rows + 4 * ROW
    return pl.pallas_call(
        functools.partial(steps_kernel, (0.2 / total, 0.5 / total)),
        out_shape=(shape((rows, cols), F32), shape((rows, cols), F32)),
        in_specs=[VMEM] * 6,
        out_specs=(VMEM, VMEM),
        scratch_shapes=[
            pltpu.VMEM((3, tall, LANES), F32),
            pltpu.VMEM((3, tall, LANES), F32),
            pltpu.VMEM((MOMENTS, 3, tall, LANES), F32),
            pltpu.VMEM((3, tall, LANES), F32),
            pltpu.VMEM((3, tall, LANES), F32),
        ],
        compiler_params=pltpu.CompilerParams(vmem_limit_bytes=24 << 20),
        name="gradient_steps",
    )(heights, albedo, mine, theirs, sides, ends)


def solution(mesh):
    return jax.shard_map(
        shards,
        mesh=mesh,
        in_specs=(
            P("gy", "gx"),
            P("gy", "gx"),
            P("img", "gy", "gx"),
            P("img", "gy", "gx"),
            P("img"),
            P("img"),
            P(),
            P(),
            P(),
        ),
        out_specs=(P("gy", "gx"), P("gy", "gx")),
        check_vma=False,
    )
```

```python
import functools

import jax
import jax.numpy as jnp
from jax import lax
from jax.experimental import pallas as pl
from jax.experimental.pallas import tpu as pltpu
from jax.sharding import PartitionSpec as P

ITERS = 3
AXES = ("gy", "gx", "img")
LANES = 128
ROW = 8
CHUNKS = 4
MOMENTS = 9
PLANES = 2 + MOMENTS
WIDTHS = (6,) + (5,) * (PLANES - 1)
STARTS = tuple(6 if k == 0 else 17 + 10 * (k - 1) for k in range(PLANES))
F32 = jnp.float32


def lane_ids(rows):
    return lax.broadcasted_iota(jnp.int32, (rows, LANES), 1)


def east_lanes(lane):
    hit = lane < 0
    for start, width in zip(STARTS, WIDTHS):
        hit = hit | ((lane >= start) & (lane < start + width))
    return hit


def moments_kernel(
    sun_index_hbm, expo_index_hbm, azimuth_hbm, elevation_hbm, exposure_hbm, height_hbm, albedo_hbm, images_hbm,
    weights_hbm, height, albedo, keep, send, edges, sun_index, expo_index, azimuth, elevation, exposure, images,
    weights, sums, small_sems, large_sems
):
    count, rows, _ = images.shape
    small = [
        pltpu.make_async_copy(src, dst, small_sems.at[n])
        for n, (src, dst) in enumerate((
            (sun_index_hbm, sun_index), (expo_index_hbm, expo_index), (azimuth_hbm, azimuth),
            (elevation_hbm, elevation), (exposure_hbm, exposure),
        ))
    ]
    for copy in small:
        copy.start()
    part = rows // CHUNKS
    large = []
    for c in range(CHUNKS):
        at = pl.ds(c * part, part)
        large.append([
            pltpu.make_async_copy(weights_hbm.at[:, at, :], weights.at[:, at, :], large_sems.at[c, 0]),
            pltpu.make_async_copy(images_hbm.at[:, at, :], images.at[:, at, :], large_sems.at[c, 1]),
            pltpu.make_async_copy(height_hbm.at[at, :], height.at[at, :], large_sems.at[c, 2]),
            pltpu.make_async_copy(albedo_hbm.at[at, :], albedo.at[at, :], large_sems.at[c, 3]),
        ])
        for copy in large[c]:
            copy.start()
    for copy in small:
        copy.wait()
    line = lax.broadcasted_iota(jnp.int32, (ROW, LANES), 0)
    azim = jnp.zeros((ROW, LANES), F32)
    elev = jnp.zeros((ROW, LANES), F32)
    gain = jnp.zeros((ROW, LANES), F32)
    for k in range(count):
        azim = jnp.where(line == k, azimuth[sun_index[k]], azim)
        elev = jnp.where(line == k, elevation[sun_index[k]], elev)
        gain = jnp.where(line == k, exposure[expo_index[k]], gain)
    flat = jnp.cos(elev)
    sx = gain * flat * jnp.cos(azim)
    sy = gain * flat * jnp.sin(azim)
    sz = gain * jnp.sin(elev)
    factors = (sx * sx, sx * sy, sx * sz, sy * sy, sy * sz, sz * sz, sx, sy, sz)
    step = 16
    lane = lane_ids(step)
    masks = [(lane >= s - w) & (lane < s + w) for s, w in zip(STARTS, WIDTHS)]

    for c in range(CHUNKS):
        for copy in large[c]:
            copy.wait()
        for i in range(c * part, (c + 1) * part, step):
            at = pl.ds(i, step)
            acc = [None] * MOMENTS
            for k in range(count):
                w = weights[k, at, :].astype(F32)
                u = w * images[k, at, :].astype(F32)
                for m, factor in enumerate(factors):
                    term = (w if m < 6 else u) * factor[k : k + 1, :1]
                    acc[m] = term if k == 0 else acc[m] + term
            for m in range(MOMENTS):
                sums[m, at, :] = acc[m]
            packed = jnp.zeros((step, LANES), F32)
            planes = [0.5 * height[at, :], 0.5 * albedo[at, :]] + acc
            for start, mask, plane in zip(STARTS, masks, planes):
                ends = jnp.where(lane < LANES // 2, plane[:, :LANES], plane[:, -LANES:])
                packed = jnp.where(mask, pltpu.roll(ends, start, 1), packed)
            edges[at, :] = packed
    core = lax.axis_index("img")
    for out, first in ((keep, core), (send, 1 - core)):
        first = first * (rows - out.shape[1])
        for m in range(MOMENTS):
            for i in range(0, out.shape[1], ROW):
                out[m, pl.ds(i, ROW), :] = sums[m, pl.ds(pl.multiple_of(first + i, ROW), ROW), :]


def place_kernel(halves, height, albedo, sems):
    half = halves.shape[2]
    copies = [
        pltpu.make_async_copy(halves.at[c, n], out.at[pl.ds(c * half, half), :], sems.at[c, n])
        for c in range(2)
        for n, out in enumerate((height, albedo))
    ]
    for copy in copies:
        copy.start()
    for copy in copies:
        copy.wait()


def rows_kernel(height, albedo, sums, sides, out):
    rows = height.shape[0]
    core = lax.axis_index("img")
    at = pl.ds(pl.multiple_of(core * (rows - ROW), ROW), ROW)
    of_sums = pl.ds(pl.multiple_of(core * (sums.shape[1] - ROW), ROW), ROW)
    out[pl.ds(0, ROW), :] = height[at, :]
    out[pl.ds(ROW, ROW), :] = albedo[at, :]
    for m in range(MOMENTS):
        out[pl.ds((2 + m) * ROW, ROW), :] = sums[m, of_sums, :]
    both = jnp.where(east_lanes(lane_ids(ROW)), sides[1, at, :], sides[0, at, :])
    out[pl.ds(PLANES * ROW, ROW), :] = jnp.concatenate([both, both], axis=1)


def steps_kernel(rates, height, albedo, sums, sides, ends, out, hs, al, mo, gps, gqs):
    rows, cols = height.shape
    own = sums.shape[1]
    half = rows // 2
    core = lax.axis_index("img")
    first_y = (lax.axis_index("gy") == 0) & (core == 0)
    last_y = (lax.axis_index("gy") == lax.axis_size("gy") - 1) & (core == 1)
    first_x = lax.axis_index("gx") == 0
    last_x = lax.axis_index("gx") == lax.axis_size("gx") - 1
    rate_h, rate_a = rates
    top = 2 * ROW
    bottom = top + half

    def plane(k):
        return hs if k == 0 else al if k == 1 else mo.at[k - 2]

    east = east_lanes(lane_ids(ROW))
    first = core * (rows - own)
    place = top - core * ROW
    for i in range(0, own, ROW):
        src = pl.ds(pl.multiple_of(first + i, ROW), ROW)
        dst = pl.ds(pl.multiple_of(place + i, ROW), ROW)
        both = jnp.where(east, sides[1, src, :], sides[0, src, :])
        for k in range(PLANES):
            if k == 0:
                body = height[src, :]
            elif k == 1:
                body = albedo[src, :]
            else:
                body = sums[k - 2, pl.ds(i, ROW), :]
            ref = plane(k)
            ref[0, dst, :] = body[:, :LANES]
            ref[1, dst, :] = body[:, LANES:]
            ref[2, dst, :] = pltpu.roll(both, LANES - STARTS[k], 1)
    dst = pl.ds(pl.multiple_of(ROW + core * own, ROW), ROW)
    both = ends[pl.ds(PLANES * ROW, ROW), :LANES]
    for k in range(PLANES):
        ref = plane(k)
        body = ends[pl.ds(k * ROW, ROW), :]
        ref[0, dst, :] = body[:, :LANES]
        ref[1, dst, :] = body[:, LANES:]
        ref[2, dst, :] = pltpu.roll(both, LANES - STARTS[k], 1)

    lane = lane_ids(ROW)
    head = lane == 0
    tail = lane == LANES - 1
    wall_w = head & first_x
    wall_e = tail & last_x

    def beside(blocks, sign):
        fore = [pltpu.roll(b, LANES - 1, 1) for b in blocks]
        back = [pltpu.roll(b, 1, 1) for b in blocks]
        easts = [jnp.where(tail, fore[(t + 1) % 3], fore[t]) for t in range(3)]
        wests = [jnp.where(head, back[(t + 2) % 3], back[t]) for t in range(3)]
        easts[1] = jnp.where(wall_e, sign * blocks[1], easts[1])
        wests[0] = jnp.where(wall_w, sign * blocks[0], wests[0])
        return easts, wests

    def borders(ref, sign):
        @pl.when(first_y)
        def _():
            ref[:, pl.ds(top - 1, 1), :] = sign * ref[:, pl.ds(top, 1), :]

        @pl.when(last_y)
        def _():
            ref[:, pl.ds(bottom, 1), :] = sign * ref[:, pl.ds(bottom - 1, 1), :]

    def slopes(i, carry):
        base = pl.multiple_of(i * ROW, ROW)
        at = pl.ds(pl.multiple_of(base + ROW, ROW), ROW)
        easts, wests = beside([hs[t, at, :] for t in range(3)], 1.0)
        for t in range(3):
            p = 0.5 * (easts[t] - wests[t])
            q = 0.5 * (hs[t, pl.ds(base + ROW + 1, ROW), :] - hs[t, pl.ds(base + ROW - 1, ROW), :])
            scale = lax.rsqrt(1.0 + p * p + q * q)
            xx, xy, xz, yy, yz, zz, vx, vy, vz = [mo[m, t, at, :] for m in range(MOMENTS)]
            alb = al[t, at, :]
            lit = alb * scale
            gx = lit * (xz - p * xx - q * xy) - vx
            gy = lit * (yz - p * xy - q * yy) - vy
            gz = lit * (zz - p * xz - q * yz) - vz
            grad_a = scale * (gz - p * gx - q * gy)
            turn = scale * grad_a
            bend = 0.3 - lit * turn
            gps[t, at, :] = p * bend - lit * gx
            gqs[t, at, :] = q * bend - lit * gy
            al[t, at, :] = alb - rate_a * grad_a
        return carry

    def descend(i, carry):
        base = pl.multiple_of(i * ROW, ROW)
        at = pl.ds(pl.multiple_of(base + ROW, ROW), ROW)
        easts, wests = beside([gps[t, at, :] for t in range(3)], -1.0)
        for t in range(3):
            grad_h = 0.5 * (wests[t] - easts[t]) + 0.5 * (
                gqs[t, pl.ds(base + ROW - 1, ROW), :] - gqs[t, pl.ds(base + ROW + 1, ROW), :]
            )
            hs[t, at, :] = hs[t, at, :] - rate_h * grad_h
        return carry

    blocks = half // ROW + 2
    borders(hs, 1.0)

    def iterate(n, carry):
        lax.fori_loop(0, blocks, slopes, 0, unroll=blocks)
        borders(gqs, -1.0)
        lax.fori_loop(0, blocks, descend, 0, unroll=blocks)
        borders(hs, 1.0)
        return carry

    lax.fori_loop(0, ITERS, iterate, 0)
    center = pl.ds(top, half)
    for t in range(2):
        lanes = pl.ds(t * LANES, LANES)
        out[0, :, lanes] = hs[t, center, :]
        out[1, :, lanes] = al[t, center, :]


def pair_groups(sizes, axis):
    ny, nx = sizes

    def flat(y, x, core):
        return (y * nx + x) * 2 + core

    if axis == "gx":
        groups = [[flat(y, x, 1), flat(y, x + 1, 0)] for y in range(ny) for x in range(nx - 1)]
        for y in range(0, ny, 2):
            groups += [[flat(y, x, core), flat(y + 1, x, core)] for x, core in ((0, 0), (nx - 1, 1))]
    else:
        groups = [[flat(y, x, 1), flat(y + 1, x, 0)] for y in range(ny - 1) for x in range(nx)]
        for x in range(0, nx, 2):
            groups += [[flat(y, x, core), flat(y, x + 1, core)] for y, core in ((0, 0), (ny - 1, 1))]
    return groups


def from_next(x, axis, core):
    groups = pair_groups((lax.axis_size("gy"), lax.axis_size("gx")), axis)
    both = lax.all_gather(x, AXES, axis_index_groups=groups)
    return lax.dynamic_index_in_dim(both, core, 0, keepdims=False)


VMEM = pl.BlockSpec(memory_space=pltpu.VMEM)
HBM = pl.BlockSpec(memory_space=pltpu.HBM)


def in_vmem(*args):
    return tuple(pltpu.with_memory_space_constraint(x, pltpu.VMEM) for x in args)


def params(mib):
    return pltpu.CompilerParams(vmem_limit_bytes=mib << 20)


def run_moments(*args):
    args = tuple(pltpu.with_memory_space_constraint(x, pltpu.HBM) for x in args)
    rows, cols = args[5].shape
    part = pltpu.VMEM((MOMENTS, rows // 2 + ROW, cols), F32)
    return pl.pallas_call(
        moments_kernel,
        out_shape=tuple(pltpu.VMEM(x.shape, x.dtype) for x in args[5:7])
        + (part, part, pltpu.VMEM((rows, LANES), F32)),
        in_specs=[HBM] * len(args),
        out_specs=(VMEM,) * 5,
        scratch_shapes=[pltpu.SMEM(x.shape, x.dtype) for x in args[:5]]
        + [pltpu.VMEM(x.shape, x.dtype) for x in args[7:]]
        + [pltpu.VMEM((MOMENTS, rows, cols), F32)]
        + [pltpu.SemaphoreType.DMA((5,)), pltpu.SemaphoreType.DMA((CHUNKS, 4))],
        compiler_params=params(8),
        name="moments",
    )(*args)


def run_rows(heights, albedo, sums, sides):
    return pl.pallas_call(
        rows_kernel,
        out_shape=pltpu.VMEM(((PLANES + 1) * ROW, heights.shape[1]), F32),
        in_specs=[VMEM] * 4,
        out_specs=VMEM,
        compiler_params=params(8),
        name="edge_rows",
    )(*in_vmem(heights, albedo, sums, sides))


def run_steps(total, heights, albedo, sums, sides, ends):
    rows, cols = heights.shape
    block = pltpu.VMEM((3, rows // 2 + 4 * ROW, LANES), F32)
    return pl.pallas_call(
        functools.partial(steps_kernel, (0.2 / total, 0.5 / total)),
        out_shape=pltpu.VMEM((2, rows // 2, cols), F32),
        in_specs=[VMEM] * 5,
        out_specs=VMEM,
        scratch_shapes=[block, block, pltpu.VMEM((MOMENTS, *block.shape), F32), block, block],
        compiler_params=params(12),
        name="gradient_steps",
    )(*in_vmem(heights, albedo, sums, sides, ends))


def run_place(halves):
    _, _, half, cols = halves.shape
    out = jax.ShapeDtypeStruct((2 * half, cols), F32)
    return pl.pallas_call(
        place_kernel,
        out_shape=(out, out),
        in_specs=[VMEM],
        out_specs=(HBM, HBM),
        scratch_shapes=[pltpu.SemaphoreType.DMA((2, 2))],
        compiler_params=params(8),
        name="place",
    )(*in_vmem(halves))


def shards(
    heights, albedo, images, weights, sun_index, expo_index, sun_azimuth, sun_elevation, exposure
):
    total = images.shape[0] * lax.axis_size("img")
    core = lax.axis_index("img")
    heights, albedo, keep, send, edges = run_moments(
        sun_index, expo_index, sun_azimuth, sun_elevation, exposure, heights, albedo, images, weights
    )
    edges, send = lax.optimization_barrier((lax.all_gather(edges, "img"), send))
    theirs = lax.ppermute(send, "img", [(0, 1), (1, 0)])
    edges = jnp.sum(edges, axis=0)
    sides = lax.all_gather(from_next(edges, "gx", core), "img")
    sums = keep + theirs
    ends = from_next(run_rows(heights, albedo, sums, sides), "gy", core)
    halves = run_steps(total, heights, albedo, sums, sides, ends)
    return run_place(lax.all_gather(halves, "img"))


def solution(mesh):
    return jax.shard_map(
        shards,
        mesh=mesh,
        in_specs=(
            P("gy", "gx"),
            P("gy", "gx"),
            P("img", "gy", "gx"),
            P("img", "gy", "gx"),
            P("img"),
            P("img"),
            P(),
            P(),
            P(),
        ),
        out_specs=(P("gy", "gx"), P("gy", "gx")),
        check_vma=False,
    )
```

```python
import functools

import jax
import jax.numpy as jnp
from jax import lax
from jax.experimental import pallas as pl
from jax.experimental.pallas import tpu as pltpu
from jax.sharding import PartitionSpec as P

ITERS = 3
AXES = ("gy", "gx", "img")
LANES = 128
ROW = 8
CHUNKS = 4
MOMENTS = 9
PLANES = 2 + MOMENTS
WIDTHS = (6,) + (5,) * (PLANES - 1)
STARTS = tuple(6 if k == 0 else 17 + 10 * (k - 1) for k in range(PLANES))
ROW_STARTS = tuple(sum(WIDTHS[:k]) for k in range(PLANES + 1))
F32 = jnp.float32


def lane_ids(rows):
    return lax.broadcasted_iota(jnp.int32, (rows, LANES), 1)


def east_lanes(lane):
    hit = lane < 0
    for start, width in zip(STARTS, WIDTHS):
        hit = hit | ((lane >= start) & (lane < start + width))
    return hit


def edges_kernel(
    sun_index_hbm, expo_index_hbm, azimuth_hbm, elevation_hbm, exposure_hbm, height_hbm, albedo_hbm, images_hbm,
    weights_hbm, height, albedo, images, weights, tables, own_fold, own_rows, pack, sun_index, expo_index, azimuth,
    elevation, exposure, folds, ends_of_rows, small_sems, large_sems
):
    count, _, half, _ = images.shape
    small = [
        pltpu.make_async_copy(src, dst, small_sems.at[n])
        for n, (src, dst) in enumerate((
            (sun_index_hbm, sun_index), (expo_index_hbm, expo_index), (azimuth_hbm, azimuth),
            (elevation_hbm, elevation), (exposure_hbm, exposure),
        ))
    ]
    for copy in small:
        copy.start()
    part = half // CHUNKS
    large = []
    for c in range(CHUNKS):
        at = pl.ds(c * part, part)
        large.append([
            pltpu.make_async_copy(weights_hbm.at[:, :, at, :], weights.at[:, :, at, :], large_sems.at[c, 0]),
            pltpu.make_async_copy(images_hbm.at[:, :, at, :], images.at[:, :, at, :], large_sems.at[c, 1]),
            pltpu.make_async_copy(height_hbm.at[:, at, :], height.at[:, at, :], large_sems.at[c, 2]),
            pltpu.make_async_copy(albedo_hbm.at[:, at, :], albedo.at[:, at, :], large_sems.at[c, 3]),
        ])
        for copy in large[c]:
            copy.start()
    for copy in small:
        copy.wait()
    line = lax.broadcasted_iota(jnp.int32, (ROW, LANES), 0)
    azim = jnp.zeros((ROW, LANES), F32)
    elev = jnp.zeros((ROW, LANES), F32)
    gain = jnp.zeros((ROW, LANES), F32)
    for k in range(count):
        azim = jnp.where(line == k, azimuth[sun_index[k]], azim)
        elev = jnp.where(line == k, elevation[sun_index[k]], elev)
        gain = jnp.where(line == k, exposure[expo_index[k]], gain)
    flat = jnp.cos(elev)
    sx = gain * flat * jnp.cos(azim)
    sy = gain * flat * jnp.sin(azim)
    sz = gain * jnp.sin(elev)
    factors = (sx * sx, sx * sy, sx * sz, sy * sy, sy * sz, sz * sz, sx, sy, sz)
    for m, factor in enumerate(factors):
        tables[m] = factor
    step = 16
    lane = lane_ids(step)

    def sums(s, at, view):
        return add_moments(
            lambda k: view(weights[k, s, at, :].astype(F32)), lambda k: view(images[k, s, at, :].astype(F32)), count,
            lambda m, k: factors[m][k : k + 1, :1]
        )

    def ends(x):
        return jnp.where(lane < LANES // 2, x[:, :LANES], x[:, -LANES:])

    for c in range(CHUNKS):
        for copy in large[c]:
            copy.wait()
        for i in range(c * part, (c + 1) * part, step):
            at = pl.ds(i, step)
            upper, lower = (
                [ends(0.5 * height[s, at, :]), ends(0.5 * albedo[s, at, :])] + sums(s, at, ends) for s in range(2)
            )
            west = jnp.zeros((step, LANES), F32)
            east = jnp.zeros((step, LANES), F32)
            for start, width, above, below in zip(STARTS, WIDTHS, upper, lower):
                low = (lane >= start - width) & (lane < start)
                high = (lane >= start) & (lane < start + width)
                above = pltpu.roll(above, start, 1)
                west = jnp.where(high, above, jnp.where(low, pltpu.roll(below, start - width, 1), west))
                east = jnp.where(low, above, jnp.where(high, pltpu.roll(below, start + width, 1), east))
            folds[0, at, :] = west
            folds[1, at, :] = east
    for side, first in enumerate((0, half - step)):
        acc = sums(side, pl.ds(first, step), lambda x: x)
        for m in range(MOMENTS):
            ends_of_rows[side, m] = acc[m][:ROW] if side == 0 else acc[m][-ROW:]
    core = lax.axis_index("img")
    own_fold[...] = folds[core]
    pack[pl.ds(0, half), :] = folds[1 - core]
    for m in range(MOMENTS):
        own_rows[pl.ds(m * ROW, ROW), :] = ends_of_rows[core, m]
        for t in range(2):
            pack[pl.ds(half + (2 * m + t) * ROW, ROW), :] = ends_of_rows[1 - core, m, :, t * LANES : (t + 1) * LANES]


def add_moments(weight, image, count, factor):
    acc = [None] * MOMENTS
    for k in range(count):
        w = weight(k)
        u = w * image(k)
        for m in range(MOMENTS):
            term = (w if m < 6 else u) * factor(m, k)
            acc[m] = term if k == 0 else acc[m] + term
    return acc


def moments_kernel(images, weights, tables, keep, send, sums):
    count, rows, _ = images.shape
    step = 16
    for i in range(0, rows, step):
        at = pl.ds(i, step)
        acc = add_moments(
            lambda k: weights[k, at, :].astype(F32), lambda k: images[k, at, :].astype(F32), count,
            lambda m, k: tables[m, k : k + 1, :1]
        )
        for m in range(MOMENTS):
            sums[m, at, :] = acc[m]
    core = lax.axis_index("img")
    for out, first in ((keep, core), (send, 1 - core)):
        first = first * (rows - out.shape[1])
        for m in range(MOMENTS):
            for i in range(0, out.shape[1], ROW):
                out[m, pl.ds(i, ROW), :] = sums[m, pl.ds(pl.multiple_of(first + i, ROW), ROW), :]


def place_kernel(halves, height, albedo, sems):
    half = halves.shape[2]
    copies = [
        pltpu.make_async_copy(halves.at[c, n], out.at[pl.ds(c * half, half), :], sems.at[c, n])
        for c in range(2)
        for n, out in enumerate((height, albedo))
    ]
    for copy in copies:
        copy.start()
    for copy in copies:
        copy.wait()


def rows_kernel(height, albedo, own_rows, packs, sides, both, out):
    rows = height.shape[0]
    half = rows // 2
    core = lax.axis_index("img")
    lane = lane_ids(ROW)
    east = east_lanes(lane)
    wide = lane < STARTS[0] + WIDTHS[0]
    for i in range(0, half, ROW):
        at = pl.ds(i, ROW)
        west_side, east_side = sides[0, at, :], sides[1, at, :]
        both[at, :] = jnp.where(east, east_side, west_side)
        moved_e, moved_w = (
            jnp.where(wide, pltpu.roll(x, 6 * d % LANES, 1), pltpu.roll(x, 5 * d % LANES, 1))
            for x, d in ((east_side, 1), (west_side, -1))
        )
        both[pl.ds(half + i, ROW), :] = jnp.where(east, moved_e, moved_w)
    at = pl.ds(pl.multiple_of(core * (rows - ROW), ROW), ROW)
    upper = core == 0

    def edge(x, n):
        return jnp.where(upper, x[:n], x[ROW - n :])

    out[pl.ds(0, WIDTHS[0]), :] = edge(height[at, :], WIDTHS[0])
    for k in range(1, PLANES):
        if k == 1:
            plane = albedo[at, :]
        else:
            m = k - 2
            theirs = [packs[1 - core, pl.ds(half + (2 * m + t) * ROW, ROW), :] for t in range(2)]
            plane = own_rows[pl.ds(m * ROW, ROW), :] + jnp.concatenate(theirs, axis=1)
        out[pl.ds(ROW_STARTS[k], WIDTHS[k]), :] = edge(plane, WIDTHS[k])
    corner = both[at, :]
    out[pl.ds(ROW_STARTS[PLANES], ROW), :] = jnp.concatenate([corner, corner], axis=1)


def fill_kernel(height, albedo, keep, both, ends, hs, al, mo):
    rows = height.shape[0]
    own = keep.shape[1]
    core = lax.axis_index("img")

    def plane(k):
        return hs if k == 0 else al if k == 1 else mo.at[k - 2]

    first = core * (rows - own)
    place = 2 * ROW - core * ROW
    for i in range(0, own, ROW):
        src = pl.ds(pl.multiple_of(first + i, ROW), ROW)
        dst = pl.ds(pl.multiple_of(place + i, ROW), ROW)
        sides = both[src, :]
        for k in range(PLANES):
            body = height[src, :] if k == 0 else albedo[src, :] if k == 1 else keep[k - 2, pl.ds(i, ROW), :]
            ref = plane(k)
            ref[0, dst, :] = body[:, :LANES]
            ref[1, dst, :] = body[:, LANES:]
            ref[2, dst, :] = pltpu.roll(sides, LANES - STARTS[k], 1)
    dst = pl.ds(pl.multiple_of(ROW + core * own, ROW), ROW)
    sides = ends[pl.ds(ROW_STARTS[PLANES], ROW), :LANES]
    for k in range(PLANES):
        ref = plane(k)
        begin, spare = ROW_STARTS[k], ROW - WIDTHS[k]
        after = ends[pl.ds(begin, ROW), :]
        before = pltpu.roll(after, spare, 0) if k == 0 else ends[pl.ds(begin - spare, ROW), :]
        body = jnp.where(core == 0, before, after)
        ref[0, dst, :] = body[:, :LANES]
        ref[1, dst, :] = body[:, LANES:]
        ref[2, dst, :] = pltpu.roll(sides, LANES - STARTS[k], 1)


def steps_kernel(rates, hs_in, al_in, mo_in, theirs, out, hs, al, mo, gps, gqs):
    own = theirs.shape[1]
    half = out.shape[1]
    core = lax.axis_index("img")
    first_y = (lax.axis_index("gy") == 0) & (core == 0)
    last_y = (lax.axis_index("gy") == lax.axis_size("gy") - 1) & (core == 1)
    first_x = lax.axis_index("gx") == 0
    last_x = lax.axis_index("gx") == lax.axis_size("gx") - 1
    rate_h, rate_a = rates
    top = 2 * ROW
    bottom = top + half
    place = top - core * ROW
    for i in range(0, own, ROW):
        dst = pl.ds(pl.multiple_of(place + i, ROW), ROW)
        for m in range(MOMENTS):
            for t in range(2):
                mo[m, t, dst, :] += theirs[m, pl.ds(i, ROW), t * LANES : (t + 1) * LANES]

    lane = lane_ids(ROW)
    head = lane == 0
    tail = lane == LANES - 1
    wall_w = head & first_x
    wall_e = tail & last_x

    def beside(blocks, sign):
        fore = [pltpu.roll(b, LANES - 1, 1) for b in blocks]
        back = [pltpu.roll(b, 1, 1) for b in blocks]
        easts = [jnp.where(tail, fore[(t + 1) % 3], fore[t]) for t in range(3)]
        wests = [jnp.where(head, back[(t + 2) % 3], back[t]) for t in range(3)]
        easts[1] = jnp.where(wall_e, sign * blocks[1], easts[1])
        wests[0] = jnp.where(wall_w, sign * blocks[0], wests[0])
        return easts, wests

    def borders(ref, sign):
        @pl.when(first_y)
        def _():
            ref[:, pl.ds(top - 1, 1), :] = sign * ref[:, pl.ds(top, 1), :]

        @pl.when(last_y)
        def _():
            ref[:, pl.ds(bottom, 1), :] = sign * ref[:, pl.ds(bottom - 1, 1), :]

    def slopes(i, carry):
        base = pl.multiple_of(i * ROW, ROW)
        at = pl.ds(pl.multiple_of(base + ROW, ROW), ROW)
        easts, wests = beside([hs[t, at, :] for t in range(3)], 1.0)
        for t in range(3):
            p = 0.5 * (easts[t] - wests[t])
            q = 0.5 * (hs[t, pl.ds(base + ROW + 1, ROW), :] - hs[t, pl.ds(base + ROW - 1, ROW), :])
            scale = lax.rsqrt(1.0 + p * p + q * q)
            xx, xy, xz, yy, yz, zz, vx, vy, vz = [mo[m, t, at, :] for m in range(MOMENTS)]
            alb = al[t, at, :]
            lit = alb * scale
            gx = lit * (xz - p * xx - q * xy) - vx
            gy = lit * (yz - p * xy - q * yy) - vy
            gz = lit * (zz - p * xz - q * yz) - vz
            grad_a = scale * (gz - p * gx - q * gy)
            turn = scale * grad_a
            bend = 0.3 - lit * turn
            gps[t, at, :] = p * bend - lit * gx
            gqs[t, at, :] = q * bend - lit * gy
            al[t, at, :] = alb - rate_a * grad_a
        return carry

    def descend(i, carry):
        base = pl.multiple_of(i * ROW, ROW)
        at = pl.ds(pl.multiple_of(base + ROW, ROW), ROW)
        easts, wests = beside([gps[t, at, :] for t in range(3)], -1.0)
        for t in range(3):
            grad_h = 0.5 * (wests[t] - easts[t]) + 0.5 * (
                gqs[t, pl.ds(base + ROW - 1, ROW), :] - gqs[t, pl.ds(base + ROW + 1, ROW), :]
            )
            hs[t, at, :] = hs[t, at, :] - rate_h * grad_h
        return carry

    blocks = half // ROW + 2
    borders(hs, 1.0)

    def iterate(n, carry):
        lax.fori_loop(0, blocks, slopes, 0, unroll=blocks)
        borders(gqs, -1.0)
        lax.fori_loop(0, blocks, descend, 0, unroll=blocks)
        borders(hs, 1.0)
        return carry

    lax.fori_loop(0, ITERS, iterate, 0)
    center = pl.ds(top, half)
    for t in range(2):
        lanes = pl.ds(t * LANES, LANES)
        out[0, :, lanes] = hs[t, center, :]
        out[1, :, lanes] = al[t, center, :]


def pair_groups(sizes):
    ny, nx = sizes

    def flat(y, x, core):
        return (y * nx + x) * 2 + core

    groups = [[flat(y, x, 1), flat(y, x + 1, 0)] for y in range(ny) for x in range(nx - 1)]
    for y in range(0, ny, 2):
        groups += [[flat(y, x, core), flat(y + 1, x, core)] for x, core in ((0, 0), (nx - 1, 1))]
    return groups


def from_next(x, core):
    groups = pair_groups((lax.axis_size("gy"), lax.axis_size("gx")))
    both = lax.all_gather(x, AXES, axis_index_groups=groups)
    return lax.dynamic_index_in_dim(both, core, 0, keepdims=False)


def neighbours(sizes):
    ny, nx = sizes

    def flat(y, x, core):
        return (y * nx + x) * 2 + core

    pairs = [(flat(y, x, 1), flat(y + 1, x, 0)) for y in range(ny - 1) for x in range(nx)]
    return pairs + [(b, a) for a, b in pairs]


VMEM = pl.BlockSpec(memory_space=pltpu.VMEM)
HBM = pl.BlockSpec(memory_space=pltpu.HBM)


def in_vmem(*args):
    return tuple(pltpu.with_memory_space_constraint(x, pltpu.VMEM) for x in args)


def cost(mib):
    return pl.CostEstimate(flops=1 << 20, bytes_accessed=mib << 20, transcendentals=0)


def params(mib):
    return pltpu.CompilerParams(vmem_limit_bytes=mib << 20)


def run_edges(sun_index, expo_index, azimuth, elevation, exposure, heights, albedo, images, weights):
    rows, cols = heights.shape
    half = rows // 2
    tiles = [x.reshape(*x.shape[:-2], 2, half, cols) for x in (heights, albedo, images, weights)]
    args = [
        pltpu.with_memory_space_constraint(x, pltpu.HBM)
        for x in (sun_index, expo_index, azimuth, elevation, exposure, *tiles)
    ]
    out = pl.pallas_call(
        edges_kernel,
        out_shape=tuple(pltpu.VMEM(x.shape, x.dtype) for x in tiles)
        + (
            pltpu.VMEM((MOMENTS, ROW, LANES), F32),
            pltpu.VMEM((half, LANES), F32),
            pltpu.VMEM((MOMENTS * ROW, cols), F32),
            pltpu.VMEM((half + 2 * MOMENTS * ROW, LANES), F32),
        ),
        in_specs=[HBM] * len(args),
        out_specs=(VMEM,) * 8,
        scratch_shapes=[pltpu.SMEM(x.shape, x.dtype) for x in args[:5]]
        + [pltpu.VMEM((2, half, LANES), F32), pltpu.VMEM((2, MOMENTS, ROW, cols), F32)]
        + [pltpu.SemaphoreType.DMA((5,)), pltpu.SemaphoreType.DMA((CHUNKS, 4))],
        compiler_params=params(8),
        name="edges",
    )(*args)
    return tuple(x.reshape(*x.shape[:-3], rows, cols) for x in out[:4]) + out[4:]


def run_moments(images, weights, tables):
    _, rows, cols = images.shape
    part = pltpu.VMEM((MOMENTS, rows // 2 + ROW, cols), F32)
    return pl.pallas_call(
        moments_kernel,
        out_shape=(part, part),
        in_specs=[VMEM] * 3,
        out_specs=(VMEM, VMEM),
        scratch_shapes=[pltpu.VMEM((MOMENTS, rows, cols), F32)],
        compiler_params=params(8),
        cost_estimate=cost(4),
        name="moments",
    )(*in_vmem(images, weights, tables))


def run_rows(heights, albedo, own_rows, packs, sides):
    rows, cols = heights.shape
    return pl.pallas_call(
        rows_kernel,
        out_shape=(pltpu.VMEM((rows, LANES), F32), pltpu.VMEM((ROW_STARTS[PLANES] + ROW, cols), F32)),
        in_specs=[VMEM] * 5,
        out_specs=(VMEM,) * 2,
        compiler_params=params(8),
        name="edge_rows",
    )(*in_vmem(heights, albedo, own_rows, packs, sides))


def frame(rows):
    return (3, rows // 2 + 4 * ROW, LANES)


def run_fill(heights, albedo, keep, both, ends):
    block = pltpu.VMEM(frame(heights.shape[0]), F32)
    return pl.pallas_call(
        fill_kernel,
        out_shape=(block, block, pltpu.VMEM((MOMENTS, *block.shape), F32)),
        in_specs=[VMEM] * 5,
        out_specs=(VMEM,) * 3,
        compiler_params=params(8),
        cost_estimate=pl.CostEstimate(flops=1 << 34, bytes_accessed=1 << 20, transcendentals=0),
        name="fill",
    )(*in_vmem(heights, albedo, keep, both, ends))


def run_steps(total, hs, al, mo, theirs):
    _, tall, _ = hs.shape
    half = tall - 4 * ROW
    block = pltpu.VMEM(hs.shape, F32)
    return pl.pallas_call(
        functools.partial(steps_kernel, (0.2 / total, 0.5 / total)),
        out_shape=(pltpu.VMEM((2, half, 2 * LANES), F32), block, block, pltpu.VMEM(mo.shape, F32)),
        in_specs=[VMEM] * 4,
        out_specs=(VMEM,) * 4,
        scratch_shapes=[block, block],
        input_output_aliases={0: 1, 1: 2, 2: 3},
        compiler_params=params(8),
        name="gradient_steps",
    )(*in_vmem(hs, al, mo, theirs))[0]


def run_place(halves):
    _, _, half, cols = halves.shape
    out = jax.ShapeDtypeStruct((2 * half, cols), F32)
    return pl.pallas_call(
        place_kernel,
        out_shape=(out, out),
        in_specs=[VMEM],
        out_specs=(HBM, HBM),
        scratch_shapes=[pltpu.SemaphoreType.DMA((2, 2))],
        compiler_params=params(8),
        name="place",
    )(*in_vmem(halves))


def shards(
    heights, albedo, images, weights, sun_index, expo_index, sun_azimuth, sun_elevation, exposure
):
    total = images.shape[0] * lax.axis_size("img")
    core = lax.axis_index("img")
    heights, albedo, images, weights, tables, own_fold, own_rows, pack = run_edges(
        sun_index, expo_index, sun_azimuth, sun_elevation, exposure, heights, albedo, images, weights
    )
    packs = lax.all_gather(pack, "img")
    fold = own_fold + lax.dynamic_index_in_dim(packs, 1 - core, 0, keepdims=False)[: own_fold.shape[0]]
    sides = lax.all_gather(from_next(fold, core), "img")
    both, ends = run_rows(heights, albedo, own_rows, packs, sides)
    ends, images = lax.optimization_barrier((ends, images))
    ends = lax.ppermute(ends, AXES, neighbours((lax.axis_size("gy"), lax.axis_size("gx"))))
    keep, send = run_moments(images, weights, tables)
    theirs = lax.ppermute(send, "img", [(0, 1), (1, 0)])
    halves = run_steps(total, *run_fill(heights, albedo, keep, both, ends), theirs)
    return run_place(lax.all_gather(halves, "img"))


def solution(mesh):
    return jax.shard_map(
        shards,
        mesh=mesh,
        in_specs=(
            P("gy", "gx"),
            P("gy", "gx"),
            P("img", "gy", "gx"),
            P("img", "gy", "gx"),
            P("img"),
            P("img"),
            P(),
            P(),
            P(),
        ),
        out_specs=(P("gy", "gx"), P("gy", "gx")),
        check_vma=False,
    )
```

```python
import functools

import jax
import jax.numpy as jnp
from jax import lax
from jax.experimental import pallas as pl
from jax.experimental.pallas import tpu as pltpu
from jax.sharding import PartitionSpec as P

ITERS = 3
AXES = ("gy", "gx", "img")
LANES = 128
ROW = 8
CHUNKS = 2
MOMENTS = 9
PLANES = 2 + MOMENTS
WIDTHS = (6,) + (5,) * (PLANES - 1)
STARTS = tuple(6 if k == 0 else 17 + 10 * (k - 1) for k in range(PLANES))
ROW_STARTS = tuple(sum(WIDTHS[:k]) for k in range(PLANES + 1))
F32 = jnp.float32


def lane_ids(rows):
    return lax.broadcasted_iota(jnp.int32, (rows, LANES), 1)


def east_lanes(lane):
    hit = lane < 0
    for start, width in zip(STARTS, WIDTHS):
        hit = hit | ((lane >= start) & (lane < start + width))
    return hit


def edges_kernel(
    sun_index_hbm, expo_index_hbm, azimuth_hbm, elevation_hbm, exposure_hbm, height_hbm, albedo_hbm, images_hbm,
    weights_hbm, height, albedo, images, weights, tables, own_fold, own_rows, pack, sun_index, expo_index, azimuth,
    elevation, exposure, folds, ends_of_rows, small_sems, large_sems
):
    count, _, half, _ = images.shape
    small = [
        pltpu.make_async_copy(src, dst, small_sems.at[n])
        for n, (src, dst) in enumerate((
            (sun_index_hbm, sun_index), (expo_index_hbm, expo_index), (azimuth_hbm, azimuth),
            (elevation_hbm, elevation), (exposure_hbm, exposure),
        ))
    ]
    for copy in small:
        copy.start()
    part = half // CHUNKS
    large = []
    for c in range(CHUNKS):
        at = pl.ds(c * part, part)
        large.append([
            pltpu.make_async_copy(weights_hbm.at[:, :, at, :], weights.at[:, :, at, :], large_sems.at[c, 0]),
            pltpu.make_async_copy(images_hbm.at[:, :, at, :], images.at[:, :, at, :], large_sems.at[c, 1]),
        ])
    large.append([
        pltpu.make_async_copy(height_hbm, height, large_sems.at[CHUNKS, 0]),
        pltpu.make_async_copy(albedo_hbm, albedo, large_sems.at[CHUNKS, 1]),
    ])
    for copies in large:
        for copy in copies:
            copy.start()
    for copy in small:
        copy.wait()
    line = lax.broadcasted_iota(jnp.int32, (ROW, LANES), 0)
    azim = jnp.zeros((ROW, LANES), F32)
    elev = jnp.zeros((ROW, LANES), F32)
    gain = jnp.zeros((ROW, LANES), F32)
    for k in range(count):
        azim = jnp.where(line == k, azimuth[sun_index[k]], azim)
        elev = jnp.where(line == k, elevation[sun_index[k]], elev)
        gain = jnp.where(line == k, exposure[expo_index[k]], gain)
    flat = jnp.cos(elev)
    sx = gain * flat * jnp.cos(azim)
    sy = gain * flat * jnp.sin(azim)
    sz = gain * jnp.sin(elev)
    factors = (sx * sx, sx * sy, sx * sz, sy * sy, sy * sz, sz * sz, sx, sy, sz)
    for m, factor in enumerate(factors):
        tables[m] = factor
    lane = lane_ids(ROW)
    block = jnp.zeros((ROW, LANES), F32)
    for m, factor in enumerate(factors):
        block = jnp.where(lane == m, factor, block)
    pack[pl.ds(half + 2 * MOMENTS * ROW, ROW), :] = block
    step = 16
    lane = lane_ids(step)

    def sums(s, at, view):
        return add_moments(
            lambda k: view(weights[k, s, at, :].astype(F32)), lambda k: view(images[k, s, at, :].astype(F32)), count,
            lambda m, k: factors[m][k : k + 1, :1]
        )

    def ends(x):
        return jnp.where(lane < LANES // 2, x[:, :LANES], x[:, -LANES:])

    def fold(planes, first, west, east):
        for above, below, start, width in zip(*planes, STARTS[first:], WIDTHS[first:]):
            low = (lane >= start - width) & (lane < start)
            high = (lane >= start) & (lane < start + width)
            above = pltpu.roll(above, start, 1)
            west = jnp.where(high, above, jnp.where(low, pltpu.roll(below, start - width, 1), west))
            east = jnp.where(low, above, jnp.where(high, pltpu.roll(below, start + width, 1), east))
        return west, east

    def edge_rows(side, first):
        acc = sums(side, pl.ds(first, step), lambda x: x)
        for m in range(MOMENTS):
            ends_of_rows[side, m] = acc[m][:ROW] if side == 0 else acc[m][-ROW:]

    zero = jnp.zeros((step, LANES), F32)
    for c in range(CHUNKS):
        for copy in large[c]:
            copy.wait()
        for i in range(c * part, (c + 1) * part, step):
            at = pl.ds(i, step)
            folds[0, at, :], folds[1, at, :] = fold([sums(s, at, ends) for s in range(2)], 2, zero, zero)
        if c == 0:
            edge_rows(0, 0)
        if c == CHUNKS - 1:
            edge_rows(1, half - step)
    core = lax.axis_index("img")
    for m in range(MOMENTS):
        own_rows[pl.ds(m * ROW, ROW), :] = ends_of_rows[core, m]
        for t in range(2):
            pack[pl.ds(half + (2 * m + t) * ROW, ROW), :] = ends_of_rows[1 - core, m, :, t * LANES : (t + 1) * LANES]
    for copy in large[CHUNKS]:
        copy.wait()
    for i in range(0, half, step):
        at = pl.ds(i, step)
        planes = [[ends(0.5 * height[s, at, :]), ends(0.5 * albedo[s, at, :])] for s in range(2)]
        west, east = fold(planes, 0, folds[0, at, :], folds[1, at, :])
        own_fold[at, :] = jnp.where(core == 0, west, east)
        pack[at, :] = jnp.where(core == 0, east, west)


def add_moments(weight, image, count, factor):
    acc = [None] * MOMENTS
    for k in range(count):
        w = weight(k)
        u = w * image(k)
        for m in range(MOMENTS):
            term = (w if m < 6 else u) * factor(m, k)
            acc[m] = term if k == 0 else acc[m] + term
    return acc


def part_rows(core, half):
    step = 16
    near = pl.multiple_of(core * (half - step), step)
    yield 1 - core, pl.ds(near, step), None
    for i in range(0, half, step):
        yield core, pl.ds(i, step), pl.ds(ROW + i, step)


def put(out, plane, dst, value, core):
    if dst is None:
        out[plane, pl.ds(0, ROW), :] = jnp.where(core == 0, value[:ROW], value[-ROW:])
    else:
        out[plane, dst, :] = value


def sent_kernel(images, weights, tables, out):
    count, _, half, _ = images.shape
    core = 1 - lax.axis_index("img")
    for s, at, dst in part_rows(core, half):
        acc = [None] * 3
        for k in range(count):
            w = weights[k, s, at, :].astype(F32)
            put(out, k, dst, w, core)
            u = w * images[k, s, at, :].astype(F32)
            for m in range(3):
                term = u * tables[6 + m, k : k + 1, :1]
                acc[m] = term if k == 0 else acc[m] + term
        for m in range(3):
            put(out, count + m, dst, acc[m], core)


def own_kernel(images, weights, tables, out):
    count, _, half, _ = images.shape
    core = lax.axis_index("img")
    for s, at, dst in part_rows(core, half):
        acc = add_moments(
            lambda k: weights[k, s, at, :].astype(F32), lambda k: images[k, s, at, :].astype(F32), count,
            lambda m, k: tables[m, k : k + 1, :1]
        )
        for m in range(MOMENTS):
            put(out, m, dst, acc[m], core)


def place_kernel(halves, height, albedo, sems):
    half = halves.shape[2]
    copies = [
        pltpu.make_async_copy(halves.at[c, n], out.at[pl.ds(c * half, half), :], sems.at[c, n])
        for c in range(2)
        for n, out in enumerate((height, albedo))
    ]
    for copy in copies:
        copy.start()
    for copy in copies:
        copy.wait()


def rows_kernel(height, albedo, own_rows, packs, sides, both, out):
    rows = height.shape[0]
    half = rows // 2
    core = lax.axis_index("img")
    lane = lane_ids(ROW)
    east = east_lanes(lane)
    wide = lane < STARTS[0] + WIDTHS[0]
    for i in range(0, half, ROW):
        at = pl.ds(i, ROW)
        west_side, east_side = sides[0, at, :], sides[1, at, :]
        both[at, :] = jnp.where(east, east_side, west_side)
        moved_e, moved_w = (
            jnp.where(wide, pltpu.roll(x, 6 * d % LANES, 1), pltpu.roll(x, 5 * d % LANES, 1))
            for x, d in ((east_side, 1), (west_side, -1))
        )
        both[pl.ds(half + i, ROW), :] = jnp.where(east, moved_e, moved_w)
    at = pl.ds(pl.multiple_of(core * (rows - ROW), ROW), ROW)
    upper = core == 0

    def edge(x, n):
        return jnp.where(upper, x[:n], x[ROW - n :])

    out[pl.ds(0, WIDTHS[0]), :] = edge(height[at, :], WIDTHS[0])
    for k in range(1, PLANES):
        if k == 1:
            plane = albedo[at, :]
        else:
            m = k - 2
            theirs = [packs[1 - core, pl.ds(half + (2 * m + t) * ROW, ROW), :] for t in range(2)]
            plane = own_rows[pl.ds(m * ROW, ROW), :] + jnp.concatenate(theirs, axis=1)
        out[pl.ds(ROW_STARTS[k], WIDTHS[k]), :] = edge(plane, WIDTHS[k])
    corner = both[at, :]
    out[pl.ds(ROW_STARTS[PLANES], ROW), :] = jnp.concatenate([corner, corner], axis=1)


def inner_row(core, half):
    return ROW + (1 - core) * (half + ROW)


def fill_kernel(height, albedo, keep, both, ends, hs, al, mo):
    rows = height.shape[0]
    core = lax.axis_index("img")

    def plane(k):
        return hs if k == 0 else al if k == 1 else mo.at[k - 2]

    half = rows // 2
    inner = core * (half - ROW) + (1 - core) * half
    for i in range(-ROW, half, ROW):
        if i < 0:
            src, dst = pl.ds(pl.multiple_of(inner, ROW), ROW), pl.ds(pl.multiple_of(inner_row(core, half), ROW), ROW)
        else:
            src, dst = pl.ds(pl.multiple_of(core * half + i, ROW), ROW), pl.ds(2 * ROW + i, ROW)
        sides = both[src, :]
        for k in range(PLANES):
            body = height[src, :] if k == 0 else albedo[src, :] if k == 1 else keep[k - 2, pl.ds(ROW + i, ROW), :]
            ref = plane(k)
            ref[0, dst, :] = body[:, :LANES]
            ref[1, dst, :] = body[:, LANES:]
            ref[2, dst, :] = pltpu.roll(sides, LANES - STARTS[k], 1)
    dst = pl.ds(pl.multiple_of(inner_row(1 - core, half), ROW), ROW)
    sides = ends[pl.ds(ROW_STARTS[PLANES], ROW), :LANES]
    for k in range(PLANES):
        ref = plane(k)
        begin, spare = ROW_STARTS[k], ROW - WIDTHS[k]
        after = ends[pl.ds(begin, ROW), :]
        before = pltpu.roll(after, spare, 0) if k == 0 else ends[pl.ds(begin - spare, ROW), :]
        body = jnp.where(core == 0, before, after)
        ref[0, dst, :] = body[:, :LANES]
        ref[1, dst, :] = body[:, LANES:]
        ref[2, dst, :] = pltpu.roll(sides, LANES - STARTS[k], 1)


def steps_kernel(rates, hs_in, al_in, mo_in, theirs, packs, out, hs, al, mo, gps, gqs):
    half = out.shape[1]
    core = lax.axis_index("img")
    first_y = (lax.axis_index("gy") == 0) & (core == 0)
    last_y = (lax.axis_index("gy") == lax.axis_size("gy") - 1) & (core == 1)
    first_x = lax.axis_index("gx") == 0
    last_x = lax.axis_index("gx") == lax.axis_size("gx") - 1
    rate_h, rate_a = rates
    top = 2 * ROW
    bottom = top + half
    hs[...] = 0.5 * hs_in[...]
    al[...] = al_in[...]
    outer = pl.ds(pl.multiple_of(inner_row(1 - core, half), ROW), ROW)
    inner = pl.ds(pl.multiple_of(inner_row(core, half), ROW), ROW)
    count = theirs.shape[0] - 3
    table = packs[1 - core, packs.shape[1] - ROW :, :]
    factors = [[jnp.broadcast_to(table[k : k + 1, m : m + 1], (ROW, LANES)) for k in range(count)] for m in range(6)]
    for t in range(2):
        lanes = slice(t * LANES, (t + 1) * LANES)
        for i in range(-ROW, half, ROW):
            src = pl.ds(ROW + i, ROW)
            at = inner if i < 0 else pl.ds(top + i, ROW)
            w = [theirs[k, src, lanes] for k in range(count)]
            for m in range(MOMENTS):
                if m < 6:
                    extra = sum((w[k] * factors[m][k] for k in range(1, count)), w[0] * factors[m][0])
                else:
                    extra = theirs[count + m - 6, src, lanes]
                mo[m, t, at, :] = mo_in[m, t, at, :] + extra
        for m in range(MOMENTS):
            mo[m, t, outer, :] = mo_in[m, t, outer, :]

    lane = lane_ids(ROW)
    head = lane == 0
    tail = lane == LANES - 1
    wall_w = head & first_x
    wall_e = tail & last_x

    def beside(blocks, sign):
        fore = [pltpu.roll(b, LANES - 1, 1) for b in blocks]
        back = [pltpu.roll(b, 1, 1) for b in blocks]
        easts = [jnp.where(tail, fore[(t + 1) % 3], fore[t]) for t in range(3)]
        wests = [jnp.where(head, back[(t + 2) % 3], back[t]) for t in range(3)]
        easts[1] = jnp.where(wall_e, sign * blocks[1], easts[1])
        wests[0] = jnp.where(wall_w, sign * blocks[0], wests[0])
        return easts, wests

    def borders(ref, sign):
        @pl.when(first_y)
        def _():
            ref[:, pl.ds(top - 1, 1), :] = sign * ref[:, pl.ds(top, 1), :]

        @pl.when(last_y)
        def _():
            ref[:, pl.ds(bottom, 1), :] = sign * ref[:, pl.ds(bottom - 1, 1), :]

    def slopes(i, carry):
        base = pl.multiple_of(i * ROW, ROW)
        at = pl.ds(pl.multiple_of(base + ROW, ROW), ROW)
        easts, wests = beside([hs[t, at, :] for t in range(3)], 1.0)
        for t in range(3):
            p = easts[t] - wests[t]
            q = hs[t, pl.ds(base + ROW + 1, ROW), :] - hs[t, pl.ds(base + ROW - 1, ROW), :]
            scale = lax.rsqrt(1.0 + p * p + q * q)
            xx, xy, xz, yy, yz, zz, vx, vy, vz = [(mo if t < 2 else mo_in)[m, t, at, :] for m in range(MOMENTS)]
            alb = al[t, at, :]
            lit = alb * scale
            gx = lit * (xz - p * xx - q * xy) - vx
            gy = lit * (yz - p * xy - q * yy) - vy
            gz = lit * (zz - p * xz - q * yz) - vz
            grad_a = scale * (gz - p * gx - q * gy)
            turn = scale * grad_a
            bend = 0.3 - lit * turn
            gps[t, at, :] = p * bend - lit * gx
            gqs[t, at, :] = q * bend - lit * gy
            al[t, at, :] = alb - rate_a * grad_a
        return carry

    def descend(i, carry):
        base = pl.multiple_of(i * ROW, ROW)
        at = pl.ds(pl.multiple_of(base + ROW, ROW), ROW)
        easts, wests = beside([gps[t, at, :] for t in range(3)], -1.0)
        for t in range(3):
            fall = (wests[t] - easts[t]) + (gqs[t, pl.ds(base + ROW - 1, ROW), :] - gqs[t, pl.ds(base + ROW + 1, ROW), :])
            hs[t, at, :] = hs[t, at, :] - (0.25 * rate_h) * fall
        return carry

    blocks = half // ROW + 2
    borders(hs, 1.0)

    for _ in range(ITERS):
        lax.fori_loop(0, blocks, slopes, 0, unroll=blocks)
        borders(gqs, -1.0)
        lax.fori_loop(0, blocks, descend, 0, unroll=blocks)
        borders(hs, 1.0)
    center = pl.ds(top, half)
    for t in range(2):
        lanes = pl.ds(t * LANES, LANES)
        out[0, :, lanes] = 2.0 * hs[t, center, :]
        out[1, :, lanes] = al[t, center, :]


def pair_groups(sizes):
    ny, nx = sizes

    def flat(y, x, core):
        return (y * nx + x) * 2 + core

    groups = [[flat(y, x, 1), flat(y, x + 1, 0)] for y in range(ny) for x in range(nx - 1)]
    for y in range(0, ny, 2):
        groups += [[flat(y, x, core), flat(y + 1, x, core)] for x, core in ((0, 0), (nx - 1, 1))]
    return groups


def from_next(x, core):
    groups = pair_groups((lax.axis_size("gy"), lax.axis_size("gx")))
    both = lax.all_gather(x, AXES, axis_index_groups=groups)
    return lax.dynamic_index_in_dim(both, core, 0, keepdims=False)


def neighbours(sizes):
    ny, nx = sizes

    def flat(y, x, core):
        return (y * nx + x) * 2 + core

    pairs = [(flat(y, x, 1), flat(y + 1, x, 0)) for y in range(ny - 1) for x in range(nx)]
    return pairs + [(b, a) for a, b in pairs]


VMEM = pl.BlockSpec(memory_space=pltpu.VMEM)
HBM = pl.BlockSpec(memory_space=pltpu.HBM)


def in_vmem(*args):
    return tuple(pltpu.with_memory_space_constraint(x, pltpu.VMEM) for x in args)


def cost(mib):
    return pl.CostEstimate(flops=1 << 20, bytes_accessed=mib << 20, transcendentals=0)


def params(mib):
    return pltpu.CompilerParams(vmem_limit_bytes=mib << 20)


def run_edges(sun_index, expo_index, azimuth, elevation, exposure, heights, albedo, images, weights):
    rows, cols = heights.shape
    half = rows // 2
    tiles = [x.reshape(*x.shape[:-2], 2, half, cols) for x in (heights, albedo, images, weights)]
    args = [
        pltpu.with_memory_space_constraint(x, pltpu.HBM)
        for x in (sun_index, expo_index, azimuth, elevation, exposure, *tiles)
    ]
    out = pl.pallas_call(
        edges_kernel,
        out_shape=tuple(pltpu.VMEM(x.shape, x.dtype) for x in tiles)
        + (
            pltpu.VMEM((MOMENTS, ROW, LANES), F32),
            pltpu.VMEM((half, LANES), F32),
            pltpu.VMEM((MOMENTS * ROW, cols), F32),
            pltpu.VMEM((half + 2 * MOMENTS * ROW + ROW, LANES), F32),
        ),
        in_specs=[HBM] * len(args),
        out_specs=(VMEM,) * 8,
        scratch_shapes=[pltpu.SMEM(x.shape, x.dtype) for x in args[:5]]
        + [pltpu.VMEM((2, half, LANES), F32), pltpu.VMEM((2, MOMENTS, ROW, cols), F32)]
        + [pltpu.SemaphoreType.DMA((5,)), pltpu.SemaphoreType.DMA((CHUNKS + 1, 2))],
        compiler_params=params(8),
        name="edges",
    )(*args)
    return tuple(x.reshape(rows, cols) for x in out[:2]) + out[2:]


def run_moments(kernel, planes, images, weights, tables):
    _, _, half, cols = images.shape
    return pl.pallas_call(
        kernel,
        out_shape=pltpu.VMEM((planes, half + ROW, cols), F32),
        in_specs=[VMEM] * 3,
        out_specs=VMEM,
        compiler_params=params(8),
        cost_estimate=cost(4),
        name=kernel.__name__,
    )(*in_vmem(images, weights, tables))


def run_rows(heights, albedo, own_rows, packs, sides):
    rows, cols = heights.shape
    return pl.pallas_call(
        rows_kernel,
        out_shape=(pltpu.VMEM((rows, LANES), F32), pltpu.VMEM((ROW_STARTS[PLANES] + ROW, cols), F32)),
        in_specs=[VMEM] * 5,
        out_specs=(VMEM,) * 2,
        compiler_params=params(8),
        name="edge_rows",
    )(*in_vmem(heights, albedo, own_rows, packs, sides))


def frame(rows):
    return (3, rows // 2 + 4 * ROW, LANES)


def run_fill(heights, albedo, keep, both, ends):
    block = pltpu.VMEM(frame(heights.shape[0]), F32)
    return pl.pallas_call(
        fill_kernel,
        out_shape=(block, block, pltpu.VMEM((MOMENTS, *block.shape), F32)),
        in_specs=[VMEM] * 5,
        out_specs=(VMEM,) * 3,
        compiler_params=params(8),
        cost_estimate=pl.CostEstimate(flops=1 << 34, bytes_accessed=1 << 20, transcendentals=0),
        name="fill",
    )(*in_vmem(heights, albedo, keep, both, ends))


def run_steps(total, hs, al, mo, theirs, packs):
    _, tall, _ = hs.shape
    half = tall - 4 * ROW
    block = pltpu.VMEM(hs.shape, F32)
    return pl.pallas_call(
        functools.partial(steps_kernel, (0.2 / total, 0.5 / total)),
        out_shape=pltpu.VMEM((2, half, 2 * LANES), F32),
        in_specs=[VMEM] * 5,
        out_specs=VMEM,
        scratch_shapes=[block, block, pltpu.VMEM((MOMENTS, 2, tall, LANES), F32), block, block],
        compiler_params=params(8),
        name="gradient_steps",
    )(*in_vmem(hs, al, mo, theirs, packs))


def run_place(halves):
    _, _, half, cols = halves.shape
    out = jax.ShapeDtypeStruct((2 * half, cols), F32)
    return pl.pallas_call(
        place_kernel,
        out_shape=(out, out),
        in_specs=[VMEM],
        out_specs=(HBM, HBM),
        scratch_shapes=[pltpu.SemaphoreType.DMA((2, 2))],
        compiler_params=params(8),
        name="place",
    )(*in_vmem(halves))


def shards(
    heights, albedo, images, weights, sun_index, expo_index, sun_azimuth, sun_elevation, exposure
):
    total = images.shape[0] * lax.axis_size("img")
    core = lax.axis_index("img")
    heights, albedo, images, weights, tables, own_fold, own_rows, pack = run_edges(
        sun_index, expo_index, sun_azimuth, sun_elevation, exposure, heights, albedo, images, weights
    )
    packs = lax.all_gather(pack, "img")
    fold = own_fold + lax.dynamic_index_in_dim(packs, 1 - core, 0, keepdims=False)[: own_fold.shape[0]]
    sides = lax.all_gather(from_next(fold, core), "img")
    both, ends = run_rows(heights, albedo, own_rows, packs, sides)
    ends, images = lax.optimization_barrier((ends, images))
    ends = lax.ppermute(ends, AXES, neighbours((lax.axis_size("gy"), lax.axis_size("gx"))))
    send = run_moments(sent_kernel, images.shape[0] + 3, images, weights, tables)
    theirs = lax.ppermute(send, "img", [(0, 1), (1, 0)])
    keep = run_moments(own_kernel, MOMENTS, images, weights, tables)
    halves = run_steps(total, *run_fill(heights, albedo, keep, both, ends), theirs, packs)
    return run_place(lax.all_gather(halves, "img"))


def solution(mesh):
    return jax.shard_map(
        shards,
        mesh=mesh,
        in_specs=(
            P("gy", "gx"),
            P("gy", "gx"),
            P("img", "gy", "gx"),
            P("img", "gy", "gx"),
            P("img"),
            P("img"),
            P(),
            P(),
            P(),
        ),
        out_specs=(P("gy", "gx"), P("gy", "gx")),
        check_vma=False,
    )
```

```python
import functools

import jax
import jax.numpy as jnp
from jax import lax
from jax.experimental import pallas as pl
from jax.experimental.pallas import tpu as pltpu
from jax.sharding import PartitionSpec as P

ITERS = 3
AXES = ("gy", "gx", "img")
LANES = 128
ROW = 8
CHUNKS = 2
MOMENTS = 9
PLANES = 2 + MOMENTS
WIDTHS = (6,) + (5,) * (PLANES - 1)
STARTS = tuple(6 if k == 0 else 17 + 10 * (k - 1) for k in range(PLANES))
ROW_STARTS = tuple(sum(WIDTHS[:k]) for k in range(PLANES + 1))
F32 = jnp.float32


def lane_ids(rows):
    return lax.broadcasted_iota(jnp.int32, (rows, LANES), 1)


def east_lanes(lane):
    hit = lane < 0
    for start, width in zip(STARTS, WIDTHS):
        hit = hit | ((lane >= start) & (lane < start + width))
    return hit


def edges_kernel(
    sun_index_hbm, expo_index_hbm, azimuth_hbm, elevation_hbm, exposure_hbm, height_hbm, albedo_hbm, images_hbm,
    weights_hbm, height, albedo, images, weights, tables, own_fold, own_rows, pack, sun_index, expo_index, azimuth,
    elevation, exposure, spreads, ends_of_rows, small_sems, large_sems
):
    count, _, half, _ = images.shape
    small = [
        pltpu.make_async_copy(src, dst, small_sems.at[n])
        for n, (src, dst) in enumerate((
            (sun_index_hbm, sun_index), (expo_index_hbm, expo_index), (azimuth_hbm, azimuth),
            (elevation_hbm, elevation), (exposure_hbm, exposure),
        ))
    ]
    part = half // CHUNKS
    large = []
    for c in range(CHUNKS):
        at = pl.ds(c * part, part)
        large.append([
            pltpu.make_async_copy(weights_hbm.at[:, :, at, :], weights.at[:, :, at, :], large_sems.at[c, 0]),
            pltpu.make_async_copy(images_hbm.at[:, :, at, :], images.at[:, :, at, :], large_sems.at[c, 1]),
        ])
    large.append([
        pltpu.make_async_copy(height_hbm, height, large_sems.at[CHUNKS, 0]),
        pltpu.make_async_copy(albedo_hbm, albedo, large_sems.at[CHUNKS, 1]),
    ])
    for copies in large:
        for copy in copies:
            copy.start()
    for copy in small:
        copy.start()
    for copy in small:
        copy.wait()
    line = lax.broadcasted_iota(jnp.int32, (ROW, LANES), 0)
    azim = jnp.zeros((ROW, LANES), F32)
    elev = jnp.zeros((ROW, LANES), F32)
    gain = jnp.zeros((ROW, LANES), F32)
    for k in range(count):
        azim = jnp.where(line == k, azimuth[sun_index[k]], azim)
        elev = jnp.where(line == k, elevation[sun_index[k]], elev)
        gain = jnp.where(line == k, exposure[expo_index[k]], gain)
    flat = jnp.cos(elev)
    sx = gain * flat * jnp.cos(azim)
    sy = gain * flat * jnp.sin(azim)
    sz = gain * jnp.sin(elev)
    factors = (sx * sx, sx * sy, sx * sz, sy * sy, sy * sz, sz * sz, sx, sy, sz)
    for m, factor in enumerate(factors):
        tables[m] = factor
    lane = lane_ids(ROW)
    block = jnp.zeros((ROW, LANES), F32)
    for m, factor in enumerate(factors):
        block = jnp.where(lane == m, factor, block)
    pack[pl.ds(half + 2 * MOMENTS * ROW, ROW), :] = block
    step = 16
    lane = lane_ids(step)

    def sums(view):
        return add_moments(lambda k: view(weights, k), lambda k: view(images, k), count, lambda m, k: factors[m][k : k + 1, :1])

    def ends(x):
        return jnp.where(lane < LANES // 2, x[:, :LANES], x[:, -LANES:])

    middle = (lane >= LANES // 4) & (lane < 3 * LANES // 4)

    def all_ends(upper, lower):
        return jnp.where(middle, pltpu.roll(ends(lower), LANES // 2, 1), ends(upper)).astype(F32)

    def spread(planes, first, upper, lower):
        for plane, start, width in zip(planes, STARTS[first:], WIDTHS[first:]):
            plane = pltpu.roll(plane, start, 1)
            upper = jnp.where((lane >= start - width) & (lane < start + width), plane, upper)
            away = (lane - start - LANES // 2 + width) & (LANES - 1)
            lower = jnp.where(away < 2 * width, plane, lower)
        return upper, lower

    def edge_rows(side):
        at = pl.ds(side * (half - step), step)
        ends_of_rows[side] = jnp.stack(sums(lambda ref, k: ref[k, side, at, :].astype(F32)[side * ROW : (side + 1) * ROW]))

    zero = jnp.zeros((step, LANES), F32)
    for c in range(CHUNKS):
        for copy in large[c]:
            copy.wait()
        for i in range(c * part, (c + 1) * part, step):
            at = pl.ds(i, step)
            planes = sums(lambda ref, k: all_ends(ref[k, 0, at, :], ref[k, 1, at, :]))
            spreads[0, at, :], spreads[1, at, :] = spread(planes, 2, zero, zero)
        if c == 0:
            edge_rows(0)
        if c == CHUNKS - 1:
            edge_rows(1)
    core = lax.axis_index("img")
    for m in range(MOMENTS):
        own_rows[pl.ds(m * ROW, ROW), :] = ends_of_rows[core, m]
        for t in range(2):
            pack[pl.ds(half + (2 * m + t) * ROW, ROW), :] = ends_of_rows[1 - core, m, :, t * LANES : (t + 1) * LANES]
    for copy in large[CHUNKS]:
        copy.wait()
    high = east_lanes(lane)
    wide = lane < STARTS[0] + WIDTHS[0]
    for i in range(0, half, step):
        at = pl.ds(i, step)
        planes = [0.5 * all_ends(x[0, at, :], x[1, at, :]) for x in (height, albedo)]
        upper, lower = spread(planes, 0, spreads[0, at, :], spreads[1, at, :])
        to_west, to_east = (
            jnp.where(wide, pltpu.roll(lower, (64 + 6 * d) % LANES, 1), pltpu.roll(lower, (64 + 5 * d) % LANES, 1))
            for d in (-1, 1)
        )
        west = jnp.where(high, upper, to_west)
        east = jnp.where(high, to_east, upper)
        own_fold[at, :] = jnp.where(core == 0, west, east)
        pack[at, :] = jnp.where(core == 0, east, west)


def add_moments(weight, image, count, factor):
    acc = [None] * MOMENTS
    for k in range(count):
        w = weight(k)
        u = w * image(k)
        for m in range(MOMENTS):
            term = (w if m < 6 else u) * factor(m, k)
            acc[m] = term if k == 0 else acc[m] + term
    return acc


def part_rows(core, half):
    step = 16
    near = pl.multiple_of(core * (half - step), step)
    yield 1 - core, pl.ds(near, step), None
    for i in range(0, half, step):
        yield core, pl.ds(i, step), pl.ds(ROW + i, step)


def put(out, plane, dst, value, core):
    if dst is None:
        out[plane, pl.ds(0, ROW), :] = jnp.where(core == 0, value[:ROW], value[-ROW:])
    else:
        out[plane, dst, :] = value


def sent_kernel(images, weights, tables, out):
    count, _, half, _ = images.shape
    core = 1 - lax.axis_index("img")
    for s, at, dst in part_rows(core, half):
        acc = [None] * 3
        for k in range(count):
            w = weights[k, s, at, :].astype(F32)
            put(out, k, dst, w, core)
            u = w * images[k, s, at, :].astype(F32)
            for m in range(3):
                term = u * tables[6 + m, k : k + 1, :1]
                acc[m] = term if k == 0 else acc[m] + term
        for m in range(3):
            put(out, count + m, dst, acc[m], core)


def own_kernel(images, weights, tables, out):
    count, _, half, _ = images.shape
    core = lax.axis_index("img")
    for s, at, dst in part_rows(core, half):
        acc = add_moments(
            lambda k: weights[k, s, at, :].astype(F32), lambda k: images[k, s, at, :].astype(F32), count,
            lambda m, k: tables[m, k : k + 1, :1]
        )
        for m in range(MOMENTS):
            put(out, m, dst, acc[m], core)


def place_kernel(halves, height, albedo, sems):
    half = halves.shape[2]
    copies = [
        pltpu.make_async_copy(halves.at[c, n], out.at[pl.ds(c * half, half), :], sems.at[c, n])
        for c in range(2)
        for n, out in enumerate((height, albedo))
    ]
    for copy in copies:
        copy.start()
    for copy in copies:
        copy.wait()


def rows_kernel(height, albedo, own_rows, packs, sides, both, out):
    rows = height.shape[0]
    half = rows // 2
    core = lax.axis_index("img")
    lane = lane_ids(ROW)
    east = east_lanes(lane)
    wide = lane < STARTS[0] + WIDTHS[0]
    for i in range(0, half, ROW):
        at = pl.ds(i, ROW)
        west_side, east_side = sides[0, at, :], sides[1, at, :]
        both[at, :] = jnp.where(east, east_side, west_side)
        moved_e, moved_w = (
            jnp.where(wide, pltpu.roll(x, 6 * d % LANES, 1), pltpu.roll(x, 5 * d % LANES, 1))
            for x, d in ((east_side, 1), (west_side, -1))
        )
        both[pl.ds(half + i, ROW), :] = jnp.where(east, moved_e, moved_w)
    at = pl.ds(pl.multiple_of(core * (rows - ROW), ROW), ROW)
    upper = core == 0

    def edge(x, n):
        return jnp.where(upper, x[:n], x[ROW - n :])

    out[pl.ds(0, WIDTHS[0]), :] = edge(height[at, :], WIDTHS[0])
    for k in range(1, PLANES):
        if k == 1:
            plane = albedo[at, :]
        else:
            m = k - 2
            theirs = [packs[1 - core, pl.ds(half + (2 * m + t) * ROW, ROW), :] for t in range(2)]
            plane = own_rows[pl.ds(m * ROW, ROW), :] + jnp.concatenate(theirs, axis=1)
        out[pl.ds(ROW_STARTS[k], WIDTHS[k]), :] = edge(plane, WIDTHS[k])
    corner = both[at, :]
    out[pl.ds(ROW_STARTS[PLANES], ROW), :] = jnp.concatenate([corner, corner], axis=1)


def inner_row(core, half):
    return ROW + (1 - core) * (half + ROW)


def fill_kernel(height, albedo, keep, both, ends, hs, al, mo):
    rows = height.shape[0]
    core = lax.axis_index("img")

    def plane(k):
        return hs if k == 0 else al if k == 1 else mo.at[k - 2]

    half = rows // 2
    inner = core * (half - ROW) + (1 - core) * half
    for i in range(-ROW, half, ROW):
        if i < 0:
            src, dst = pl.ds(pl.multiple_of(inner, ROW), ROW), pl.ds(pl.multiple_of(inner_row(core, half), ROW), ROW)
        else:
            src, dst = pl.ds(pl.multiple_of(core * half + i, ROW), ROW), pl.ds(2 * ROW + i, ROW)
        sides = both[src, :]
        for k in range(PLANES):
            body = height[src, :] if k == 0 else albedo[src, :] if k == 1 else keep[k - 2, pl.ds(ROW + i, ROW), :]
            ref = plane(k)
            ref[0, dst, :] = body[:, :LANES]
            ref[1, dst, :] = body[:, LANES:]
            ref[2, dst, :] = pltpu.roll(sides, LANES - STARTS[k], 1)
    dst = pl.ds(pl.multiple_of(inner_row(1 - core, half), ROW), ROW)
    sides = ends[pl.ds(ROW_STARTS[PLANES], ROW), :LANES]
    for k in range(PLANES):
        ref = plane(k)
        begin, spare = ROW_STARTS[k], ROW - WIDTHS[k]
        after = ends[pl.ds(begin, ROW), :]
        before = pltpu.roll(after, spare, 0) if k == 0 else ends[pl.ds(begin - spare, ROW), :]
        body = jnp.where(core == 0, before, after)
        ref[0, dst, :] = body[:, :LANES]
        ref[1, dst, :] = body[:, LANES:]
        ref[2, dst, :] = pltpu.roll(sides, LANES - STARTS[k], 1)


def steps_kernel(rates, hs_in, al_in, mo_in, theirs, packs, out, hs, al, mo, gps, gqs):
    half = out.shape[1]
    core = lax.axis_index("img")
    first_y = (lax.axis_index("gy") == 0) & (core == 0)
    last_y = (lax.axis_index("gy") == lax.axis_size("gy") - 1) & (core == 1)
    first_x = lax.axis_index("gx") == 0
    last_x = lax.axis_index("gx") == lax.axis_size("gx") - 1
    rate_h, rate_a = rates
    top = 2 * ROW
    bottom = top + half
    hs[...] = 0.5 * hs_in[...]
    al[...] = al_in[...]
    count = theirs.shape[0] - 3
    table = packs[1 - core, packs.shape[1] - ROW :, :]
    factors = [[jnp.broadcast_to(table[k : k + 1, m : m + 1], (ROW, LANES)) for k in range(count)] for m in range(6)]
    for t in range(2):
        lanes = slice(t * LANES, (t + 1) * LANES)
        for i in range(-ROW, half, ROW):
            src = pl.ds(ROW + i, ROW)
            w = [theirs[k, src, lanes] for k in range(count)]
            for m in range(MOMENTS):
                if m < 6:
                    extra = sum((w[k] * factors[m][k] for k in range(1, count)), w[0] * factors[m][0])
                else:
                    extra = theirs[count + m - 6, src, lanes]
                if i >= 0:
                    at = pl.ds(top + i, ROW)
                    mo[m, t, at, :] = mo_in[m, t, at, :] + extra
                else:
                    for at, owner in ((pl.ds(ROW, ROW), 1), (pl.ds(bottom, ROW), 0)):
                        halo = mo_in[m, t, at, :]
                        mo[m, t, at, :] = jnp.where(core == owner, halo + extra, halo)

    def beside(blocks, sign):
        lane = lane_ids(blocks[0].shape[0])
        head = lane == 0
        tail = lane == LANES - 1
        fore = [pltpu.roll(b, LANES - 1, 1) for b in blocks]
        back = [pltpu.roll(b, 1, 1) for b in blocks]
        easts = [jnp.where(tail, fore[(t + 1) % 3], fore[t]) for t in range(3)]
        wests = [jnp.where(head, back[(t + 2) % 3], back[t]) for t in range(3)]
        easts[1] = jnp.where(tail & last_x, sign * blocks[1], easts[1])
        wests[0] = jnp.where(head & first_x, sign * blocks[0], wests[0])
        return easts, wests

    def borders(ref, sign):
        for flag, out_row, row in ((first_y, top - 1, top), (last_y, bottom, bottom - 1)):
            for t in range(3):
                at = pl.ds(out_row, 1)
                ref[t, at, :] = jnp.where(flag, sign * ref[t, pl.ds(row, 1), :], ref[t, at, :])

    def slopes(row, size, last):
        at = pl.ds(row, size)
        easts, wests = beside([hs[t, at, :] for t in range(3)], 1.0)
        for t in range(3):
            p = easts[t] - wests[t]
            q = hs[t, pl.ds(row + 1, size), :] - hs[t, pl.ds(row - 1, size), :]
            scale = lax.rsqrt(1.0 + p * p + q * q)
            xx, xy, xz, yy, yz, zz, vx, vy, vz = [(mo if t < 2 else mo_in)[m, t, at, :] for m in range(MOMENTS)]
            alb = al[t, at, :]
            lit = alb * scale
            gx = lit * (xz - p * xx - q * xy) - vx
            gy = lit * (yz - p * xy - q * yy) - vy
            gz = lit * (zz - p * xz - q * yz) - vz
            grad_a = scale * (gz - p * gx - q * gy)
            turn = scale * grad_a
            bend = 0.3 - lit * turn
            gps[t, at, :] = p * bend - lit * gx
            if not (last and t == 2):
                gqs[t, at, :] = q * bend - lit * gy
                al[t, at, :] = alb - rate_a * grad_a

    def descend(row, size, last):
        at = pl.ds(row, size)
        easts, wests = beside([gps[t, at, :] for t in range(3)], -1.0)
        for t in range(2 if last else 3):
            fall = (wests[t] - easts[t]) + (gqs[t, pl.ds(row - 1, size), :] - gqs[t, pl.ds(row + 1, size), :])
            now = hs[t, at, :] - (0.25 * rate_h) * fall
            if last:
                lanes = slice(t * LANES, (t + 1) * LANES)
                out[0, row - top : row - top + size, lanes] = 2.0 * now
                out[1, row - top : row - top + size, lanes] = al[t, at, :]
            else:
                hs[t, at, :] = now

    borders(hs, 1.0)
    for n in range(ITERS):
        last = n == ITERS - 1
        for row in range(ROW, bottom + ROW, 16):
            slopes(row, 16, last)
        borders(gqs, -1.0)
        if last:
            for row in range(top, bottom, 16):
                descend(row, 16, True)
        else:
            for row in range(ROW, bottom + ROW, 16):
                descend(row, 16, False)
            borders(hs, 1.0)


def pair_groups(sizes):
    ny, nx = sizes

    def flat(y, x, core):
        return (y * nx + x) * 2 + core

    groups = [[flat(y, x, 1), flat(y, x + 1, 0)] for y in range(ny) for x in range(nx - 1)]
    for y in range(0, ny, 2):
        groups += [[flat(y, x, core), flat(y + 1, x, core)] for x, core in ((0, 0), (nx - 1, 1))]
    return groups


def from_next(x, core):
    groups = pair_groups((lax.axis_size("gy"), lax.axis_size("gx")))
    both = lax.all_gather(x, AXES, axis_index_groups=groups)
    return lax.dynamic_index_in_dim(both, core, 0, keepdims=False)


def neighbours(sizes):
    ny, nx = sizes

    def flat(y, x, core):
        return (y * nx + x) * 2 + core

    pairs = [(flat(y, x, 1), flat(y + 1, x, 0)) for y in range(ny - 1) for x in range(nx)]
    return pairs + [(b, a) for a, b in pairs]


VMEM = pl.BlockSpec(memory_space=pltpu.VMEM)
HBM = pl.BlockSpec(memory_space=pltpu.HBM)


def in_vmem(*args):
    return tuple(pltpu.with_memory_space_constraint(x, pltpu.VMEM) for x in args)


def cost(mib):
    return pl.CostEstimate(flops=1 << 20, bytes_accessed=mib << 20, transcendentals=0)


def params(mib):
    return pltpu.CompilerParams(vmem_limit_bytes=mib << 20)


def run_edges(sun_index, expo_index, azimuth, elevation, exposure, heights, albedo, images, weights):
    rows, cols = heights.shape
    half = rows // 2
    tiles = [x.reshape(*x.shape[:-2], 2, half, cols) for x in (heights, albedo, images, weights)]
    args = [
        pltpu.with_memory_space_constraint(x, pltpu.HBM)
        for x in (sun_index, expo_index, azimuth, elevation, exposure, *tiles)
    ]
    out = pl.pallas_call(
        edges_kernel,
        out_shape=tuple(pltpu.VMEM(x.shape, x.dtype) for x in tiles)
        + (
            pltpu.VMEM((MOMENTS, ROW, LANES), F32),
            pltpu.VMEM((half, LANES), F32),
            pltpu.VMEM((MOMENTS * ROW, cols), F32),
            pltpu.VMEM((half + 2 * MOMENTS * ROW + ROW, LANES), F32),
        ),
        in_specs=[HBM] * len(args),
        out_specs=(VMEM,) * 8,
        scratch_shapes=[pltpu.SMEM(x.shape, x.dtype) for x in args[:5]]
        + [pltpu.VMEM((2, half, LANES), F32), pltpu.VMEM((2, MOMENTS, ROW, cols), F32)]
        + [pltpu.SemaphoreType.DMA((5,)), pltpu.SemaphoreType.DMA((CHUNKS + 1, 2))],
        compiler_params=params(8),
        name="edges",
    )(*args)
    return tuple(x.reshape(rows, cols) for x in out[:2]) + out[2:]


def run_moments(kernel, planes, images, weights, tables):
    _, _, half, cols = images.shape
    return pl.pallas_call(
        kernel,
        out_shape=pltpu.VMEM((planes, half + ROW, cols), F32),
        in_specs=[VMEM] * 3,
        out_specs=VMEM,
        compiler_params=params(8),
        cost_estimate=cost(4),
        name=kernel.__name__,
    )(*in_vmem(images, weights, tables))


def run_rows(heights, albedo, own_rows, packs, sides):
    rows, cols = heights.shape
    return pl.pallas_call(
        rows_kernel,
        out_shape=(pltpu.VMEM((rows, LANES), F32), pltpu.VMEM((ROW_STARTS[PLANES] + ROW, cols), F32)),
        in_specs=[VMEM] * 5,
        out_specs=(VMEM,) * 2,
        compiler_params=params(8),
        name="edge_rows",
    )(*in_vmem(heights, albedo, own_rows, packs, sides))


def frame(rows):
    return (3, rows // 2 + 4 * ROW, LANES)


def run_fill(heights, albedo, keep, both, ends):
    block = pltpu.VMEM(frame(heights.shape[0]), F32)
    return pl.pallas_call(
        fill_kernel,
        out_shape=(block, block, pltpu.VMEM((MOMENTS, *block.shape), F32)),
        in_specs=[VMEM] * 5,
        out_specs=(VMEM,) * 3,
        compiler_params=params(8),
        cost_estimate=pl.CostEstimate(flops=1 << 34, bytes_accessed=1 << 20, transcendentals=0),
        name="fill",
    )(*in_vmem(heights, albedo, keep, both, ends))


def run_steps(total, hs, al, mo, theirs, packs):
    _, tall, _ = hs.shape
    half = tall - 4 * ROW
    block = pltpu.VMEM(hs.shape, F32)
    return pl.pallas_call(
        functools.partial(steps_kernel, (0.2 / total, 0.5 / total)),
        out_shape=pltpu.VMEM((2, half, 2 * LANES), F32),
        in_specs=[VMEM] * 5,
        out_specs=VMEM,
        scratch_shapes=[block, block, pltpu.VMEM((MOMENTS, 2, tall, LANES), F32), block, block],
        compiler_params=params(8),
        name="gradient_steps",
    )(*in_vmem(hs, al, mo, theirs, packs))


def run_place(halves):
    _, _, half, cols = halves.shape
    out = jax.ShapeDtypeStruct((2 * half, cols), F32)
    return pl.pallas_call(
        place_kernel,
        out_shape=(out, out),
        in_specs=[VMEM],
        out_specs=(HBM, HBM),
        scratch_shapes=[pltpu.SemaphoreType.DMA((2, 2))],
        compiler_params=params(8),
        name="place",
    )(*in_vmem(halves))


def shards(
    heights, albedo, images, weights, sun_index, expo_index, sun_azimuth, sun_elevation, exposure
):
    total = images.shape[0] * lax.axis_size("img")
    core = lax.axis_index("img")
    heights, albedo, images, weights, tables, own_fold, own_rows, pack = run_edges(
        sun_index, expo_index, sun_azimuth, sun_elevation, exposure, heights, albedo, images, weights
    )
    packs = lax.all_gather(pack, "img")
    fold = own_fold + lax.dynamic_index_in_dim(packs, 1 - core, 0, keepdims=False)[: own_fold.shape[0]]
    sides = lax.all_gather(from_next(fold, core), "img")
    both, ends = run_rows(heights, albedo, own_rows, packs, sides)
    ends, images = lax.optimization_barrier((ends, images))
    ends = lax.ppermute(ends, AXES, neighbours((lax.axis_size("gy"), lax.axis_size("gx"))))
    send = run_moments(sent_kernel, images.shape[0] + 3, images, weights, tables)
    theirs = lax.ppermute(send, "img", [(0, 1), (1, 0)])
    keep = run_moments(own_kernel, MOMENTS, images, weights, tables)
    halves = run_steps(total, *run_fill(heights, albedo, keep, both, ends), theirs, packs)
    return run_place(lax.all_gather(halves, "img"))


def solution(mesh):
    return jax.shard_map(
        shards,
        mesh=mesh,
        in_specs=(
            P("gy", "gx"),
            P("gy", "gx"),
            P("img", "gy", "gx"),
            P("img", "gy", "gx"),
            P("img"),
            P("img"),
            P(),
            P(),
            P(),
        ),
        out_specs=(P("gy", "gx"), P("gy", "gx")),
        check_vma=False,
    )
```

```python
import functools

import jax
import jax.numpy as jnp
from jax import lax
from jax.experimental import pallas as pl
from jax.experimental.pallas import tpu as pltpu
from jax.sharding import PartitionSpec as P

ITERS = 3
AXES = ("gy", "gx", "img")
LANES = 128
ROW = 8
CHUNKS = 2
MOMENTS = 9
PLANES = 2 + MOMENTS
WIDTHS = (6,) + (5,) * (PLANES - 1)
STARTS = tuple(6 if k == 0 else 17 + 10 * (k - 1) for k in range(PLANES))
ROW_STARTS = tuple(sum(WIDTHS[:k]) for k in range(PLANES + 1))
F32 = jnp.float32


def lane_ids(rows):
    return lax.broadcasted_iota(jnp.int32, (rows, LANES), 1)


def east_lanes(lane):
    hit = lane < 0
    for start, width in zip(STARTS, WIDTHS):
        hit = hit | ((lane >= start) & (lane < start + width))
    return hit


def edges_kernel(
    sun_index_hbm, expo_index_hbm, azimuth_hbm, elevation_hbm, exposure_hbm, height_hbm, albedo_hbm, images_hbm,
    weights_hbm, height, albedo, images, weights, tables, own_fold, own_rows, pack, sun_index, expo_index, azimuth,
    elevation, exposure, spreads, ends_of_rows, small_sems, large_sems
):
    count, _, half, _ = images.shape
    small = [
        pltpu.make_async_copy(src, dst, small_sems.at[n])
        for n, (src, dst) in enumerate((
            (sun_index_hbm, sun_index), (expo_index_hbm, expo_index), (azimuth_hbm, azimuth),
            (elevation_hbm, elevation), (exposure_hbm, exposure),
        ))
    ]
    part = half // CHUNKS
    large = []
    for c in range(CHUNKS):
        at = pl.ds(c * part, part)
        large.append([
            pltpu.make_async_copy(weights_hbm.at[:, :, at, :], weights.at[:, :, at, :], large_sems.at[c, 0]),
            pltpu.make_async_copy(images_hbm.at[:, :, at, :], images.at[:, :, at, :], large_sems.at[c, 1]),
        ])
    large.append([
        pltpu.make_async_copy(height_hbm, height, large_sems.at[CHUNKS, 0]),
        pltpu.make_async_copy(albedo_hbm, albedo, large_sems.at[CHUNKS, 1]),
    ])
    for copies in large:
        for copy in copies:
            copy.start()
    for copy in small:
        copy.start()
    for copy in small:
        copy.wait()
    line = lax.broadcasted_iota(jnp.int32, (ROW, LANES), 0)
    azim = jnp.zeros((ROW, LANES), F32)
    elev = jnp.zeros((ROW, LANES), F32)
    gain = jnp.zeros((ROW, LANES), F32)
    for k in range(count):
        azim = jnp.where(line == k, azimuth[sun_index[k]], azim)
        elev = jnp.where(line == k, elevation[sun_index[k]], elev)
        gain = jnp.where(line == k, exposure[expo_index[k]], gain)
    flat = jnp.cos(elev)
    sx = gain * flat * jnp.cos(azim)
    sy = gain * flat * jnp.sin(azim)
    sz = gain * jnp.sin(elev)
    factors = (sx * sx, sx * sy, sx * sz, sy * sy, sy * sz, sz * sz, sx, sy, sz)
    for m, factor in enumerate(factors):
        tables[m] = factor
    lane = lane_ids(ROW)
    block = jnp.zeros((ROW, LANES), F32)
    for m, factor in enumerate(factors):
        block = jnp.where(lane == m, factor, block)
    pack[pl.ds(half + 2 * MOMENTS * ROW, ROW), :] = block
    step = 16
    lane = lane_ids(step)

    def sums(view):
        return add_moments(lambda k: view(weights, k), lambda k: view(images, k), count, lambda m, k: factors[m][k : k + 1, :1])

    def ends(x):
        return jnp.where(lane < LANES // 2, x[:, :LANES], x[:, -LANES:])

    middle = (lane >= LANES // 4) & (lane < 3 * LANES // 4)

    def all_ends(upper, lower):
        return jnp.where(middle, pltpu.roll(ends(lower), LANES // 2, 1), ends(upper)).astype(F32)

    def spread(planes, first, upper, lower):
        for plane, start, width in zip(planes, STARTS[first:], WIDTHS[first:]):
            plane = pltpu.roll(plane, start, 1)
            upper = jnp.where((lane >= start - width) & (lane < start + width), plane, upper)
            away = (lane - start - LANES // 2 + width) & (LANES - 1)
            lower = jnp.where(away < 2 * width, plane, lower)
        return upper, lower

    def edge_rows(side):
        at = pl.ds(side * (half - step), step)
        ends_of_rows[side] = jnp.stack(sums(lambda ref, k: ref[k, side, at, :].astype(F32)[side * ROW : (side + 1) * ROW]))

    zero = jnp.zeros((step, LANES), F32)
    for c in range(CHUNKS):
        for copy in large[c]:
            copy.wait()
        for i in range(c * part, (c + 1) * part, step):
            at = pl.ds(i, step)
            planes = sums(lambda ref, k: all_ends(ref[k, 0, at, :], ref[k, 1, at, :]))
            spreads[0, at, :], spreads[1, at, :] = spread(planes, 2, zero, zero)
        if c == 0:
            edge_rows(0)
        if c == CHUNKS - 1:
            edge_rows(1)
    core = lax.axis_index("img")
    for m in range(MOMENTS):
        own_rows[pl.ds(m * ROW, ROW), :] = ends_of_rows[core, m]
        for t in range(2):
            pack[pl.ds(half + (2 * m + t) * ROW, ROW), :] = ends_of_rows[1 - core, m, :, t * LANES : (t + 1) * LANES]
    for copy in large[CHUNKS]:
        copy.wait()
    high = east_lanes(lane)
    wide = lane < STARTS[0] + WIDTHS[0]
    for i in range(0, half, step):
        at = pl.ds(i, step)
        planes = [0.5 * all_ends(x[0, at, :], x[1, at, :]) for x in (height, albedo)]
        upper, lower = spread(planes, 0, spreads[0, at, :], spreads[1, at, :])
        to_west, to_east = (
            jnp.where(wide, pltpu.roll(lower, (64 + 6 * d) % LANES, 1), pltpu.roll(lower, (64 + 5 * d) % LANES, 1))
            for d in (-1, 1)
        )
        west = jnp.where(high, upper, to_west)
        east = jnp.where(high, to_east, upper)
        own_fold[at, :] = jnp.where(core == 0, west, east)
        pack[at, :] = jnp.where(core == 0, east, west)


def add_moments(weight, image, count, factor):
    acc = [None] * MOMENTS
    for k in range(count):
        w = weight(k)
        u = w * image(k)
        for m in range(MOMENTS):
            term = (w if m < 6 else u) * factor(m, k)
            acc[m] = term if k == 0 else acc[m] + term
    return acc


def part_rows(core, half):
    step = 16
    near = pl.multiple_of(core * (half - step), step)
    yield 1 - core, pl.ds(near, step), None
    for i in range(0, half, step):
        yield core, pl.ds(i, step), pl.ds(ROW + i, step)


def put(out, plane, dst, value, core):
    if dst is None:
        out[plane, pl.ds(0, ROW), :] = jnp.where(core == 0, value[:ROW], value[-ROW:])
    else:
        out[plane, dst, :] = value


def sent_kernel(images, weights, tables, out):
    count, _, half, _ = images.shape
    core = 1 - lax.axis_index("img")
    for s, at, dst in part_rows(core, half):
        acc = [None] * 3
        for k in range(count):
            w = weights[k, s, at, :].astype(F32)
            put(out, k, dst, w, core)
            u = w * images[k, s, at, :].astype(F32)
            for m in range(3):
                term = u * tables[6 + m, k : k + 1, :1]
                acc[m] = term if k == 0 else acc[m] + term
        for m in range(3):
            put(out, count + m, dst, acc[m], core)


def own_kernel(images, weights, tables, out):
    count, _, half, _ = images.shape
    core = lax.axis_index("img")
    for s, at, dst in part_rows(core, half):
        acc = add_moments(
            lambda k: weights[k, s, at, :].astype(F32), lambda k: images[k, s, at, :].astype(F32), count,
            lambda m, k: tables[m, k : k + 1, :1]
        )
        for m in range(MOMENTS):
            put(out, m, dst, acc[m], core)


def place_kernel(halves, height, albedo, sems):
    copies = [pltpu.make_async_copy(halves.at[:, n], out, sems.at[n]) for n, out in enumerate((height, albedo))]
    for copy in copies:
        copy.start()
    for copy in copies:
        copy.wait()


def rows_kernel(height, albedo, own_rows, packs, sides, both, out):
    rows = height.shape[0]
    half = rows // 2
    core = lax.axis_index("img")
    lane = lane_ids(ROW)
    east = east_lanes(lane)
    wide = lane < STARTS[0] + WIDTHS[0]
    for i in range(0, half, ROW):
        at = pl.ds(i, ROW)
        west_side, east_side = sides[0, at, :], sides[1, at, :]
        both[at, :] = jnp.where(east, east_side, west_side)
        moved_e, moved_w = (
            jnp.where(wide, pltpu.roll(x, 6 * d % LANES, 1), pltpu.roll(x, 5 * d % LANES, 1))
            for x, d in ((east_side, 1), (west_side, -1))
        )
        both[pl.ds(half + i, ROW), :] = jnp.where(east, moved_e, moved_w)
    at = pl.ds(pl.multiple_of(core * (rows - ROW), ROW), ROW)
    upper = core == 0

    def edge(x, n):
        return jnp.where(upper, x[:n], x[ROW - n :])

    out[pl.ds(0, WIDTHS[0]), :] = edge(height[at, :], WIDTHS[0])
    for k in range(1, PLANES):
        if k == 1:
            plane = albedo[at, :]
        else:
            m = k - 2
            theirs = [packs[1 - core, pl.ds(half + (2 * m + t) * ROW, ROW), :] for t in range(2)]
            plane = own_rows[pl.ds(m * ROW, ROW), :] + jnp.concatenate(theirs, axis=1)
        out[pl.ds(ROW_STARTS[k], WIDTHS[k]), :] = edge(plane, WIDTHS[k])
    corner = both[at, :]
    out[pl.ds(ROW_STARTS[PLANES], ROW), :] = jnp.concatenate([corner, corner], axis=1)


def neighbours_in_ring(blocks, sign, first_x, last_x):
    lane = lane_ids(blocks[0].shape[0])
    head = lane == 0
    tail = lane == LANES - 1
    fore = [pltpu.roll(b, LANES - 1, 1) for b in blocks]
    back = [pltpu.roll(b, 1, 1) for b in blocks]
    easts = [jnp.where(tail, fore[(t + 1) % 3], fore[t]) for t in range(3)]
    wests = [jnp.where(head, back[(t + 2) % 3], back[t]) for t in range(3)]
    easts[1] = jnp.where(tail & last_x, sign * blocks[1], easts[1])
    wests[0] = jnp.where(head & first_x, sign * blocks[0], wests[0])
    return easts, wests


def mirror(ref, sign, top, bottom):
    core = lax.axis_index("img")
    first_y = (lax.axis_index("gy") == 0) & (core == 0)
    last_y = (lax.axis_index("gy") == lax.axis_size("gy") - 1) & (core == 1)
    for flag, out_row, row in ((first_y, top - 1, top), (last_y, bottom, bottom - 1)):
        for t in range(3):
            at = pl.ds(out_row, 1)
            ref[t, at, :] = jnp.where(flag, sign * ref[t, pl.ds(row, 1), :], ref[t, at, :])


def slopes_at(hs, row, size, first_x, last_x):
    at = pl.ds(row, size)
    easts, wests = neighbours_in_ring([hs[t, at, :] for t in range(3)], 1.0, first_x, last_x)
    for t in range(3):
        p = easts[t] - wests[t]
        q = hs[t, pl.ds(row + 1, size), :] - hs[t, pl.ds(row - 1, size), :]
        yield p, q, lax.rsqrt(1.0 + p * p + q * q)


def inner_row(core, half):
    return ROW + (1 - core) * (half + ROW)


def fill_kernel(height, albedo, keep, both, ends, hs, al, mo, ps, qs, cs):
    rows = height.shape[0]
    core = lax.axis_index("img")

    def plane(k):
        return hs if k == 0 else al if k == 1 else mo.at[k - 2]

    half = rows // 2
    inner = core * (half - ROW) + (1 - core) * half
    for i in range(-ROW, half, ROW):
        if i < 0:
            src, dst = pl.ds(pl.multiple_of(inner, ROW), ROW), pl.ds(pl.multiple_of(inner_row(core, half), ROW), ROW)
        else:
            src, dst = pl.ds(pl.multiple_of(core * half + i, ROW), ROW), pl.ds(2 * ROW + i, ROW)
        sides = both[src, :]
        for k in range(PLANES):
            body = 0.5 * height[src, :] if k == 0 else albedo[src, :] if k == 1 else keep[k - 2, pl.ds(ROW + i, ROW), :]
            ref = plane(k)
            ref[0, dst, :] = body[:, :LANES]
            ref[1, dst, :] = body[:, LANES:]
            side = pltpu.roll(sides, LANES - STARTS[k], 1)
            ref[2, dst, :] = 0.5 * side if k == 0 else side
    dst = pl.ds(pl.multiple_of(inner_row(1 - core, half), ROW), ROW)
    sides = ends[pl.ds(ROW_STARTS[PLANES], ROW), :LANES]
    for k in range(PLANES):
        ref = plane(k)
        begin, spare = ROW_STARTS[k], ROW - WIDTHS[k]
        after = ends[pl.ds(begin, ROW), :]
        before = pltpu.roll(after, spare, 0) if k == 0 else ends[pl.ds(begin - spare, ROW), :]
        body = jnp.where(core == 0, before, after) * (0.5 if k == 0 else 1.0)
        ref[0, dst, :] = body[:, :LANES]
        ref[1, dst, :] = body[:, LANES:]
        side = pltpu.roll(sides, LANES - STARTS[k], 1)
        ref[2, dst, :] = 0.5 * side if k == 0 else side
    first_x = lax.axis_index("gx") == 0
    last_x = lax.axis_index("gx") == lax.axis_size("gx") - 1
    mirror(hs, 1.0, 2 * ROW, 2 * ROW + half)
    for row in range(ROW, half + 3 * ROW, 16):
        for t, (p, q, scale) in enumerate(slopes_at(hs, row, 16, first_x, last_x)):
            ps[t, pl.ds(row, 16), :], qs[t, pl.ds(row, 16), :], cs[t, pl.ds(row, 16), :] = p, q, scale


def steps_kernel(rates, hs_in, al_in, mo_in, ps, qs, cs, theirs, packs, out, hs, al, mo, gps, gqs):
    half = out.shape[1]
    core = lax.axis_index("img")
    first_x = lax.axis_index("gx") == 0
    last_x = lax.axis_index("gx") == lax.axis_size("gx") - 1
    rate_h, rate_a = rates
    top = 2 * ROW
    bottom = top + half
    count = theirs.shape[0] - 3
    table = packs[1 - core, packs.shape[1] - ROW :, :]
    factors = [[jnp.broadcast_to(table[k : k + 1, m : m + 1], (ROW, LANES)) for k in range(count)] for m in range(6)]
    for t in range(2):
        lanes = slice(t * LANES, (t + 1) * LANES)
        for i in range(-ROW, half, ROW):
            src = pl.ds(ROW + i, ROW)
            w = [theirs[k, src, lanes] for k in range(count)]
            for m in range(MOMENTS):
                if m < 6:
                    extra = sum((w[k] * factors[m][k] for k in range(1, count)), w[0] * factors[m][0])
                else:
                    extra = theirs[count + m - 6, src, lanes]
                if i >= 0:
                    at = pl.ds(top + i, ROW)
                    mo[m, t, at, :] = mo_in[m, t, at, :] + extra
                else:
                    for at, owner in ((pl.ds(ROW, ROW), 1), (pl.ds(bottom, ROW), 0)):
                        halo = mo_in[m, t, at, :]
                        mo[m, t, at, :] = jnp.where(core == owner, halo + extra, halo)

    def beside(blocks, sign):
        return neighbours_in_ring(blocks, sign, first_x, last_x)

    def borders(ref, sign):
        mirror(ref, sign, top, bottom)

    def slopes(row, size, first, last):
        at = pl.ds(row, size)
        if first:
            parts = [(ps[t, at, :], qs[t, at, :], cs[t, at, :]) for t in range(3)]
        else:
            parts = slopes_at(hs, row, size, first_x, last_x)
        for t, (p, q, scale) in enumerate(parts):
            xx, xy, xz, yy, yz, zz, vx, vy, vz = [(mo if t < 2 else mo_in)[m, t, at, :] for m in range(MOMENTS)]
            alb = (al_in if first else al)[t, at, :]
            lit = alb * scale
            gx = lit * (xz - p * xx - q * xy) - vx
            gy = lit * (yz - p * xy - q * yy) - vy
            gz = lit * (zz - p * xz - q * yz) - vz
            grad_a = scale * (gz - p * gx - q * gy)
            turn = scale * grad_a
            bend = 0.3 - lit * turn
            gps[t, at, :] = p * bend - lit * gx
            if not (last and t == 2):
                gqs[t, at, :] = q * bend - lit * gy
                al[t, at, :] = alb - rate_a * grad_a

    def descend(row, size, first, last):
        at = pl.ds(row, size)
        easts, wests = beside([gps[t, at, :] for t in range(3)], -1.0)
        for t in range(2 if last else 3):
            fall = (wests[t] - easts[t]) + (gqs[t, pl.ds(row - 1, size), :] - gqs[t, pl.ds(row + 1, size), :])
            now = (hs_in if first else hs)[t, at, :] - (0.25 * rate_h) * fall
            if last:
                lanes = slice(t * LANES, (t + 1) * LANES)
                out[0, row - top : row - top + size, lanes] = 2.0 * now
                out[1, row - top : row - top + size, lanes] = al[t, at, :]
            else:
                hs[t, at, :] = now

    for n in range(ITERS):
        first, last = n == 0, n == ITERS - 1
        for row in range(ROW, bottom + ROW, 16):
            slopes(row, 16, first, last)
        borders(gqs, -1.0)
        for row in range(top, bottom, 16) if last else range(ROW, bottom + ROW, 16):
            descend(row, 16, first, last)
        if not last:
            borders(hs, 1.0)


def pair_groups(sizes):
    ny, nx = sizes

    def flat(y, x, core):
        return (y * nx + x) * 2 + core

    groups = [[flat(y, x, 1), flat(y, x + 1, 0)] for y in range(ny) for x in range(nx - 1)]
    for y in range(0, ny, 2):
        groups += [[flat(y, x, core), flat(y + 1, x, core)] for x, core in ((0, 0), (nx - 1, 1))]
    return groups


def from_next(x, core):
    groups = pair_groups((lax.axis_size("gy"), lax.axis_size("gx")))
    both = lax.all_gather(x, AXES, axis_index_groups=groups)
    return lax.dynamic_index_in_dim(both, core, 0, keepdims=False)


def neighbours(sizes):
    ny, nx = sizes

    def flat(y, x, core):
        return (y * nx + x) * 2 + core

    pairs = [(flat(y, x, 1), flat(y + 1, x, 0)) for y in range(ny - 1) for x in range(nx)]
    return pairs + [(b, a) for a, b in pairs]


VMEM = pl.BlockSpec(memory_space=pltpu.VMEM)
HBM = pl.BlockSpec(memory_space=pltpu.HBM)


def in_vmem(*args):
    return tuple(pltpu.with_memory_space_constraint(x, pltpu.VMEM) for x in args)


def cost(mib):
    return pl.CostEstimate(flops=1 << 20, bytes_accessed=mib << 20, transcendentals=0)


def params(mib):
    return pltpu.CompilerParams(vmem_limit_bytes=mib << 20)


def run_edges(sun_index, expo_index, azimuth, elevation, exposure, heights, albedo, images, weights):
    rows, cols = heights.shape
    half = rows // 2
    tiles = [x.reshape(*x.shape[:-2], 2, half, cols) for x in (heights, albedo, images, weights)]
    args = [
        pltpu.with_memory_space_constraint(x, pltpu.HBM)
        for x in (sun_index, expo_index, azimuth, elevation, exposure, *tiles)
    ]
    out = pl.pallas_call(
        edges_kernel,
        out_shape=tuple(pltpu.VMEM(x.shape, x.dtype) for x in tiles)
        + (
            pltpu.VMEM((MOMENTS, ROW, LANES), F32),
            pltpu.VMEM((half, LANES), F32),
            pltpu.VMEM((MOMENTS * ROW, cols), F32),
            pltpu.VMEM((half + 2 * MOMENTS * ROW + ROW, LANES), F32),
        ),
        in_specs=[HBM] * len(args),
        out_specs=(VMEM,) * 8,
        scratch_shapes=[pltpu.SMEM(x.shape, x.dtype) for x in args[:5]]
        + [pltpu.VMEM((2, half, LANES), F32), pltpu.VMEM((2, MOMENTS, ROW, cols), F32)]
        + [pltpu.SemaphoreType.DMA((5,)), pltpu.SemaphoreType.DMA((CHUNKS + 1, 2))],
        compiler_params=params(8),
        name="edges",
    )(*args)
    return tuple(x.reshape(rows, cols) for x in out[:2]) + out[2:]


def run_moments(kernel, planes, images, weights, tables):
    _, _, half, cols = images.shape
    return pl.pallas_call(
        kernel,
        out_shape=pltpu.VMEM((planes, half + ROW, cols), F32),
        in_specs=[VMEM] * 3,
        out_specs=VMEM,
        compiler_params=params(8),
        cost_estimate=cost(4),
        name=kernel.__name__,
    )(*in_vmem(images, weights, tables))


def run_rows(heights, albedo, own_rows, packs, sides):
    rows, cols = heights.shape
    return pl.pallas_call(
        rows_kernel,
        out_shape=(pltpu.VMEM((rows, LANES), F32), pltpu.VMEM((ROW_STARTS[PLANES] + ROW, cols), F32)),
        in_specs=[VMEM] * 5,
        out_specs=(VMEM,) * 2,
        compiler_params=params(8),
        name="edge_rows",
    )(*in_vmem(heights, albedo, own_rows, packs, sides))


def frame(rows):
    return (3, rows // 2 + 4 * ROW, LANES)


def run_fill(heights, albedo, keep, both, ends):
    block = pltpu.VMEM(frame(heights.shape[0]), F32)
    return pl.pallas_call(
        fill_kernel,
        out_shape=(block, block, pltpu.VMEM((MOMENTS, *block.shape), F32), block, block, block),
        in_specs=[VMEM] * 5,
        out_specs=(VMEM,) * 6,
        compiler_params=params(8),
        cost_estimate=pl.CostEstimate(flops=1 << 34, bytes_accessed=1 << 20, transcendentals=0),
        name="fill",
    )(*in_vmem(heights, albedo, keep, both, ends))


def run_steps(total, *args):
    _, tall, _ = args[0].shape
    half = tall - 4 * ROW
    block = pltpu.VMEM(args[0].shape, F32)
    return pl.pallas_call(
        functools.partial(steps_kernel, (0.2 / total, 0.5 / total)),
        out_shape=pltpu.VMEM((2, half, 2 * LANES), F32),
        in_specs=[VMEM] * len(args),
        out_specs=VMEM,
        scratch_shapes=[block, block, pltpu.VMEM((MOMENTS, 2, tall, LANES), F32), block, block],
        compiler_params=params(8),
        name="gradient_steps",
    )(*in_vmem(*args))


def run_place(halves):
    _, _, half, cols = halves.shape
    out = jax.ShapeDtypeStruct((2, half, cols), F32)
    placed = pl.pallas_call(
        place_kernel,
        out_shape=(out, out),
        in_specs=[VMEM],
        out_specs=(HBM, HBM),
        scratch_shapes=[pltpu.SemaphoreType.DMA((2,))],
        compiler_params=params(8),
        name="place",
    )(*in_vmem(halves))
    return tuple(x.reshape(2 * half, cols) for x in placed)


def shards(
    heights, albedo, images, weights, sun_index, expo_index, sun_azimuth, sun_elevation, exposure
):
    total = images.shape[0] * lax.axis_size("img")
    core = lax.axis_index("img")
    heights, albedo, images, weights, tables, own_fold, own_rows, pack = run_edges(
        sun_index, expo_index, sun_azimuth, sun_elevation, exposure, heights, albedo, images, weights
    )
    packs = lax.all_gather(pack, "img")
    fold = own_fold + lax.dynamic_index_in_dim(packs, 1 - core, 0, keepdims=False)[: own_fold.shape[0]]
    sides = lax.all_gather(from_next(fold, core), "img")
    both, ends = run_rows(heights, albedo, own_rows, packs, sides)
    ends, images = lax.optimization_barrier((ends, images))
    ends = lax.ppermute(ends, AXES, neighbours((lax.axis_size("gy"), lax.axis_size("gx"))))
    send = run_moments(sent_kernel, images.shape[0] + 3, images, weights, tables)
    theirs = lax.ppermute(send, "img", [(0, 1), (1, 0)])
    keep = run_moments(own_kernel, MOMENTS, images, weights, tables)
    halves = run_steps(total, *run_fill(heights, albedo, keep, both, ends), theirs, packs)
    return run_place(lax.all_gather(halves, "img"))


def solution(mesh):
    return jax.shard_map(
        shards,
        mesh=mesh,
        in_specs=(
            P("gy", "gx"),
            P("gy", "gx"),
            P("img", "gy", "gx"),
            P("img", "gy", "gx"),
            P("img"),
            P("img"),
            P(),
            P(),
            P(),
        ),
        out_specs=(P("gy", "gx"), P("gy", "gx")),
        check_vma=False,
    )
```

```python
import functools

import jax
import jax.numpy as jnp
from jax import lax
from jax.experimental import pallas as pl
from jax.experimental.pallas import tpu as pltpu
from jax.sharding import PartitionSpec as P

ITERS = 3
AXES = ("gy", "gx", "img")
LANES = 128
ROW = 8
CHUNKS = 2
MOMENTS = 9
PLANES = 2 + MOMENTS
WIDTHS = (6,) + (5,) * (PLANES - 1)
STARTS = tuple(6 if k == 0 else 17 + 10 * (k - 1) for k in range(PLANES))
ROW_STARTS = tuple(sum(WIDTHS[:k]) for k in range(PLANES + 1))
F32 = jnp.float32


def part_of(core):
    return (core + 1 + lax.axis_index("gy")) % 2


def side_of(core):
    return (core + 1 + lax.axis_index("gx")) % 2


def lane_ids(rows):
    return lax.broadcasted_iota(jnp.int32, (rows, LANES), 1)


def east_lanes(lane):
    hit = lane < 0
    for start, width in zip(STARTS, WIDTHS):
        hit = hit | ((lane >= start) & (lane < start + width))
    return hit


def edges_kernel(
    sun_index_hbm, expo_index_hbm, azimuth_hbm, elevation_hbm, exposure_hbm, height_hbm, albedo_hbm, images_hbm,
    weights_hbm, height, albedo, images, weights, tables, own_fold, own_rows, pack, sun_index, expo_index, azimuth,
    elevation, exposure, spreads, ends_of_rows, small_sems, large_sems
):
    count, _, half, _ = images.shape
    small = [
        pltpu.make_async_copy(src, dst, small_sems.at[n])
        for n, (src, dst) in enumerate((
            (sun_index_hbm, sun_index), (expo_index_hbm, expo_index), (azimuth_hbm, azimuth),
            (elevation_hbm, elevation), (exposure_hbm, exposure),
        ))
    ]
    part = half // CHUNKS
    large = []
    for c in range(CHUNKS):
        at = pl.ds(c * part, part)
        large.append([
            pltpu.make_async_copy(weights_hbm.at[:, :, at, :], weights.at[:, :, at, :], large_sems.at[c, 0]),
            pltpu.make_async_copy(images_hbm.at[:, :, at, :], images.at[:, :, at, :], large_sems.at[c, 1]),
        ])
    large.append([
        pltpu.make_async_copy(height_hbm, height, large_sems.at[CHUNKS, 0]),
        pltpu.make_async_copy(albedo_hbm, albedo, large_sems.at[CHUNKS, 1]),
    ])
    for copies in large:
        for copy in copies:
            copy.start()
    for copy in small:
        copy.start()
    for copy in small:
        copy.wait()
    line = lax.broadcasted_iota(jnp.int32, (ROW, LANES), 0)
    azim = jnp.zeros((ROW, LANES), F32)
    elev = jnp.zeros((ROW, LANES), F32)
    gain = jnp.zeros((ROW, LANES), F32)
    for k in range(count):
        azim = jnp.where(line == k, azimuth[sun_index[k]], azim)
        elev = jnp.where(line == k, elevation[sun_index[k]], elev)
        gain = jnp.where(line == k, exposure[expo_index[k]], gain)
    flat = jnp.cos(elev)
    sx = gain * flat * jnp.cos(azim)
    sy = gain * flat * jnp.sin(azim)
    sz = gain * jnp.sin(elev)
    factors = (sx * sx, sx * sy, sx * sz, sy * sy, sy * sz, sz * sz, sx, sy, sz)
    for m, factor in enumerate(factors):
        tables[m] = factor
    lane = lane_ids(ROW)
    block = jnp.zeros((ROW, LANES), F32)
    for m, factor in enumerate(factors):
        block = jnp.where(lane == m, factor, block)
    pack[pl.ds(half + 2 * MOMENTS * ROW, ROW), :] = block
    step = 16
    lane = lane_ids(step)

    def sums(view):
        return add_moments(lambda k: view(weights, k), lambda k: view(images, k), count, lambda m, k: factors[m][k : k + 1, :1])

    def ends(x):
        return jnp.where(lane < LANES // 2, x[:, :LANES], x[:, -LANES:])

    middle = (lane >= LANES // 4) & (lane < 3 * LANES // 4)

    def all_ends(upper, lower):
        return jnp.where(middle, pltpu.roll(ends(lower), LANES // 2, 1), ends(upper)).astype(F32)

    def spread(planes, first, upper, lower):
        for plane, start, width in zip(planes, STARTS[first:], WIDTHS[first:]):
            plane = pltpu.roll(plane, start, 1)
            upper = jnp.where((lane >= start - width) & (lane < start + width), plane, upper)
            away = (lane - start - LANES // 2 + width) & (LANES - 1)
            lower = jnp.where(away < 2 * width, plane, lower)
        return upper, lower

    def edge_rows(side):
        at = pl.ds(side * (half - step), step)
        ends_of_rows[side] = jnp.stack(sums(lambda ref, k: ref[k, side, at, :].astype(F32)[side * ROW : (side + 1) * ROW]))

    zero = jnp.zeros((step, LANES), F32)
    for c in range(CHUNKS):
        for copy in large[c]:
            copy.wait()
        for i in range(c * part, (c + 1) * part, step):
            at = pl.ds(i, step)
            planes = sums(lambda ref, k: all_ends(ref[k, 0, at, :], ref[k, 1, at, :]))
            spreads[0, at, :], spreads[1, at, :] = spread(planes, 2, zero, zero)
        if c == 0:
            edge_rows(0)
        if c == CHUNKS - 1:
            edge_rows(1)
    part = part_of(lax.axis_index("img"))
    side = side_of(lax.axis_index("img"))
    for m in range(MOMENTS):
        own_rows[pl.ds(m * ROW, ROW), :] = ends_of_rows[part, m]
        for t in range(2):
            pack[pl.ds(half + (2 * m + t) * ROW, ROW), :] = ends_of_rows[1 - part, m, :, t * LANES : (t + 1) * LANES]
    for copy in large[CHUNKS]:
        copy.wait()
    high = east_lanes(lane)
    wide = lane < STARTS[0] + WIDTHS[0]
    for i in range(0, half, step):
        at = pl.ds(i, step)
        planes = [0.5 * all_ends(x[0, at, :], x[1, at, :]) for x in (height, albedo)]
        upper, lower = spread(planes, 0, spreads[0, at, :], spreads[1, at, :])
        to_west, to_east = (
            jnp.where(wide, pltpu.roll(lower, (64 + 6 * d) % LANES, 1), pltpu.roll(lower, (64 + 5 * d) % LANES, 1))
            for d in (-1, 1)
        )
        west = jnp.where(high, upper, to_west)
        east = jnp.where(high, to_east, upper)
        own_fold[at, :] = jnp.where(side == 0, west, east)
        pack[at, :] = jnp.where(side == 0, east, west)


def add_moments(weight, image, count, factor):
    acc = [None] * MOMENTS
    for k in range(count):
        w = weight(k)
        u = w * image(k)
        for m in range(MOMENTS):
            term = (w if m < 6 else u) * factor(m, k)
            acc[m] = term if k == 0 else acc[m] + term
    return acc


def part_rows(core, half):
    step = 16
    near = pl.multiple_of(core * (half - step), step)
    yield 1 - core, pl.ds(near, step), None
    for i in range(0, half, step):
        yield core, pl.ds(i, step), pl.ds(ROW + i, step)


def put(out, plane, dst, value, core):
    if dst is None:
        out[plane, pl.ds(0, ROW), :] = jnp.where(core == 0, value[:ROW], value[-ROW:])
    else:
        out[plane, dst, :] = value


def sent_kernel(images, weights, tables, out):
    count, _, half, _ = images.shape
    core = 1 - part_of(lax.axis_index("img"))
    for s, at, dst in part_rows(core, half):
        acc = [None] * 3
        for k in range(count):
            w = weights[k, s, at, :].astype(F32)
            put(out, k, dst, w, core)
            u = w * images[k, s, at, :].astype(F32)
            for m in range(3):
                term = u * tables[6 + m, k : k + 1, :1]
                acc[m] = term if k == 0 else acc[m] + term
        for m in range(3):
            put(out, count + m, dst, acc[m], core)


def own_kernel(images, weights, tables, out):
    count, _, half, _ = images.shape
    core = part_of(lax.axis_index("img"))
    for s, at, dst in part_rows(core, half):
        acc = add_moments(
            lambda k: weights[k, s, at, :].astype(F32), lambda k: images[k, s, at, :].astype(F32), count,
            lambda m, k: tables[m, k : k + 1, :1]
        )
        for m in range(MOMENTS):
            put(out, m, dst, acc[m], core)


def place_kernel(halves, height, albedo, sems):
    half = halves.shape[2]
    copies = [
        pltpu.make_async_copy(halves.at[part_of(part), n], out.at[pl.ds(part * half, half), :], sems.at[part, n])
        for part in range(2)
        for n, out in enumerate((height, albedo))
    ]
    for copy in copies:
        copy.start()
    for copy in copies:
        copy.wait()


def rows_kernel(height, albedo, own_rows, packs, sides, both, out):
    rows = height.shape[0]
    half = rows // 2
    core = lax.axis_index("img")
    part = part_of(core)
    west_core = side_of(0)
    lane = lane_ids(ROW)
    east = east_lanes(lane)
    wide = lane < STARTS[0] + WIDTHS[0]
    for i in range(0, half, ROW):
        at = pl.ds(i, ROW)
        west_side, east_side = sides[west_core, at, :], sides[1 - west_core, at, :]
        both[at, :] = jnp.where(east, east_side, west_side)
        moved_e, moved_w = (
            jnp.where(wide, pltpu.roll(x, 6 * d % LANES, 1), pltpu.roll(x, 5 * d % LANES, 1))
            for x, d in ((east_side, 1), (west_side, -1))
        )
        both[pl.ds(half + i, ROW), :] = jnp.where(east, moved_e, moved_w)
    at = pl.ds(pl.multiple_of(part * (rows - ROW), ROW), ROW)
    upper = part == 0

    def edge(x, n):
        return jnp.where(upper, x[:n], x[ROW - n :])

    out[pl.ds(0, WIDTHS[0]), :] = edge(height[at, :], WIDTHS[0])
    for k in range(1, PLANES):
        if k == 1:
            plane = albedo[at, :]
        else:
            m = k - 2
            theirs = [packs[1 - core, pl.ds(half + (2 * m + t) * ROW, ROW), :] for t in range(2)]
            plane = own_rows[pl.ds(m * ROW, ROW), :] + jnp.concatenate(theirs, axis=1)
        out[pl.ds(ROW_STARTS[k], WIDTHS[k]), :] = edge(plane, WIDTHS[k])
    corner = both[at, :]
    out[pl.ds(ROW_STARTS[PLANES], ROW), :] = jnp.concatenate([corner, corner], axis=1)


def neighbours_in_ring(blocks, sign, first_x, last_x):
    lane = lane_ids(blocks[0].shape[0])
    head = lane == 0
    tail = lane == LANES - 1
    fore = [pltpu.roll(b, LANES - 1, 1) for b in blocks]
    back = [pltpu.roll(b, 1, 1) for b in blocks]
    easts = [jnp.where(tail, fore[(t + 1) % 3], fore[t]) for t in range(3)]
    wests = [jnp.where(head, back[(t + 2) % 3], back[t]) for t in range(3)]
    easts[1] = jnp.where(tail & last_x, sign * blocks[1], easts[1])
    wests[0] = jnp.where(head & first_x, sign * blocks[0], wests[0])
    return easts, wests


def mirror(ref, sign, top, bottom):
    part = part_of(lax.axis_index("img"))
    first_y = (lax.axis_index("gy") == 0) & (part == 0)
    last_y = (lax.axis_index("gy") == lax.axis_size("gy") - 1) & (part == 1)
    for flag, out_row, row in ((first_y, top - 1, top), (last_y, bottom, bottom - 1)):
        for t in range(3):
            at = pl.ds(out_row, 1)
            ref[t, at, :] = jnp.where(flag, sign * ref[t, pl.ds(row, 1), :], ref[t, at, :])


def slopes_at(hs, row, size, first_x, last_x):
    at = pl.ds(row, size)
    easts, wests = neighbours_in_ring([hs[t, at, :] for t in range(3)], 1.0, first_x, last_x)
    for t in range(3):
        p = easts[t] - wests[t]
        q = hs[t, pl.ds(row + 1, size), :] - hs[t, pl.ds(row - 1, size), :]
        yield p, q, lax.rsqrt(1.0 + p * p + q * q)


def inner_row(core, half):
    return ROW + (1 - core) * (half + ROW)


def fill_kernel(height, albedo, keep, both, ends, hs, al, mo, ps, qs, cs):
    rows = height.shape[0]
    core = part_of(lax.axis_index("img"))

    def plane(k):
        return hs if k == 0 else al if k == 1 else mo.at[k - 2]

    half = rows // 2
    inner = core * (half - ROW) + (1 - core) * half
    for i in range(-ROW, half, ROW):
        if i < 0:
            src, dst = pl.ds(pl.multiple_of(inner, ROW), ROW), pl.ds(pl.multiple_of(inner_row(core, half), ROW), ROW)
        else:
            src, dst = pl.ds(pl.multiple_of(core * half + i, ROW), ROW), pl.ds(2 * ROW + i, ROW)
        sides = both[src, :]
        for k in range(PLANES):
            body = 0.5 * height[src, :] if k == 0 else albedo[src, :] if k == 1 else keep[k - 2, pl.ds(ROW + i, ROW), :]
            ref = plane(k)
            ref[0, dst, :] = body[:, :LANES]
            ref[1, dst, :] = body[:, LANES:]
            side = pltpu.roll(sides, LANES - STARTS[k], 1)
            ref[2, dst, :] = 0.5 * side if k == 0 else side
    dst = pl.ds(pl.multiple_of(inner_row(1 - core, half), ROW), ROW)
    sides = ends[pl.ds(ROW_STARTS[PLANES], ROW), :LANES]
    for k in range(PLANES):
        ref = plane(k)
        begin, spare = ROW_STARTS[k], ROW - WIDTHS[k]
        after = ends[pl.ds(begin, ROW), :]
        before = pltpu.roll(after, spare, 0) if k == 0 else ends[pl.ds(begin - spare, ROW), :]
        body = jnp.where(core == 0, before, after) * (0.5 if k == 0 else 1.0)
        ref[0, dst, :] = body[:, :LANES]
        ref[1, dst, :] = body[:, LANES:]
        side = pltpu.roll(sides, LANES - STARTS[k], 1)
        ref[2, dst, :] = 0.5 * side if k == 0 else side
    first_x = lax.axis_index("gx") == 0
    last_x = lax.axis_index("gx") == lax.axis_size("gx") - 1
    mirror(hs, 1.0, 2 * ROW, 2 * ROW + half)
    for row in range(ROW, half + 3 * ROW, 16):
        for t, (p, q, scale) in enumerate(slopes_at(hs, row, 16, first_x, last_x)):
            ps[t, pl.ds(row, 16), :], qs[t, pl.ds(row, 16), :], cs[t, pl.ds(row, 16), :] = p, q, scale


def steps_kernel(rates, hs_in, al_in, mo_in, ps, qs, cs, theirs, packs, out, hs, al, mo, gps, gqs):
    half = out.shape[1]
    core = lax.axis_index("img")
    part = part_of(core)
    first_x = lax.axis_index("gx") == 0
    last_x = lax.axis_index("gx") == lax.axis_size("gx") - 1
    rate_h, rate_a = rates
    top = 2 * ROW
    bottom = top + half
    count = theirs.shape[0] - 3
    table = packs[1 - core, packs.shape[1] - ROW :, :]
    factors = [[jnp.broadcast_to(table[k : k + 1, m : m + 1], (ROW, LANES)) for k in range(count)] for m in range(6)]
    for t in range(2):
        lanes = slice(t * LANES, (t + 1) * LANES)
        for i in range(-ROW, half, ROW):
            src = pl.ds(ROW + i, ROW)
            w = [theirs[k, src, lanes] for k in range(count)]
            for m in range(MOMENTS):
                if m < 6:
                    extra = sum((w[k] * factors[m][k] for k in range(1, count)), w[0] * factors[m][0])
                else:
                    extra = theirs[count + m - 6, src, lanes]
                if i >= 0:
                    at = pl.ds(top + i, ROW)
                    mo[m, t, at, :] = mo_in[m, t, at, :] + extra
                else:
                    for at, owner in ((pl.ds(ROW, ROW), 1), (pl.ds(bottom, ROW), 0)):
                        halo = mo_in[m, t, at, :]
                        mo[m, t, at, :] = jnp.where(part == owner, halo + extra, halo)

    def beside(blocks, sign):
        return neighbours_in_ring(blocks, sign, first_x, last_x)

    def borders(ref, sign):
        mirror(ref, sign, top, bottom)

    def slopes(row, size, first, last):
        at = pl.ds(row, size)
        if first:
            parts = [(ps[t, at, :], qs[t, at, :], cs[t, at, :]) for t in range(3)]
        else:
            parts = slopes_at(hs, row, size, first_x, last_x)
        for t, (p, q, scale) in enumerate(parts):
            xx, xy, xz, yy, yz, zz, vx, vy, vz = [(mo if t < 2 else mo_in)[m, t, at, :] for m in range(MOMENTS)]
            alb = (al_in if first else al)[t, at, :]
            lit = alb * scale
            gx = lit * (xz - p * xx - q * xy) - vx
            gy = lit * (yz - p * xy - q * yy) - vy
            gz = lit * (zz - p * xz - q * yz) - vz
            grad_a = scale * (gz - p * gx - q * gy)
            turn = scale * grad_a
            bend = 0.3 - lit * turn
            gps[t, at, :] = p * bend - lit * gx
            if not (last and t == 2):
                gqs[t, at, :] = q * bend - lit * gy
                al[t, at, :] = alb - rate_a * grad_a

    def descend(row, size, first, last):
        at = pl.ds(row, size)
        easts, wests = beside([gps[t, at, :] for t in range(3)], -1.0)
        for t in range(2 if last else 3):
            fall = (wests[t] - easts[t]) + (gqs[t, pl.ds(row - 1, size), :] - gqs[t, pl.ds(row + 1, size), :])
            now = (hs_in if first else hs)[t, at, :] - (0.25 * rate_h) * fall
            if last:
                lanes = slice(t * LANES, (t + 1) * LANES)
                out[0, row - top : row - top + size, lanes] = 2.0 * now
                out[1, row - top : row - top + size, lanes] = al[t, at, :]
            else:
                hs[t, at, :] = now

    for n in range(ITERS):
        first, last = n == 0, n == ITERS - 1
        for row in range(ROW, bottom + ROW, 16):
            slopes(row, 16, first, last)
        borders(gqs, -1.0)
        for row in range(top, bottom, 16) if last else range(ROW, bottom + ROW, 16):
            descend(row, 16, first, last)
        if not last:
            borders(hs, 1.0)


def seams(size):
    return [(i, i % 2) for i in range(size - 1)]


def flat(sizes, y, x, core):
    return (y * sizes[1] + x) * 2 + core


def column_groups(sizes):
    ny, nx = sizes
    groups = [[flat(sizes, y, x, core), flat(sizes, y, x + 1, core)] for y in range(ny) for x, core in seams(nx)]
    for y in range(0, ny, 2):
        groups += [[flat(sizes, y, x, 1), flat(sizes, y + 1, x, 1)] for x in (0, nx - 1)]
    return groups


def from_beside(x, core):
    groups = column_groups((lax.axis_size("gy"), lax.axis_size("gx")))
    both = lax.all_gather(x, AXES, axis_index_groups=groups)
    return lax.dynamic_index_in_dim(both, side_of(core), 0, keepdims=False)


def row_pairs(sizes):
    ny, nx = sizes
    pairs = [(flat(sizes, y, x, core), flat(sizes, y + 1, x, core)) for y, core in seams(ny) for x in range(nx)]
    return pairs + [(b, a) for a, b in pairs]


VMEM = pl.BlockSpec(memory_space=pltpu.VMEM)
HBM = pl.BlockSpec(memory_space=pltpu.HBM)


def in_vmem(*args):
    return tuple(pltpu.with_memory_space_constraint(x, pltpu.VMEM) for x in args)


def cost(mib):
    return pl.CostEstimate(flops=1 << 20, bytes_accessed=mib << 20, transcendentals=0)


def params(mib):
    return pltpu.CompilerParams(vmem_limit_bytes=mib << 20)


def run_edges(sun_index, expo_index, azimuth, elevation, exposure, heights, albedo, images, weights):
    rows, cols = heights.shape
    half = rows // 2
    tiles = [x.reshape(*x.shape[:-2], 2, half, cols) for x in (heights, albedo, images, weights)]
    args = [
        pltpu.with_memory_space_constraint(x, pltpu.HBM)
        for x in (sun_index, expo_index, azimuth, elevation, exposure, *tiles)
    ]
    out = pl.pallas_call(
        edges_kernel,
        out_shape=tuple(pltpu.VMEM(x.shape, x.dtype) for x in tiles)
        + (
            pltpu.VMEM((MOMENTS, ROW, LANES), F32),
            pltpu.VMEM((half, LANES), F32),
            pltpu.VMEM((MOMENTS * ROW, cols), F32),
            pltpu.VMEM((half + 2 * MOMENTS * ROW + ROW, LANES), F32),
        ),
        in_specs=[HBM] * len(args),
        out_specs=(VMEM,) * 8,
        scratch_shapes=[pltpu.SMEM(x.shape, x.dtype) for x in args[:5]]
        + [pltpu.VMEM((2, half, LANES), F32), pltpu.VMEM((2, MOMENTS, ROW, cols), F32)]
        + [pltpu.SemaphoreType.DMA((5,)), pltpu.SemaphoreType.DMA((CHUNKS + 1, 2))],
        compiler_params=params(8),
        name="edges",
    )(*args)
    return tuple(x.reshape(rows, cols) for x in out[:2]) + out[2:]


def run_moments(kernel, planes, images, weights, tables):
    _, _, half, cols = images.shape
    return pl.pallas_call(
        kernel,
        out_shape=pltpu.VMEM((planes, half + ROW, cols), F32),
        in_specs=[VMEM] * 3,
        out_specs=VMEM,
        compiler_params=params(8),
        cost_estimate=cost(4),
        name=kernel.__name__,
    )(*in_vmem(images, weights, tables))


def run_rows(heights, albedo, own_rows, packs, sides):
    rows, cols = heights.shape
    return pl.pallas_call(
        rows_kernel,
        out_shape=(pltpu.VMEM((rows, LANES), F32), pltpu.VMEM((ROW_STARTS[PLANES] + ROW, cols), F32)),
        in_specs=[VMEM] * 5,
        out_specs=(VMEM,) * 2,
        compiler_params=params(8),
        name="edge_rows",
    )(*in_vmem(heights, albedo, own_rows, packs, sides))


def frame(rows):
    return (3, rows // 2 + 4 * ROW, LANES)


def run_fill(heights, albedo, keep, both, ends):
    block = pltpu.VMEM(frame(heights.shape[0]), F32)
    return pl.pallas_call(
        fill_kernel,
        out_shape=(block, block, pltpu.VMEM((MOMENTS, *block.shape), F32), block, block, block),
        in_specs=[VMEM] * 5,
        out_specs=(VMEM,) * 6,
        compiler_params=params(8),
        cost_estimate=pl.CostEstimate(flops=1 << 34, bytes_accessed=1 << 20, transcendentals=0),
        name="fill",
    )(*in_vmem(heights, albedo, keep, both, ends))


def run_steps(total, *args):
    _, tall, _ = args[0].shape
    half = tall - 4 * ROW
    block = pltpu.VMEM(args[0].shape, F32)
    return pl.pallas_call(
        functools.partial(steps_kernel, (0.2 / total, 0.5 / total)),
        out_shape=pltpu.VMEM((2, half, 2 * LANES), F32),
        in_specs=[VMEM] * len(args),
        out_specs=VMEM,
        scratch_shapes=[block, block, pltpu.VMEM((MOMENTS, 2, tall, LANES), F32), block, block],
        compiler_params=params(8),
        name="gradient_steps",
    )(*in_vmem(*args))


def run_place(halves):
    _, _, half, cols = halves.shape
    out = jax.ShapeDtypeStruct((2 * half, cols), F32)
    return pl.pallas_call(
        place_kernel,
        out_shape=(out, out),
        in_specs=[VMEM],
        out_specs=(HBM, HBM),
        scratch_shapes=[pltpu.SemaphoreType.DMA((2, 2))],
        compiler_params=params(8),
        name="place",
    )(*in_vmem(halves))


def shards(
    heights, albedo, images, weights, sun_index, expo_index, sun_azimuth, sun_elevation, exposure
):
    total = images.shape[0] * lax.axis_size("img")
    core = lax.axis_index("img")
    heights, albedo, images, weights, tables, own_fold, own_rows, pack = run_edges(
        sun_index, expo_index, sun_azimuth, sun_elevation, exposure, heights, albedo, images, weights
    )
    packs = lax.all_gather(pack, "img")
    fold = own_fold + lax.dynamic_index_in_dim(packs, 1 - core, 0, keepdims=False)[: own_fold.shape[0]]
    sides = lax.all_gather(from_beside(fold, core), "img")
    both, ends = run_rows(heights, albedo, own_rows, packs, sides)
    ends, images = lax.optimization_barrier((ends, images))
    ends = lax.ppermute(ends, AXES, row_pairs((lax.axis_size("gy"), lax.axis_size("gx"))))
    send = run_moments(sent_kernel, images.shape[0] + 3, images, weights, tables)
    theirs = lax.ppermute(send, "img", [(0, 1), (1, 0)])
    keep = run_moments(own_kernel, MOMENTS, images, weights, tables)
    halves = run_steps(total, *run_fill(heights, albedo, keep, both, ends), theirs, packs)
    return run_place(lax.all_gather(halves, "img"))


def solution(mesh):
    return jax.shard_map(
        shards,
        mesh=mesh,
        in_specs=(
            P("gy", "gx"),
            P("gy", "gx"),
            P("img", "gy", "gx"),
            P("img", "gy", "gx"),
            P("img"),
            P("img"),
            P(),
            P(),
            P(),
        ),
        out_specs=(P("gy", "gx"), P("gy", "gx")),
        check_vma=False,
    )
```

```python
import functools

import jax
import jax.numpy as jnp
from jax import lax
from jax.experimental import pallas as pl
from jax.experimental.pallas import tpu as pltpu
from jax.sharding import PartitionSpec as P

ITERS = 3
AXES = ("gy", "gx", "img")
LANES = 128
ROW = 8
CHUNKS = 2
MOMENTS = 9
PLANES = 2 + MOMENTS
WIDTHS = (6,) + (5,) * (PLANES - 1)
STARTS = tuple(6 if k == 0 else 17 + 10 * (k - 1) for k in range(PLANES))
ROW_STARTS = tuple(sum(WIDTHS[:k]) for k in range(PLANES + 1))
F32 = jnp.float32


def part_of(core):
    return (core + 1 + lax.axis_index("gy")) % 2


def side_of(core):
    return (core + 1 + lax.axis_index("gx")) % 2


def lane_ids(rows):
    return lax.broadcasted_iota(jnp.int32, (rows, LANES), 1)


def east_lanes(lane):
    hit = lane < 0
    for start, width in zip(STARTS, WIDTHS):
        hit = hit | ((lane >= start) & (lane < start + width))
    return hit


def edges_kernel(
    sun_index_hbm, expo_index_hbm, azimuth_hbm, elevation_hbm, exposure_hbm, height_hbm, albedo_hbm, images_hbm,
    weights_hbm, height, albedo, images, weights, tables, own_fold, own_rows, pack, sun_index, expo_index, azimuth,
    elevation, exposure, spreads, ends_of_rows, small_sems, large_sems
):
    count, _, half, _ = images.shape
    small = [
        pltpu.make_async_copy(src, dst, small_sems.at[n])
        for n, (src, dst) in enumerate((
            (sun_index_hbm, sun_index), (expo_index_hbm, expo_index), (azimuth_hbm, azimuth),
            (elevation_hbm, elevation), (exposure_hbm, exposure),
        ))
    ]
    part = half // CHUNKS
    large = []
    for c in range(CHUNKS):
        at = pl.ds(c * part, part)
        large.append([
            pltpu.make_async_copy(weights_hbm.at[:, :, at, :], weights.at[:, :, at, :], large_sems.at[c, 0]),
            pltpu.make_async_copy(images_hbm.at[:, :, at, :], images.at[:, :, at, :], large_sems.at[c, 1]),
        ])
    large.append([
        pltpu.make_async_copy(height_hbm, height, large_sems.at[CHUNKS, 0]),
        pltpu.make_async_copy(albedo_hbm, albedo, large_sems.at[CHUNKS, 1]),
    ])
    for copies in large:
        for copy in copies:
            copy.start()
    for copy in small:
        copy.start()
    for copy in small:
        copy.wait()
    line = lax.broadcasted_iota(jnp.int32, (ROW, LANES), 0)
    azim = jnp.zeros((ROW, LANES), F32)
    elev = jnp.zeros((ROW, LANES), F32)
    gain = jnp.zeros((ROW, LANES), F32)
    for k in range(count):
        azim = jnp.where(line == k, azimuth[sun_index[k]], azim)
        elev = jnp.where(line == k, elevation[sun_index[k]], elev)
        gain = jnp.where(line == k, exposure[expo_index[k]], gain)
    flat = jnp.cos(elev)
    sx = gain * flat * jnp.cos(azim)
    sy = gain * flat * jnp.sin(azim)
    sz = gain * jnp.sin(elev)
    factors = (sx * sx, sx * sy, sx * sz, sy * sy, sy * sz, sz * sz, sx, sy, sz)
    for m, factor in enumerate(factors):
        tables[m] = factor
    lane = lane_ids(ROW)
    block = jnp.zeros((ROW, LANES), F32)
    for m, factor in enumerate(factors):
        block = jnp.where(lane == m, factor, block)
    pack[pl.ds(half + 2 * MOMENTS * ROW, ROW), :] = block
    step = 16
    lane = lane_ids(step)

    def sums(view):
        return add_moments(lambda k: view(weights, k), lambda k: view(images, k), count, lambda m, k: factors[m][k : k + 1, :1])

    def ends(x):
        return jnp.where(lane < LANES // 2, x[:, :LANES], x[:, -LANES:])

    middle = (lane >= LANES // 4) & (lane < 3 * LANES // 4)

    def all_ends(upper, lower):
        return jnp.where(middle, pltpu.roll(ends(lower), LANES // 2, 1), ends(upper)).astype(F32)

    def spread(planes, first, upper, lower):
        for plane, start, width in zip(planes, STARTS[first:], WIDTHS[first:]):
            plane = pltpu.roll(plane, start, 1)
            upper = jnp.where((lane >= start - width) & (lane < start + width), plane, upper)
            away = (lane - start - LANES // 2 + width) & (LANES - 1)
            lower = jnp.where(away < 2 * width, plane, lower)
        return upper, lower

    def edge_rows(side):
        at = pl.ds(side * (half - step), step)
        ends_of_rows[side] = jnp.stack(sums(lambda ref, k: ref[k, side, at, :].astype(F32)[side * ROW : (side + 1) * ROW]))

    zero = jnp.zeros((step, LANES), F32)
    for c in range(CHUNKS):
        for copy in large[c]:
            copy.wait()
        for i in range(c * part, (c + 1) * part, step):
            at = pl.ds(i, step)
            planes = sums(lambda ref, k: all_ends(ref[k, 0, at, :], ref[k, 1, at, :]))
            spreads[0, at, :], spreads[1, at, :] = spread(planes, 2, zero, zero)
        if c == 0:
            edge_rows(0)
        if c == CHUNKS - 1:
            edge_rows(1)
    part = part_of(lax.axis_index("img"))
    side = side_of(lax.axis_index("img"))
    for m in range(MOMENTS):
        own_rows[pl.ds(m * ROW, ROW), :] = ends_of_rows[part, m]
        for t in range(2):
            pack[pl.ds(half + (2 * m + t) * ROW, ROW), :] = ends_of_rows[1 - part, m, :, t * LANES : (t + 1) * LANES]
    for copy in large[CHUNKS]:
        copy.wait()
    high = east_lanes(lane)
    wide = lane < STARTS[0] + WIDTHS[0]
    for i in range(0, half, step):
        at = pl.ds(i, step)
        planes = [0.5 * all_ends(x[0, at, :], x[1, at, :]) for x in (height, albedo)]
        upper, lower = spread(planes, 0, spreads[0, at, :], spreads[1, at, :])
        to_west, to_east = (
            jnp.where(wide, pltpu.roll(lower, (64 + 6 * d) % LANES, 1), pltpu.roll(lower, (64 + 5 * d) % LANES, 1))
            for d in (-1, 1)
        )
        west = jnp.where(high, upper, to_west)
        east = jnp.where(high, to_east, upper)
        own_fold[at, :] = jnp.where(side == 0, west, east)
        pack[at, :] = jnp.where(side == 0, east, west)


def add_moments(weight, image, count, factor):
    acc = [None] * MOMENTS
    for k in range(count):
        w = weight(k)
        u = w * image(k)
        for m in range(MOMENTS):
            term = (w if m < 6 else u) * factor(m, k)
            acc[m] = term if k == 0 else acc[m] + term
    return acc


def part_rows(core, half):
    step = 16
    near = pl.multiple_of(core * (half - step), step)
    yield 1 - core, pl.ds(near, step), None
    for i in range(0, half, step):
        yield core, pl.ds(i, step), pl.ds(ROW + i, step)


def put(out, plane, dst, value, core):
    if dst is None:
        out[plane, pl.ds(0, ROW), :] = jnp.where(core == 0, value[:ROW], value[-ROW:])
    else:
        out[plane, dst, :] = value


def sent_kernel(images, weights, tables, out):
    count, _, half, _ = images.shape
    core = 1 - part_of(lax.axis_index("img"))
    for s, at, dst in part_rows(core, half):
        acc = [None] * 3
        for k in range(count):
            w = weights[k, s, at, :].astype(F32)
            put(out, k, dst, w, core)
            u = w * images[k, s, at, :].astype(F32)
            for m in range(3):
                term = u * tables[6 + m, k : k + 1, :1]
                acc[m] = term if k == 0 else acc[m] + term
        for m in range(3):
            put(out, count + m, dst, acc[m], core)


def own_kernel(images, weights, tables, out):
    count, _, half, _ = images.shape
    core = part_of(lax.axis_index("img"))
    for s, at, dst in part_rows(core, half):
        acc = add_moments(
            lambda k: weights[k, s, at, :].astype(F32), lambda k: images[k, s, at, :].astype(F32), count,
            lambda m, k: tables[m, k : k + 1, :1]
        )
        for m in range(MOMENTS):
            put(out, m, dst, acc[m], core)


def place_kernel(halves, height, albedo, sems):
    half = halves.shape[2]
    copies = [
        pltpu.make_async_copy(halves.at[part_of(part), n], out.at[pl.ds(part * half, half), :], sems.at[part, n])
        for part in range(2)
        for n, out in enumerate((height, albedo))
    ]
    for copy in copies:
        copy.start()
    for copy in copies:
        copy.wait()


def rows_kernel(height, albedo, own_rows, packs, sides, both, out):
    rows = height.shape[0]
    half = rows // 2
    core = lax.axis_index("img")
    part = part_of(core)
    west_core = side_of(0)
    lane = lane_ids(ROW)
    east = east_lanes(lane)
    wide = lane < STARTS[0] + WIDTHS[0]
    for i in range(0, half, ROW):
        at = pl.ds(i, ROW)
        west_side, east_side = sides[west_core, at, :], sides[1 - west_core, at, :]
        both[at, :] = jnp.where(east, east_side, west_side)
        moved_e, moved_w = (
            jnp.where(wide, pltpu.roll(x, 6 * d % LANES, 1), pltpu.roll(x, 5 * d % LANES, 1))
            for x, d in ((east_side, 1), (west_side, -1))
        )
        both[pl.ds(half + i, ROW), :] = jnp.where(east, moved_e, moved_w)
    at = pl.ds(pl.multiple_of(part * (rows - ROW), ROW), ROW)
    upper = part == 0

    def edge(x, n):
        return jnp.where(upper, x[:n], x[ROW - n :])

    out[pl.ds(0, WIDTHS[0]), :] = edge(height[at, :], WIDTHS[0])
    for k in range(1, PLANES):
        if k == 1:
            plane = albedo[at, :]
        else:
            m = k - 2
            theirs = [packs[1 - core, pl.ds(half + (2 * m + t) * ROW, ROW), :] for t in range(2)]
            plane = own_rows[pl.ds(m * ROW, ROW), :] + jnp.concatenate(theirs, axis=1)
        out[pl.ds(ROW_STARTS[k], WIDTHS[k]), :] = edge(plane, WIDTHS[k])
    corner = both[at, :]
    out[pl.ds(ROW_STARTS[PLANES], ROW), :] = jnp.concatenate([corner, corner], axis=1)


def neighbours_in_ring(blocks, sign, first_x, last_x):
    lane = lane_ids(blocks[0].shape[0])
    head = lane == 0
    tail = lane == LANES - 1
    fore = [pltpu.roll(b, LANES - 1, 1) for b in blocks]
    back = [pltpu.roll(b, 1, 1) for b in blocks]
    easts = [jnp.where(tail, fore[(t + 1) % 3], fore[t]) for t in range(3)]
    wests = [jnp.where(head, back[(t + 2) % 3], back[t]) for t in range(3)]
    easts[1] = jnp.where(tail & last_x, sign * blocks[1], easts[1])
    wests[0] = jnp.where(head & first_x, sign * blocks[0], wests[0])
    return easts, wests


def mirror(ref, sign, top, bottom):
    part = part_of(lax.axis_index("img"))
    first_y = (lax.axis_index("gy") == 0) & (part == 0)
    last_y = (lax.axis_index("gy") == lax.axis_size("gy") - 1) & (part == 1)
    for flag, out_row, row in ((first_y, top - 1, top), (last_y, bottom, bottom - 1)):
        for t in range(3):
            at = pl.ds(out_row, 1)
            ref[t, at, :] = jnp.where(flag, sign * ref[t, pl.ds(row, 1), :], ref[t, at, :])


def slopes_at(hs, row, size, first_x, last_x):
    at = pl.ds(row, size)
    easts, wests = neighbours_in_ring([hs[t, at, :] for t in range(3)], 1.0, first_x, last_x)
    for t in range(3):
        p = easts[t] - wests[t]
        q = hs[t, pl.ds(row + 1, size), :] - hs[t, pl.ds(row - 1, size), :]
        yield p, q, lax.rsqrt(1.0 + p * p + q * q)


def inner_row(core, half):
    return ROW + (1 - core) * (half + ROW)


def fill_kernel(height, albedo, keep, both, ends, packs, hs, al, mo, ps, qs, cs, factors):
    rows = height.shape[0]
    core = part_of(lax.axis_index("img"))

    def plane(k):
        return hs if k == 0 else al if k == 1 else mo.at[k - 2]

    half = rows // 2
    inner = core * (half - ROW) + (1 - core) * half
    for i in range(-ROW, half, ROW):
        if i < 0:
            src, dst = pl.ds(pl.multiple_of(inner, ROW), ROW), pl.ds(pl.multiple_of(inner_row(core, half), ROW), ROW)
        else:
            src, dst = pl.ds(pl.multiple_of(core * half + i, ROW), ROW), pl.ds(2 * ROW + i, ROW)
        sides = both[src, :]
        for k in range(PLANES):
            body = 0.5 * height[src, :] if k == 0 else albedo[src, :] if k == 1 else keep[k - 2, pl.ds(ROW + i, ROW), :]
            ref = plane(k)
            ref[0, dst, :] = body[:, :LANES]
            ref[1, dst, :] = body[:, LANES:]
            side = pltpu.roll(sides, LANES - STARTS[k], 1)
            ref[2, dst, :] = 0.5 * side if k == 0 else side
    dst = pl.ds(pl.multiple_of(inner_row(1 - core, half), ROW), ROW)
    sides = ends[pl.ds(ROW_STARTS[PLANES], ROW), :LANES]
    for k in range(PLANES):
        ref = plane(k)
        begin, spare = ROW_STARTS[k], ROW - WIDTHS[k]
        after = ends[pl.ds(begin, ROW), :]
        before = pltpu.roll(after, spare, 0) if k == 0 else ends[pl.ds(begin - spare, ROW), :]
        body = jnp.where(core == 0, before, after) * (0.5 if k == 0 else 1.0)
        ref[0, dst, :] = body[:, :LANES]
        ref[1, dst, :] = body[:, LANES:]
        side = pltpu.roll(sides, LANES - STARTS[k], 1)
        ref[2, dst, :] = 0.5 * side if k == 0 else side
    table = packs[1 - lax.axis_index("img"), packs.shape[1] - ROW :, :]
    for m in range(6):
        for k in range(factors.shape[1]):
            factors[m, k] = jnp.broadcast_to(table[k : k + 1, m : m + 1], (ROW, LANES))
    first_x = lax.axis_index("gx") == 0
    last_x = lax.axis_index("gx") == lax.axis_size("gx") - 1
    mirror(hs, 1.0, 2 * ROW, 2 * ROW + half)
    for row in range(ROW, half + 3 * ROW, 16):
        for t, (p, q, scale) in enumerate(slopes_at(hs, row, 16, first_x, last_x)):
            ps[t, pl.ds(row, 16), :], qs[t, pl.ds(row, 16), :], cs[t, pl.ds(row, 16), :] = p, q, scale


def steps_kernel(rates, hs_in, al_in, mo_in, ps, qs, cs, factors, theirs, out, hs, al, mo, gps, gqs):
    half = out.shape[1]
    part = part_of(lax.axis_index("img"))
    first_x = lax.axis_index("gx") == 0
    last_x = lax.axis_index("gx") == lax.axis_size("gx") - 1
    rate_h, rate_a = rates
    top = 2 * ROW
    bottom = top + half
    count = theirs.shape[0] - 3
    for t in range(2):
        lanes = slice(t * LANES, (t + 1) * LANES)
        for i in range(-ROW, half, ROW):
            src = pl.ds(ROW + i, ROW)
            w = [theirs[k, src, lanes] for k in range(count)]
            for m in range(MOMENTS):
                if m < 6:
                    extra = sum((w[k] * factors[m, k] for k in range(1, count)), w[0] * factors[m, 0])
                else:
                    extra = theirs[count + m - 6, src, lanes]
                if i >= 0:
                    at = pl.ds(top + i, ROW)
                    mo[m, t, at, :] = mo_in[m, t, at, :] + extra
                else:
                    for at, owner in ((pl.ds(ROW, ROW), 1), (pl.ds(bottom, ROW), 0)):
                        halo = mo_in[m, t, at, :]
                        mo[m, t, at, :] = jnp.where(part == owner, halo + extra, halo)

    def beside(blocks, sign):
        return neighbours_in_ring(blocks, sign, first_x, last_x)

    def borders(ref, sign):
        mirror(ref, sign, top, bottom)

    def slopes(row, size, first, last):
        at = pl.ds(row, size)
        if first:
            parts = [(ps[t, at, :], qs[t, at, :], cs[t, at, :]) for t in range(3)]
        else:
            parts = slopes_at(hs, row, size, first_x, last_x)
        for t, (p, q, scale) in enumerate(parts):
            xx, xy, xz, yy, yz, zz, vx, vy, vz = [(mo if t < 2 else mo_in)[m, t, at, :] for m in range(MOMENTS)]
            alb = (al_in if first else al)[t, at, :]
            lit = alb * scale
            gx = lit * (xz - p * xx - q * xy) - vx
            gy = lit * (yz - p * xy - q * yy) - vy
            gz = lit * (zz - p * xz - q * yz) - vz
            grad_a = scale * (gz - p * gx - q * gy)
            turn = scale * grad_a
            bend = 0.3 - lit * turn
            gps[t, at, :] = p * bend - lit * gx
            if not (last and t == 2):
                gqs[t, at, :] = q * bend - lit * gy
                al[t, at, :] = alb - rate_a * grad_a

    def descend(row, size, first, last):
        at = pl.ds(row, size)
        easts, wests = beside([gps[t, at, :] for t in range(3)], -1.0)
        for t in range(2 if last else 3):
            fall = (wests[t] - easts[t]) + (gqs[t, pl.ds(row - 1, size), :] - gqs[t, pl.ds(row + 1, size), :])
            now = (hs_in if first else hs)[t, at, :] - (0.25 * rate_h) * fall
            if last:
                lanes = slice(t * LANES, (t + 1) * LANES)
                out[0, row - top : row - top + size, lanes] = 2.0 * now
                out[1, row - top : row - top + size, lanes] = al[t, at, :]
            else:
                hs[t, at, :] = now

    for n in range(ITERS):
        first, last = n == 0, n == ITERS - 1
        for row in range(ROW, bottom + ROW, 16):
            slopes(row, 16, first, last)
        borders(gqs, -1.0)
        for row in range(top, bottom, 16) if last else range(ROW, bottom + ROW, 16):
            descend(row, 16, first, last)
        if not last:
            borders(hs, 1.0)


def seams(size):
    return [(i, i % 2) for i in range(size - 1)]


def flat(sizes, y, x, core):
    return (y * sizes[1] + x) * 2 + core


def column_groups(sizes):
    ny, nx = sizes
    groups = [[flat(sizes, y, x, core), flat(sizes, y, x + 1, core)] for y in range(ny) for x, core in seams(nx)]
    for y in range(0, ny, 2):
        groups += [[flat(sizes, y, x, 1), flat(sizes, y + 1, x, 1)] for x in (0, nx - 1)]
    return groups


def from_beside(x, core):
    groups = column_groups((lax.axis_size("gy"), lax.axis_size("gx")))
    both = lax.all_gather(x, AXES, axis_index_groups=groups)
    return lax.dynamic_index_in_dim(both, side_of(core), 0, keepdims=False)


def row_pairs(sizes):
    ny, nx = sizes
    pairs = [(flat(sizes, y, x, core), flat(sizes, y + 1, x, core)) for y, core in seams(ny) for x in range(nx)]
    return pairs + [(b, a) for a, b in pairs]


VMEM = pl.BlockSpec(memory_space=pltpu.VMEM)
HBM = pl.BlockSpec(memory_space=pltpu.HBM)


def in_vmem(*args):
    return tuple(pltpu.with_memory_space_constraint(x, pltpu.VMEM) for x in args)


def cost(mib):
    return pl.CostEstimate(flops=1 << 20, bytes_accessed=mib << 20, transcendentals=0)


def params(mib):
    return pltpu.CompilerParams(vmem_limit_bytes=mib << 20)


def run_edges(sun_index, expo_index, azimuth, elevation, exposure, heights, albedo, images, weights):
    rows, cols = heights.shape
    half = rows // 2
    tiles = [x.reshape(*x.shape[:-2], 2, half, cols) for x in (heights, albedo, images, weights)]
    args = [
        pltpu.with_memory_space_constraint(x, pltpu.HBM)
        for x in (sun_index, expo_index, azimuth, elevation, exposure, *tiles)
    ]
    out = pl.pallas_call(
        edges_kernel,
        out_shape=tuple(pltpu.VMEM(x.shape, x.dtype) for x in tiles)
        + (
            pltpu.VMEM((MOMENTS, ROW, LANES), F32),
            pltpu.VMEM((half, LANES), F32),
            pltpu.VMEM((MOMENTS * ROW, cols), F32),
            pltpu.VMEM((half + 2 * MOMENTS * ROW + ROW, LANES), F32),
        ),
        in_specs=[HBM] * len(args),
        out_specs=(VMEM,) * 8,
        scratch_shapes=[pltpu.SMEM(x.shape, x.dtype) for x in args[:5]]
        + [pltpu.VMEM((2, half, LANES), F32), pltpu.VMEM((2, MOMENTS, ROW, cols), F32)]
        + [pltpu.SemaphoreType.DMA((5,)), pltpu.SemaphoreType.DMA((CHUNKS + 1, 2))],
        compiler_params=params(8),
        name="edges",
    )(*args)
    return tuple(x.reshape(rows, cols) for x in out[:2]) + out[2:]


def run_moments(kernel, planes, images, weights, tables):
    _, _, half, cols = images.shape
    return pl.pallas_call(
        kernel,
        out_shape=pltpu.VMEM((planes, half + ROW, cols), F32),
        in_specs=[VMEM] * 3,
        out_specs=VMEM,
        compiler_params=params(8),
        cost_estimate=cost(4),
        name=kernel.__name__,
    )(*in_vmem(images, weights, tables))


def run_rows(heights, albedo, own_rows, packs, sides):
    rows, cols = heights.shape
    return pl.pallas_call(
        rows_kernel,
        out_shape=(pltpu.VMEM((rows, LANES), F32), pltpu.VMEM((ROW_STARTS[PLANES] + ROW, cols), F32)),
        in_specs=[VMEM] * 5,
        out_specs=(VMEM,) * 2,
        compiler_params=params(8),
        name="edge_rows",
    )(*in_vmem(heights, albedo, own_rows, packs, sides))


def frame(rows):
    return (3, rows // 2 + 4 * ROW, LANES)


def run_fill(heights, albedo, keep, both, ends, packs, count):
    block = pltpu.VMEM(frame(heights.shape[0]), F32)
    return pl.pallas_call(
        fill_kernel,
        out_shape=(block, block, pltpu.VMEM((MOMENTS, *block.shape), F32), block, block, block, pltpu.VMEM((6, count, ROW, LANES), F32)),
        in_specs=[VMEM] * 6,
        out_specs=(VMEM,) * 7,
        compiler_params=params(8),
        cost_estimate=pl.CostEstimate(flops=1 << 34, bytes_accessed=1 << 20, transcendentals=0),
        name="fill",
    )(*in_vmem(heights, albedo, keep, both, ends, packs))


def run_steps(total, *args):
    _, tall, _ = args[0].shape
    half = tall - 4 * ROW
    block = pltpu.VMEM(args[0].shape, F32)
    return pl.pallas_call(
        functools.partial(steps_kernel, (0.2 / total, 0.5 / total)),
        out_shape=pltpu.VMEM((2, half, 2 * LANES), F32),
        in_specs=[VMEM] * len(args),
        out_specs=VMEM,
        scratch_shapes=[block, block, pltpu.VMEM((MOMENTS, 2, tall, LANES), F32), block, block],
        compiler_params=params(8),
        name="gradient_steps",
    )(*in_vmem(*args))


def run_place(halves):
    _, _, half, cols = halves.shape
    out = jax.ShapeDtypeStruct((2 * half, cols), F32)
    return pl.pallas_call(
        place_kernel,
        out_shape=(out, out),
        in_specs=[VMEM],
        out_specs=(HBM, HBM),
        scratch_shapes=[pltpu.SemaphoreType.DMA((2, 2))],
        compiler_params=params(8),
        name="place",
    )(*in_vmem(halves))


def shards(
    heights, albedo, images, weights, sun_index, expo_index, sun_azimuth, sun_elevation, exposure
):
    total = images.shape[0] * lax.axis_size("img")
    core = lax.axis_index("img")
    heights, albedo, images, weights, tables, own_fold, own_rows, pack = run_edges(
        sun_index, expo_index, sun_azimuth, sun_elevation, exposure, heights, albedo, images, weights
    )
    packs = lax.all_gather(pack, "img")
    fold = own_fold + lax.dynamic_index_in_dim(packs, 1 - core, 0, keepdims=False)[: own_fold.shape[0]]
    sides = lax.all_gather(from_beside(fold, core), "img")
    both, ends = run_rows(heights, albedo, own_rows, packs, sides)
    ends, images = lax.optimization_barrier((ends, images))
    ends = lax.ppermute(ends, AXES, row_pairs((lax.axis_size("gy"), lax.axis_size("gx"))))
    send = run_moments(sent_kernel, images.shape[0] + 3, images, weights, tables)
    theirs = lax.ppermute(send, "img", [(0, 1), (1, 0)])
    keep = run_moments(own_kernel, MOMENTS, images, weights, tables)
    halves = run_steps(total, *run_fill(heights, albedo, keep, both, ends, packs, images.shape[0]), theirs)
    return run_place(lax.all_gather(halves, "img"))


def solution(mesh):
    return jax.shard_map(
        shards,
        mesh=mesh,
        in_specs=(
            P("gy", "gx"),
            P("gy", "gx"),
            P("img", "gy", "gx"),
            P("img", "gy", "gx"),
            P("img"),
            P("img"),
            P(),
            P(),
            P(),
        ),
        out_specs=(P("gy", "gx"), P("gy", "gx")),
        check_vma=False,
    )
```

```python
import functools

import jax
import jax.numpy as jnp
from jax import lax
from jax.experimental import pallas as pl
from jax.experimental.pallas import tpu as pltpu
from jax.sharding import PartitionSpec as P

ITERS = 3
AXES = ("gy", "gx", "img")
LANES = 128
ROW = 8
CHUNKS = 2
MOMENTS = 9
PLANES = 2 + MOMENTS
WIDTHS = (6,) + (5,) * (PLANES - 1)
STARTS = tuple(6 if k == 0 else 17 + 10 * (k - 1) for k in range(PLANES))
ROW_STARTS = tuple(sum(WIDTHS[:k]) for k in range(PLANES + 1))
F32 = jnp.float32


def part_of(core):
    return (core + 1 + lax.axis_index("gy")) % 2


def side_of(core):
    return (core + 1 + lax.axis_index("gx")) % 2


def lane_ids(rows):
    return lax.broadcasted_iota(jnp.int32, (rows, LANES), 1)


def east_lanes(lane):
    hit = lane < 0
    for start, width in zip(STARTS, WIDTHS):
        hit = hit | ((lane >= start) & (lane < start + width))
    return hit


def edges_kernel(
    sun_index_hbm, expo_index_hbm, azimuth_hbm, elevation_hbm, exposure_hbm, height_hbm, albedo_hbm, images_hbm,
    weights_hbm, height, albedo, images, weights, tables, own_fold, own_rows, pack, sun_index, expo_index, azimuth,
    elevation, exposure, spreads, ends_of_rows, small_sems, large_sems
):
    count, _, half, _ = images.shape
    small = [
        pltpu.make_async_copy(src, dst, small_sems.at[n])
        for n, (src, dst) in enumerate((
            (sun_index_hbm, sun_index), (expo_index_hbm, expo_index), (azimuth_hbm, azimuth),
            (elevation_hbm, elevation), (exposure_hbm, exposure),
        ))
    ]
    part = half // CHUNKS
    large = []
    for c in range(CHUNKS):
        at = pl.ds(c * part, part)
        large.append([
            pltpu.make_async_copy(weights_hbm.at[:, :, at, :], weights.at[:, :, at, :], large_sems.at[c, 0]),
            pltpu.make_async_copy(images_hbm.at[:, :, at, :], images.at[:, :, at, :], large_sems.at[c, 1]),
        ])
    large.append([
        pltpu.make_async_copy(height_hbm, height, large_sems.at[CHUNKS, 0]),
        pltpu.make_async_copy(albedo_hbm, albedo, large_sems.at[CHUNKS, 1]),
    ])
    for copies in large:
        for copy in copies:
            copy.start()
    for copy in small:
        copy.start()
    for copy in small:
        copy.wait()
    line = lax.broadcasted_iota(jnp.int32, (ROW, LANES), 0)
    azim = jnp.zeros((ROW, LANES), F32)
    elev = jnp.zeros((ROW, LANES), F32)
    gain = jnp.zeros((ROW, LANES), F32)
    for k in range(count):
        azim = jnp.where(line == k, azimuth[sun_index[k]], azim)
        elev = jnp.where(line == k, elevation[sun_index[k]], elev)
        gain = jnp.where(line == k, exposure[expo_index[k]], gain)
    flat = jnp.cos(elev)
    sx = gain * flat * jnp.cos(azim)
    sy = gain * flat * jnp.sin(azim)
    sz = gain * jnp.sin(elev)
    factors = (sx * sx, sx * sy, sx * sz, sy * sy, sy * sz, sz * sz, sx, sy, sz)
    for m, factor in enumerate(factors):
        tables[m] = factor
    lane = lane_ids(ROW)
    block = jnp.zeros((ROW, LANES), F32)
    for m, factor in enumerate(factors):
        block = jnp.where(lane == m, factor, block)
    pack[pl.ds(half + 2 * MOMENTS * ROW, ROW), :] = block
    step = 16
    lane = lane_ids(step)

    def sums(view):
        return add_moments(lambda k: view(weights, k), lambda k: view(images, k), count, lambda m, k: factors[m][k : k + 1, :1])

    def ends(x):
        return jnp.where(lane < LANES // 2, x[:, :LANES], x[:, -LANES:])

    middle = (lane >= LANES // 4) & (lane < 3 * LANES // 4)

    def all_ends(upper, lower):
        return jnp.where(middle, pltpu.roll(ends(lower), LANES // 2, 1), ends(upper)).astype(F32)

    def spread(planes, first, upper, lower):
        for plane, start, width in zip(planes, STARTS[first:], WIDTHS[first:]):
            plane = pltpu.roll(plane, start, 1)
            upper = jnp.where((lane >= start - width) & (lane < start + width), plane, upper)
            away = (lane - start - LANES // 2 + width) & (LANES - 1)
            lower = jnp.where(away < 2 * width, plane, lower)
        return upper, lower

    def edge_rows(side):
        at = pl.ds(side * (half - step), step)
        ends_of_rows[side] = jnp.stack(sums(lambda ref, k: ref[k, side, at, :].astype(F32)[side * ROW : (side + 1) * ROW]))

    zero = jnp.zeros((step, LANES), F32)
    for c in range(CHUNKS):
        for copy in large[c]:
            copy.wait()
        for i in range(c * part, (c + 1) * part, step):
            at = pl.ds(i, step)
            planes = sums(lambda ref, k: all_ends(ref[k, 0, at, :], ref[k, 1, at, :]))
            spreads[0, at, :], spreads[1, at, :] = spread(planes, 2, zero, zero)
        if c == 0:
            edge_rows(0)
        if c == CHUNKS - 1:
            edge_rows(1)
    part = part_of(lax.axis_index("img"))
    side = side_of(lax.axis_index("img"))
    for m in range(MOMENTS):
        own_rows[pl.ds(m * ROW, ROW), :] = ends_of_rows[part, m]
        for t in range(2):
            pack[pl.ds(half + (2 * m + t) * ROW, ROW), :] = ends_of_rows[1 - part, m, :, t * LANES : (t + 1) * LANES]
    for copy in large[CHUNKS]:
        copy.wait()
    high = east_lanes(lane)
    wide = lane < STARTS[0] + WIDTHS[0]
    for i in range(0, half, step):
        at = pl.ds(i, step)
        planes = [0.5 * all_ends(x[0, at, :], x[1, at, :]) for x in (height, albedo)]
        upper, lower = spread(planes, 0, spreads[0, at, :], spreads[1, at, :])
        to_west, to_east = (
            jnp.where(wide, pltpu.roll(lower, (64 + 6 * d) % LANES, 1), pltpu.roll(lower, (64 + 5 * d) % LANES, 1))
            for d in (-1, 1)
        )
        west = jnp.where(high, upper, to_west)
        east = jnp.where(high, to_east, upper)
        own_fold[at, :] = jnp.where(side == 0, west, east)
        pack[at, :] = jnp.where(side == 0, east, west)


def add_moments(weight, image, count, factor):
    acc = [None] * MOMENTS
    for k in range(count):
        w = weight(k)
        u = w * image(k)
        for m in range(MOMENTS):
            term = (w if m < 6 else u) * factor(m, k)
            acc[m] = term if k == 0 else acc[m] + term
    return acc


def part_rows(core, half):
    step = 16
    near = pl.multiple_of(core * (half - step), step)
    yield 1 - core, pl.ds(near, step), None
    for i in range(0, half, step):
        yield core, pl.ds(i, step), pl.ds(ROW + i, step)


def put(out, plane, dst, value, core):
    if dst is None:
        out[plane, pl.ds(0, ROW), :] = jnp.where(core == 0, value[:ROW], value[-ROW:])
    else:
        out[plane, dst, :] = value


def sent_kernel(images, weights, tables, out):
    count, _, half, _ = images.shape
    core = 1 - part_of(lax.axis_index("img"))
    for s, at, dst in part_rows(core, half):
        acc = [None] * 3
        for k in range(count):
            w = weights[k, s, at, :].astype(F32)
            put(out, k, dst, w, core)
            u = w * images[k, s, at, :].astype(F32)
            for m in range(3):
                term = u * jnp.concatenate([tables[6 + m, k : k + 1, :]] * 2, axis=1)
                acc[m] = term if k == 0 else acc[m] + term
        for m in range(3):
            put(out, count + m, dst, acc[m], core)


def own_kernel(images, weights, tables, out):
    count, _, half, _ = images.shape
    core = part_of(lax.axis_index("img"))
    for s, at, dst in part_rows(core, half):
        acc = add_moments(
            lambda k: weights[k, s, at, :].astype(F32), lambda k: images[k, s, at, :].astype(F32), count,
            lambda m, k: tables[m, k : k + 1, :1]
        )
        for m in range(MOMENTS):
            put(out, m, dst, acc[m], core)


def place_kernel(halves, height, albedo, sems):
    half = halves.shape[2]
    copies = [
        pltpu.make_async_copy(halves.at[part_of(part), n], out.at[pl.ds(part * half, half), :], sems.at[part, n])
        for part in range(2)
        for n, out in enumerate((height, albedo))
    ]
    for copy in copies:
        copy.start()
    for copy in copies:
        copy.wait()


def rows_kernel(height, albedo, own_rows, packs, sides, both, out):
    rows = height.shape[0]
    half = rows // 2
    core = lax.axis_index("img")
    part = part_of(core)
    west_core = side_of(0)
    lane = lane_ids(ROW)
    east = east_lanes(lane)
    wide = lane < STARTS[0] + WIDTHS[0]
    for i in range(0, half, ROW):
        at = pl.ds(i, ROW)
        west_side, east_side = sides[west_core, at, :], sides[1 - west_core, at, :]
        both[at, :] = jnp.where(east, east_side, west_side)
        moved_e, moved_w = (
            jnp.where(wide, pltpu.roll(x, 6 * d % LANES, 1), pltpu.roll(x, 5 * d % LANES, 1))
            for x, d in ((east_side, 1), (west_side, -1))
        )
        both[pl.ds(half + i, ROW), :] = jnp.where(east, moved_e, moved_w)
    at = pl.ds(pl.multiple_of(part * (rows - ROW), ROW), ROW)
    upper = part == 0

    def edge(x, n):
        return jnp.where(upper, x[:n], x[ROW - n :])

    out[pl.ds(0, WIDTHS[0]), :] = edge(height[at, :], WIDTHS[0])
    for k in range(1, PLANES):
        if k == 1:
            plane = albedo[at, :]
        else:
            m = k - 2
            theirs = [packs[1 - core, pl.ds(half + (2 * m + t) * ROW, ROW), :] for t in range(2)]
            plane = own_rows[pl.ds(m * ROW, ROW), :] + jnp.concatenate(theirs, axis=1)
        out[pl.ds(ROW_STARTS[k], WIDTHS[k]), :] = edge(plane, WIDTHS[k])
    corner = both[at, :]
    out[pl.ds(ROW_STARTS[PLANES], ROW), :] = jnp.concatenate([corner, corner], axis=1)


def neighbours_in_ring(blocks, sign, first_x, last_x):
    lane = lane_ids(blocks[0].shape[0])
    head = lane == 0
    tail = lane == LANES - 1
    fore = [pltpu.roll(b, LANES - 1, 1) for b in blocks]
    back = [pltpu.roll(b, 1, 1) for b in blocks]
    easts = [jnp.where(tail, fore[(t + 1) % 3], fore[t]) for t in range(3)]
    wests = [jnp.where(head, back[(t + 2) % 3], back[t]) for t in range(3)]
    easts[1] = jnp.where(tail & last_x, sign * blocks[1], easts[1])
    wests[0] = jnp.where(head & first_x, sign * blocks[0], wests[0])
    return easts, wests


def mirror(ref, sign, top, bottom):
    part = part_of(lax.axis_index("img"))
    first_y = (lax.axis_index("gy") == 0) & (part == 0)
    last_y = (lax.axis_index("gy") == lax.axis_size("gy") - 1) & (part == 1)
    for flag, out_row, row in ((first_y, top - 1, top), (last_y, bottom, bottom - 1)):
        for t in range(3):
            at = pl.ds(out_row, 1)
            ref[t, at, :] = jnp.where(flag, sign * ref[t, pl.ds(row, 1), :], ref[t, at, :])


def slopes_at(hs, row, size, first_x, last_x):
    at = pl.ds(row, size)
    easts, wests = neighbours_in_ring([hs[t, at, :] for t in range(3)], 1.0, first_x, last_x)
    for t in range(3):
        p = easts[t] - wests[t]
        q = hs[t, pl.ds(row + 1, size), :] - hs[t, pl.ds(row - 1, size), :]
        yield p, q, lax.rsqrt(1.0 + p * p + q * q)


def inner_row(core, half):
    return ROW + (1 - core) * (half + ROW)


def fill_kernel(height, albedo, keep, both, ends, packs, hs, al, mo, ps, qs, cs, factors):
    rows = height.shape[0]
    core = part_of(lax.axis_index("img"))

    def plane(k):
        return hs if k == 0 else al if k == 1 else mo.at[k - 2]

    half = rows // 2
    inner = core * (half - ROW) + (1 - core) * half
    for i in range(-ROW, half, ROW):
        if i < 0:
            src, dst = pl.ds(pl.multiple_of(inner, ROW), ROW), pl.ds(pl.multiple_of(inner_row(core, half), ROW), ROW)
        else:
            src, dst = pl.ds(pl.multiple_of(core * half + i, ROW), ROW), pl.ds(2 * ROW + i, ROW)
        sides = both[src, :]
        for k in range(PLANES):
            body = 0.5 * height[src, :] if k == 0 else albedo[src, :] if k == 1 else keep[k - 2, pl.ds(ROW + i, ROW), :]
            ref = plane(k)
            ref[0, dst, :] = body[:, :LANES]
            ref[1, dst, :] = body[:, LANES:]
            side = pltpu.roll(sides, LANES - STARTS[k], 1)
            ref[2, dst, :] = 0.5 * side if k == 0 else side
    dst = pl.ds(pl.multiple_of(inner_row(1 - core, half), ROW), ROW)
    sides = ends[pl.ds(ROW_STARTS[PLANES], ROW), :LANES]
    for k in range(PLANES):
        ref = plane(k)
        begin, spare = ROW_STARTS[k], ROW - WIDTHS[k]
        after = ends[pl.ds(begin, ROW), :]
        before = pltpu.roll(after, spare, 0) if k == 0 else ends[pl.ds(begin - spare, ROW), :]
        body = jnp.where(core == 0, before, after) * (0.5 if k == 0 else 1.0)
        ref[0, dst, :] = body[:, :LANES]
        ref[1, dst, :] = body[:, LANES:]
        side = pltpu.roll(sides, LANES - STARTS[k], 1)
        ref[2, dst, :] = 0.5 * side if k == 0 else side
    table = packs[1 - lax.axis_index("img"), packs.shape[1] - ROW :, :]
    for m in range(6):
        for k in range(factors.shape[1]):
            factors[m, k] = jnp.broadcast_to(table[k : k + 1, m : m + 1], (ROW, LANES))
    first_x = lax.axis_index("gx") == 0
    last_x = lax.axis_index("gx") == lax.axis_size("gx") - 1
    mirror(hs, 1.0, 2 * ROW, 2 * ROW + half)
    for row in range(ROW, half + 3 * ROW, 16):
        for t, (p, q, scale) in enumerate(slopes_at(hs, row, 16, first_x, last_x)):
            ps[t, pl.ds(row, 16), :], qs[t, pl.ds(row, 16), :], cs[t, pl.ds(row, 16), :] = p, q, scale


def steps_kernel(rates, hs_in, al_in, mo_in, ps, qs, cs, factors, theirs, out, hs, al, mo, gps, gqs):
    half = out.shape[1]
    part = part_of(lax.axis_index("img"))
    first_x = lax.axis_index("gx") == 0
    last_x = lax.axis_index("gx") == lax.axis_size("gx") - 1
    rate_h, rate_a = rates
    top = 2 * ROW
    bottom = top + half
    count = theirs.shape[0] - 3
    for t in range(2):
        lanes = slice(t * LANES, (t + 1) * LANES)
        for i in range(-ROW, half, ROW):
            src = pl.ds(ROW + i, ROW)
            w = [theirs[k, src, lanes] for k in range(count)]
            for m in range(MOMENTS):
                if m < 6:
                    extra = sum((w[k] * factors[m, k] for k in range(1, count)), w[0] * factors[m, 0])
                else:
                    extra = theirs[count + m - 6, src, lanes]
                if i >= 0:
                    at = pl.ds(top + i, ROW)
                    mo[m, t, at, :] = mo_in[m, t, at, :] + extra
                else:
                    for at, owner in ((pl.ds(ROW, ROW), 1), (pl.ds(bottom, ROW), 0)):
                        halo = mo_in[m, t, at, :]
                        mo[m, t, at, :] = jnp.where(part == owner, halo + extra, halo)

    def beside(blocks, sign):
        return neighbours_in_ring(blocks, sign, first_x, last_x)

    def borders(ref, sign):
        mirror(ref, sign, top, bottom)

    def slopes(row, size, first, last):
        at = pl.ds(row, size)
        if first:
            parts = [(ps[t, at, :], qs[t, at, :], cs[t, at, :]) for t in range(3)]
        else:
            parts = slopes_at(hs, row, size, first_x, last_x)
        for t, (p, q, scale) in enumerate(parts):
            xx, xy, xz, yy, yz, zz, vx, vy, vz = [(mo if t < 2 else mo_in)[m, t, at, :] for m in range(MOMENTS)]
            alb = (al_in if first else al)[t, at, :]
            lit = alb * scale
            gx = lit * (xz - p * xx - q * xy) - vx
            gy = lit * (yz - p * xy - q * yy) - vy
            gz = lit * (zz - p * xz - q * yz) - vz
            grad_a = scale * (gz - p * gx - q * gy)
            turn = scale * grad_a
            bend = 0.3 - lit * turn
            gps[t, at, :] = p * bend - lit * gx
            if not (last and t == 2):
                gqs[t, at, :] = q * bend - lit * gy
                al[t, at, :] = alb - rate_a * grad_a

    def descend(row, size, first, last):
        at = pl.ds(row, size)
        easts, wests = beside([gps[t, at, :] for t in range(3)], -1.0)
        for t in range(2 if last else 3):
            fall = (wests[t] - easts[t]) + (gqs[t, pl.ds(row - 1, size), :] - gqs[t, pl.ds(row + 1, size), :])
            now = (hs_in if first else hs)[t, at, :] - (0.25 * rate_h) * fall
            if last:
                lanes = slice(t * LANES, (t + 1) * LANES)
                out[0, row - top : row - top + size, lanes] = 2.0 * now
                out[1, row - top : row - top + size, lanes] = al[t, at, :]
            else:
                hs[t, at, :] = now

    for n in range(ITERS):
        first, last = n == 0, n == ITERS - 1
        for row in range(ROW, bottom + ROW, 16):
            slopes(row, 16, first, last)
        borders(gqs, -1.0)
        for row in range(top, bottom, 16) if last else range(ROW, bottom + ROW, 16):
            descend(row, 16, first, last)
        if not last:
            borders(hs, 1.0)


def seams(size):
    return [(i, i % 2) for i in range(size - 1)]


def flat(sizes, y, x, core):
    return (y * sizes[1] + x) * 2 + core


def column_groups(sizes):
    ny, nx = sizes
    groups = [[flat(sizes, y, x, core), flat(sizes, y, x + 1, core)] for y in range(ny) for x, core in seams(nx)]
    for y in range(0, ny, 2):
        groups += [[flat(sizes, y, x, 1), flat(sizes, y + 1, x, 1)] for x in (0, nx - 1)]
    return groups


def from_beside(x, core):
    groups = column_groups((lax.axis_size("gy"), lax.axis_size("gx")))
    both = lax.all_gather(x, AXES, axis_index_groups=groups)
    return lax.dynamic_index_in_dim(both, side_of(core), 0, keepdims=False)


def row_pairs(sizes):
    ny, nx = sizes
    pairs = [(flat(sizes, y, x, core), flat(sizes, y + 1, x, core)) for y, core in seams(ny) for x in range(nx)]
    return pairs + [(b, a) for a, b in pairs]


VMEM = pl.BlockSpec(memory_space=pltpu.VMEM)
HBM = pl.BlockSpec(memory_space=pltpu.HBM)


def in_vmem(*args):
    return tuple(pltpu.with_memory_space_constraint(x, pltpu.VMEM) for x in args)


def cost(mib):
    return pl.CostEstimate(flops=1 << 20, bytes_accessed=mib << 20, transcendentals=0)


def params(mib):
    return pltpu.CompilerParams(vmem_limit_bytes=mib << 20)


def run_edges(sun_index, expo_index, azimuth, elevation, exposure, heights, albedo, images, weights):
    rows, cols = heights.shape
    half = rows // 2
    tiles = [x.reshape(*x.shape[:-2], 2, half, cols) for x in (heights, albedo, images, weights)]
    args = [
        pltpu.with_memory_space_constraint(x, pltpu.HBM)
        for x in (sun_index, expo_index, azimuth, elevation, exposure, *tiles)
    ]
    out = pl.pallas_call(
        edges_kernel,
        out_shape=tuple(pltpu.VMEM(x.shape, x.dtype) for x in tiles)
        + (
            pltpu.VMEM((MOMENTS, ROW, LANES), F32),
            pltpu.VMEM((half, LANES), F32),
            pltpu.VMEM((MOMENTS * ROW, cols), F32),
            pltpu.VMEM((half + 2 * MOMENTS * ROW + ROW, LANES), F32),
        ),
        in_specs=[HBM] * len(args),
        out_specs=(VMEM,) * 8,
        scratch_shapes=[pltpu.SMEM(x.shape, x.dtype) for x in args[:5]]
        + [pltpu.VMEM((2, half, LANES), F32), pltpu.VMEM((2, MOMENTS, ROW, cols), F32)]
        + [pltpu.SemaphoreType.DMA((5,)), pltpu.SemaphoreType.DMA((CHUNKS + 1, 2))],
        compiler_params=params(8),
        name="edges",
    )(*args)
    return tuple(x.reshape(rows, cols) for x in out[:2]) + out[2:]


def run_moments(kernel, planes, images, weights, tables):
    _, _, half, cols = images.shape
    return pl.pallas_call(
        kernel,
        out_shape=pltpu.VMEM((planes, half + ROW, cols), F32),
        in_specs=[VMEM] * 3,
        out_specs=VMEM,
        compiler_params=params(8),
        cost_estimate=cost(4),
        name=kernel.__name__,
    )(*in_vmem(images, weights, tables))


def run_rows(heights, albedo, own_rows, packs, sides):
    rows, cols = heights.shape
    return pl.pallas_call(
        rows_kernel,
        out_shape=(pltpu.VMEM((rows, LANES), F32), pltpu.VMEM((ROW_STARTS[PLANES] + ROW, cols), F32)),
        in_specs=[VMEM] * 5,
        out_specs=(VMEM,) * 2,
        compiler_params=params(8),
        name="edge_rows",
    )(*in_vmem(heights, albedo, own_rows, packs, sides))


def frame(rows):
    return (3, rows // 2 + 4 * ROW, LANES)


def run_fill(heights, albedo, keep, both, ends, packs, count):
    block = pltpu.VMEM(frame(heights.shape[0]), F32)
    return pl.pallas_call(
        fill_kernel,
        out_shape=(block, block, pltpu.VMEM((MOMENTS, *block.shape), F32), block, block, block, pltpu.VMEM((6, count, ROW, LANES), F32)),
        in_specs=[VMEM] * 6,
        out_specs=(VMEM,) * 7,
        compiler_params=params(8),
        cost_estimate=pl.CostEstimate(flops=1 << 34, bytes_accessed=1 << 20, transcendentals=0),
        name="fill",
    )(*in_vmem(heights, albedo, keep, both, ends, packs))


def run_steps(total, *args):
    _, tall, _ = args[0].shape
    half = tall - 4 * ROW
    block = pltpu.VMEM(args[0].shape, F32)
    return pl.pallas_call(
        functools.partial(steps_kernel, (0.2 / total, 0.5 / total)),
        out_shape=pltpu.VMEM((2, half, 2 * LANES), F32),
        in_specs=[VMEM] * len(args),
        out_specs=VMEM,
        scratch_shapes=[block, block, pltpu.VMEM((MOMENTS, 2, tall, LANES), F32), block, block],
        compiler_params=params(8),
        name="gradient_steps",
    )(*in_vmem(*args))


def run_place(halves):
    _, _, half, cols = halves.shape
    out = jax.ShapeDtypeStruct((2 * half, cols), F32)
    return pl.pallas_call(
        place_kernel,
        out_shape=(out, out),
        in_specs=[VMEM],
        out_specs=(HBM, HBM),
        scratch_shapes=[pltpu.SemaphoreType.DMA((2, 2))],
        compiler_params=params(8),
        name="place",
    )(*in_vmem(halves))


def shards(
    heights, albedo, images, weights, sun_index, expo_index, sun_azimuth, sun_elevation, exposure
):
    total = images.shape[0] * lax.axis_size("img")
    core = lax.axis_index("img")
    heights, albedo, images, weights, tables, own_fold, own_rows, pack = run_edges(
        sun_index, expo_index, sun_azimuth, sun_elevation, exposure, heights, albedo, images, weights
    )
    packs = lax.all_gather(pack, "img")
    fold = own_fold + lax.dynamic_index_in_dim(packs, 1 - core, 0, keepdims=False)[: own_fold.shape[0]]
    sides = lax.all_gather(from_beside(fold, core), "img")
    both, ends = run_rows(heights, albedo, own_rows, packs, sides)
    ends, images = lax.optimization_barrier((ends, images))
    ends = lax.ppermute(ends, AXES, row_pairs((lax.axis_size("gy"), lax.axis_size("gx"))))
    send = run_moments(sent_kernel, images.shape[0] + 3, images, weights, tables)
    theirs = lax.ppermute(send, "img", [(0, 1), (1, 0)])
    keep = run_moments(own_kernel, MOMENTS, images, weights, tables)
    halves = run_steps(total, *run_fill(heights, albedo, keep, both, ends, packs, images.shape[0]), theirs)
    return run_place(lax.all_gather(halves, "img"))


def solution(mesh):
    return jax.shard_map(
        shards,
        mesh=mesh,
        in_specs=(
            P("gy", "gx"),
            P("gy", "gx"),
            P("img", "gy", "gx"),
            P("img", "gy", "gx"),
            P("img"),
            P("img"),
            P(),
            P(),
            P(),
        ),
        out_specs=(P("gy", "gx"), P("gy", "gx")),
        check_vma=False,
    )
```
